32 devices in a mesh: dp: 8 (over z, y), tensor: 4 (over x, core).
Axes of the slice: x: 2, y: 2, z: 4, core: 2. Of those that a mesh axis runs over, the one named last changes fastest.
Arguments:
- layer_input: bfloat16 [10240, 768], P(('dp', 'tensor')), may hold values from -6 to 6
- cotangent: bfloat16 [10240, 768], P(('dp', 'tensor')), may hold values from -6 to 6
- segments: int32 [10240], replicated, may hold values from 0 to 25, as said below
- parents: int32 [26], replicated, may hold values from 0 to 17, as said below
- norm1_gain: bfloat16 [768], P('dp'), may hold values from 0.099609375 to 1.8984375
- w_query: bfloat16 [768, 768], P('dp', 'tensor'), may hold values from -0.21875 to 0.21875
- w_key: bfloat16 [768, 768], P('dp', 'tensor'), may hold values from -0.21875 to 0.21875
- w_value: bfloat16 [768, 768], P('dp', 'tensor'), may hold values from -0.21875 to 0.21875
- w_out: bfloat16 [768, 768], P('tensor', 'dp'), may hold values from -1.75 to 1.75
- norm2_gain: bfloat16 [768], P('dp'), may hold values from 0.099609375 to 1.8984375
- w_up: bfloat16 [768, 3072], P('dp', 'tensor'), may hold values from -0.21875 to 0.21875
- w_down: bfloat16 [3072, 768], P('tensor', 'dp'), may hold values from -0.109375 to 0.109375
Outputs:
- layer_output: bfloat16 [10240, 768], P(('dp', 'tensor'))
- input_grad: bfloat16 [10240, 768], P(('dp', 'tensor'))
- grad_norm1_gain: float32 [768], P('dp')
- grad_query: float32 [768, 768], P('dp', 'tensor')
- grad_key: float32 [768, 768], P('dp', 'tensor')
- grad_value: float32 [768, 768], P('dp', 'tensor')
- grad_out: float32 [768, 768], P('tensor', 'dp')
- grad_norm2_gain: float32 [768], P('dp')
- grad_up: float32 [768, 3072], P('dp', 'tensor')
- grad_down: float32 [3072, 768], P('tensor', 'dp')
The draws below stay inside these ranges and needn't reach their ends.
Inputs may be any that keep to these rules, and one draw needn't show every extreme that they name: Tree t holds bytes 5120 t to 5120 (t + 1) - 1 of the stream (the last tree may end at 10240). Its first 2048 bytes are segment 13 t, the trunk; the rest are twelve runs of 256 bytes with the segments 13 t + 1 to 13 t + 12 in some order, every run after the run of its parent segment. parents[s] is the parent segment of s: the trunk 13 t is its own parent, the branches 13 t + 1 to 13 t + 4 have the trunk, and the leaves 13 t + 5 to 13 t + 12 have one of the four branches each, two leaves a branch.
All inputs are finite; a program needn't handle non-finite values.
Results may differ from the reference program's by a relative error of at most 0.017.
Values may be sent and summed in bfloat16 or wider, within the bound.
A program may use at most 256 MiB of HBM per device.

```python
import jax
import jax.numpy as jnp
from jax import lax

D = 768
HEADS = 12
HD = 64
FF = 3072
WINDOW = 1536
SEG = 256
TRUNK = 2048
TOKENS = 10240
TREES = 2


def tree_layout(key):
    base = jax.random.fold_in(key, 7)
    first_key, second_key, third_key = jax.random.split(base, 3)
    branch_rank = jax.random.randint(first_key, (TREES, 4), 0, 8)
    leaf_keys = jax.random.split(second_key, TREES)
    leaf_order = jax.vmap(lambda single: jax.random.permutation(single, 8))(leaf_keys)
    leaf_parent = (leaf_order // 2).astype(jnp.int32)
    lifted = jax.random.randint(third_key, (TREES, 8), 1, 9)
    leaf_rank = jnp.take_along_axis(branch_rank, leaf_parent, axis=1) + lifted
    ranks = jnp.concatenate([branch_rank, leaf_rank], axis=1)
    labels = jnp.arange(1, 13, dtype=jnp.int32)
    ordering = jnp.argsort(ranks * 16 + labels[None, :], axis=1, stable=True)
    items = (ordering + 1).astype(jnp.int32)
    return (items, leaf_parent)


def draw_segments(key, part):
    items, leaf_parent = tree_layout(key)
    offsets = 13 * jnp.arange(TREES, dtype=jnp.int32)[:, None]
    runs = jnp.repeat(items, SEG, axis=1, total_repeat_length=12 * SEG)
    local = jnp.concatenate([jnp.zeros((TREES, TRUNK), jnp.int32), runs], axis=1)
    return (local + offsets).reshape(-1)[:TOKENS].astype(jnp.int32)


def draw_parents(key, part):
    items, leaf_parent = tree_layout(key)
    offsets = 13 * jnp.arange(TREES, dtype=jnp.int32)[:, None]
    local = jnp.concatenate([jnp.zeros((TREES, 5), jnp.int32), leaf_parent + 1], axis=1)
    return (local + offsets).reshape(-1).astype(jnp.int32)


def levels(stream_key, dims, pieces, smallest, largest):
    def one(dim, blocks):
        draws = jax.random.uniform(jax.random.fold_in(jax.random.fold_in(stream_key, 6), dim), (blocks,), jnp.float32, smallest / len(pieces), largest / len(pieces))
        return jnp.repeat(jnp.exp(draws), dims[dim] // blocks).reshape((-1,) + (1,) * (len(dims) - dim - 1))

    loudness = one(*pieces[0])
    for cut in pieces[1:]:
        loudness = loudness * one(*cut)
    return loudness


def centred(own_key, extent, spread, most, pieces=(), held_as=jnp.bfloat16):
    level = levels(own_key, extent, pieces, -0.22, 0.18) if pieces else 1.0
    values = jax.random.normal(own_key, extent, jnp.float32) * spread * level
    return jnp.minimum(jnp.maximum(values, -most), most).astype(held_as)


def setup_inputs(seed: int = 0) -> dict:
    seeds = jax.random.split(jax.random.key(seed), 13)
    return {
        "layer_input": centred(seeds[0], (TOKENS, D), 1.0, 6.0, ((0, 32),)),
        "cotangent": centred(seeds[1], (TOKENS, D), 1.0, 6.0, ((0, 32),)),
        "segments": draw_segments(jax.random.fold_in(seeds[12], 71), 0),
        "parents": draw_parents(jax.random.fold_in(seeds[12], 71), 0),
        "norm1_gain": jnp.clip(1.0 + 0.18 * jax.random.normal(seeds[4], (D,), jnp.float32), 0.099609375, 1.8984375).astype(jnp.bfloat16),
        "w_query": centred(seeds[5], (D, D), D ** -0.5, 0.21875, ((0, 8), (1, 4))),
        "w_key": centred(seeds[6], (D, D), D ** -0.5, 0.21875, ((0, 8), (1, 4))),
        "w_value": centred(seeds[7], (D, D), D ** -0.5, 0.21875, ((0, 8), (1, 4))),
        "w_out": centred(seeds[8], (D, D), (D // 64) ** -0.5, 1.75, ((0, 4), (1, 8))),
        "norm2_gain": jnp.clip(1.0 + 0.18 * jax.random.normal(seeds[9], (D,), jnp.float32), 0.099609375, 1.8984375).astype(jnp.bfloat16),
        "w_up": centred(seeds[10], (D, FF), D ** -0.5, 0.21875, ((0, 8), (1, 4))),
        "w_down": centred(seeds[11], (FF, D), FF ** -0.5, 0.109375, ((0, 4), (1, 8))),
    }


@jax.custom_vjp
def low(v):
    return lax.optimization_barrier(v.astype(jnp.bfloat16)).astype(jnp.float32)

@jax.custom_vjp
def low_back(v):
    return v

def low_keep(v):
    return (low(v), None)

def low_pass(kept, grad):
    return (grad,)

def back_keep(v):
    return (v, None)

def back_low(kept, grad):
    return (low(grad),)
low.defvjp(low_keep, low_pass)
low_back.defvjp(back_keep, back_low)
epsilon = 1e-06
highest = lax.Precision.HIGHEST
masked_score = -1e+30

def product(left, right):
    return jnp.dot(left, right, precision=highest, preferred_element_type=jnp.float32)

def normalized(values, gain):
    factor = lax.rsqrt(lax.optimization_barrier(jnp.mean(values * values, axis=-1, keepdims=True)) + epsilon)
    return values * factor * gain

def tree_attention(queries, keys_all, values_all, seg_tree, parent_one, parent_two):
    tree_len = TRUNK + 12 * SEG
    block_rows = 4 * SEG
    key_spots = jnp.arange(tree_len, dtype=jnp.int32)
    scaling = HD ** (-0.5)

    def one_block(block_index):
        offset = (block_index * block_rows).astype(jnp.int32)
        query_rows = lax.dynamic_slice_in_dim(queries, offset, block_rows, 0)
        query_spots = offset + jnp.arange(block_rows, dtype=jnp.int32)
        seg_query = lax.dynamic_slice_in_dim(seg_tree, offset, block_rows, 0)
        first_up = lax.dynamic_slice_in_dim(parent_one, offset, block_rows, 0)
        second_up = lax.dynamic_slice_in_dim(parent_two, offset, block_rows, 0)
        gap = query_spots[:, None] - key_spots[None, :]
        same_path = (seg_tree[None, :] == seg_query[:, None]) | (seg_tree[None, :] == first_up[:, None]) | (seg_tree[None, :] == second_up[:, None])
        allowed = (gap >= 0) & (gap < WINDOW) & same_path
        raw = jnp.einsum('qhd,khd->hqk', query_rows, keys_all, precision=highest)
        scores = low_back(raw * scaling)
        scores = jnp.where(allowed[None], scores, masked_score)
        weights = low(jax.nn.softmax(scores, axis=-1))
        return jnp.einsum('hqk,khd->qhd', weights, values_all, precision=highest)
    blocks = lax.map(jax.checkpoint(one_block), jnp.arange(tree_len // block_rows, dtype=jnp.int32))
    return blocks.reshape(tree_len, D)

def layer(inputs, seg_tree, parent_one, parent_two, gain_one, w_query, w_key, w_value, w_out, gain_two, w_up, w_down):
    normed = low(normalized(inputs, gain_one))
    queries = low_back(low(product(normed, w_query))).reshape(-1, HEADS, HD)
    keys_all = low_back(low(product(normed, w_key))).reshape(-1, HEADS, HD)
    values_all = low_back(low(product(normed, w_value))).reshape(-1, HEADS, HD)
    context = low_back(low(tree_attention(queries, keys_all, values_all, seg_tree, parent_one, parent_two)))
    middle = inputs + low_back(product(context, w_out))
    normed_two = low(normalized(middle, gain_two))
    upper = low_back(product(normed_two, w_up))
    active = low(jax.nn.gelu(upper, approximate=False))
    return middle + low_back(product(active, w_down))

def reference(layer_input, cotangent, segments, parents, norm1_gain, w_query, w_key, w_value, w_out, norm2_gain, w_up, w_down):
    tree_len = TRUNK + 12 * SEG
    padded_len = TREES * tree_len
    extra = padded_len - TOKENS
    x_all = jnp.concatenate([layer_input.astype(jnp.float32), jnp.zeros((extra, D), jnp.float32)]).reshape(TREES, tree_len, D)
    cot_all = jnp.concatenate([cotangent.astype(jnp.float32), jnp.zeros((extra, D), jnp.float32)]).reshape(TREES, tree_len, D)
    seg_all = jnp.concatenate([segments.astype(jnp.int32), jnp.full((extra,), -1, jnp.int32)])
    first_all = jnp.where(seg_all >= 0, parents[jnp.maximum(seg_all, 0)], -1).astype(jnp.int32)
    second_all = jnp.where(first_all >= 0, parents[jnp.maximum(first_all, 0)], -1).astype(jnp.int32)
    seg_all = seg_all.reshape(TREES, tree_len)
    first_all = first_all.reshape(TREES, tree_len)
    second_all = second_all.reshape(TREES, tree_len)
    weights = tuple((w.astype(jnp.float32) for w in (norm1_gain, w_query, w_key, w_value, w_out, norm2_gain, w_up, w_down)))

    def step(totals, items):
        inputs, cot_tree, seg_tree, parent_one, parent_two = items

        def forward(values, *params):
            return layer(values, seg_tree, parent_one, parent_two, *params)
        result, pull = jax.vjp(forward, inputs, *weights)
        grads = pull(cot_tree)
        updated = tuple((left + right for left, right in zip(totals, grads[1:])))
        return (updated, (result, grads[0]))
    init = tuple((jnp.zeros(w.shape, jnp.float32) for w in weights))
    sums, (results, input_grads) = lax.scan(step, init, (x_all, cot_all, seg_all, first_all, second_all))
    layer_output = results.reshape(padded_len, D)[:TOKENS].astype(jnp.bfloat16)
    input_grad = input_grads.reshape(padded_len, D)[:TOKENS].astype(jnp.bfloat16)
    return (layer_output, input_grad, sums[0], sums[1], sums[2], sums[3], sums[4], sums[5], sums[6], sums[7])
```

```python
import functools
import math

import jax
import jax.numpy as jnp
from jax import lax
from jax.experimental import pallas as pl
from jax.experimental.pallas import tpu as pltpu
from jax.sharding import PartitionSpec as P

MESH = pl.DeviceIdType.MESH
BF = jnp.bfloat16
F32 = jnp.float32
HD = 64
WINDOW = 1536
SEG = 256
TREE = 5120
LOG2E = 1.4426950408889634
NEG = -1e30
EPS = 1e-6


def nt(a, b):
    return lax.dot_general(a, b, (((1,), (1,)), ((), ())), preferred_element_type=F32)


def nn(a, b):
    return jnp.dot(a, b, preferred_element_type=F32)


class Links:
    def __init__(self, send, recv):
        self.send, self.recv, self.used = send, recv, 0

    def take(self, count):
        base = self.used
        self.used += count
        return base

    def copy(self, src, dst, send, recv, device):
        return pltpu.make_async_remote_copy(
            src_ref=src,
            dst_ref=dst,
            send_sem=self.send.at[send],
            recv_sem=self.recv.at[recv],
            device_id=device,
            device_id_type=MESH,
        )


class Spread:
    def __init__(self, links, base, dp, t, part):
        self.dp, self.t = dp, t
        self.out = [
            links.copy(part(t), part(t), base, base, (dp, t ^ 1)),
            links.copy(part(t), part(t), base + 1, base + 1, (dp, t ^ 2)),
            links.copy(part(t ^ 2), part(t ^ 2), base + 2, base + 2, (dp, t ^ 1)),
        ]
        self.arrivals = [
            links.copy(part(t ^ 1), part(t ^ 1), base, base, (dp, t ^ 1)),
            links.copy(part(t ^ 2), part(t ^ 2), base + 1, base + 1, (dp, t ^ 2)),
            links.copy(part(t ^ 3), part(t ^ 3), base + 2, base + 2, (dp, t ^ 1)),
        ]

    def start(self):
        self.out[1].start()
        self.out[0].start()

    def forward(self):
        self.arrivals[1].wait_recv()
        self.out[2].start()

    def wait(self):
        self.arrivals[0].wait_recv()
        self.arrivals[2].wait_recv()

    def finish(self):
        for copy in self.out:
            copy.wait_send()


class Gather:
    def __init__(self, links, base, dp, t, slot):
        self.links, self.base, self.dp, self.t, self.slot = links, base, dp, t, slot
        self.z, self.y = dp // 2, dp % 2

    def at(self, step):
        z = lax.rem(self.z + step, 4)
        return z, z * 2 + self.y

    def along(self, step):
        z, peer = self.at(step)
        return self.links.copy(self.slot(self.dp), self.slot(self.dp), self.base + step - 1, self.base + self.z, (peer, self.t))

    def came(self, step):
        z, peer = self.at(step)
        return self.links.copy(self.slot(peer), self.slot(peer), self.base + step - 1, self.base + z, (peer, self.t))

    def across(self, step):
        z, peer = self.at(step)
        other = z * 2 + (1 - self.y)
        return self.links.copy(self.slot(peer), self.slot(peer), self.base + 4 + step, self.base + 4 + z, (self.dp ^ 1, self.t))

    def crossed(self, step):
        z, peer = self.at(step)
        other = z * 2 + (1 - self.y)
        return self.links.copy(self.slot(other), self.slot(other), self.base + 4 + step, self.base + 4 + z, (self.dp ^ 1, self.t))

    def start(self):
        self.across(0).start()
        for step in (1, 3, 2):
            self.along(step).start()

    def forward(self, step):
        self.came(step).wait_recv()
        self.across(step).start()

    def wait(self):
        for step in range(4):
            self.crossed(step).wait_recv()

    def finish(self):
        for step in range(1, 4):
            self.along(step).wait_send()
        for step in range(4):
            self.across(step).wait_send()


def greet(dp, t):
    barrier = pltpu.get_barrier_semaphore()
    for step in range(1, 8):
        pl.semaphore_signal(barrier, inc=1, device_id=(lax.rem(dp + step, 8), t), device_id_type=MESH)
    for flip in (1, 2):
        pl.semaphore_signal(barrier, inc=1, device_id=(dp, t ^ flip), device_id_type=MESH)
    pl.semaphore_wait(barrier, 9)


def head_mask(h, rows, width):
    lane = lax.broadcasted_iota(jnp.int32, (rows, width), 1)
    return (lane >= h * HD) & (lane < (h + 1) * HD)


def block_bias(seg_ref, par_ref, block, back):
    own = seg_ref[block * SEG]
    one = par_ref[own]
    two = par_ref[one]
    far = block - back
    near = seg_ref[jnp.maximum(far, 0) * SEG]
    ok = ((near == own) | (near == one) | (near == two)) & (far >= 0)
    return jnp.where(ok, jnp.float32(0.0), jnp.float32(NEG))


def first_kernel(
    seg_ref, par_ref, x_ref, cot_ref, wa_ref, wf_ref,
    n1_ref, a_ref, f_ref, cot_all, wout_ref, q_ref, k_ref, v_ref, ct_ref, l_ref, gain_ref,
    xe_ref, wq_ref, wk_ref, wv_ref, vt_ref, s_ref, e_ref, tri_ref, send, recv,
):
    dp, t = lax.axis_index("dp"), lax.axis_index("tensor")
    rows = x_ref.shape[0]
    token = 4 * rows
    blocks = token // SEG
    back = WINDOW // SEG
    lag = WINDOW - token
    per_tree = TREE // token
    place = lax.rem(dp, per_tree)
    links = Links(send, recv)
    own = lambda p: xe_ref.at[pl.ds(WINDOW + p * rows, rows)]
    halo = lambda p: xe_ref.at[pl.ds(lag + p * rows, rows)]
    x_spread = Spread(links, links.take(3), dp, t, own)
    halo_spread = Spread(links, links.take(3), dp, t, halo)
    cot_spread = Spread(links, links.take(3), dp, t, lambda p: cot_all.at[pl.ds(p * rows, rows)])
    wide = wout_ref.shape[0] // 4
    wout_spread = Spread(links, links.take(3), dp, t, lambda p: wout_ref.at[pl.ds(p * wide, wide)])
    a_gather = Gather(links, links.take(8), dp, t, lambda s: a_ref.at[s])
    f_gather = Gather(links, links.take(8), dp, t, lambda s: f_ref.at[s])
    h1 = links.take(1)
    halo_out = links.copy(x_ref, halo(t), h1, h1, (lax.rem(dp + 1, 8), t))
    halo_in = links.copy(x_ref, halo(t), h1, h1, (lax.rem(dp + 7, 8), t))
    h2 = links.take(1)
    far_src = xe_ref.at[pl.ds(WINDOW + token - lag, lag)]
    far_dst = xe_ref.at[pl.ds(0, lag)]
    far_out = links.copy(far_src, far_dst, h2, h2, (lax.rem(dp + 2, 8), t))
    far_in = links.copy(far_src, far_dst, h2, h2, (lax.rem(dp + 6, 8), t))
    c_base = links.take(3 * blocks)

    def c_spread(i):
        at = pl.multiple_of(i * SEG, SEG)
        return Spread(
            links, c_base + 3 * i, dp, t, lambda p: ct_ref.at[pl.ds(p * wide, wide), pl.ds(at, SEG)]
        )

    greet(dp, t)
    a_ref[pl.ds(dp, 1)] = wa_ref[...][None]
    a_gather.start()
    xe_ref[pl.ds(WINDOW + t * rows, rows), :] = x_ref[...]
    x_spread.start()

    @pl.when(place < per_tree - 1)
    def _():
        halo_out.start()

    @pl.when(place < 1)
    def _():
        xe_ref[pl.ds(lag, token), :] = jnp.zeros((token, xe_ref.shape[1]), BF)

    @pl.when(place < 2)
    def _():
        xe_ref[pl.ds(0, lag), :] = jnp.zeros((lag, xe_ref.shape[1]), BF)

    row = lax.broadcasted_iota(jnp.int32, (SEG, SEG), 0)
    col = lax.broadcasted_iota(jnp.int32, (SEG, SEG), 1)
    tri_ref[0] = jnp.where(row <= col, 0.0, NEG)
    tri_ref[1] = jnp.where(row > col, 0.0, NEG)
    cot_all[pl.ds(t * rows, rows), :] = cot_ref[...]
    f_ref[pl.ds(dp, 1)] = wf_ref[...][None]
    x_spread.forward()
    for step in (1, 3, 2):
        a_gather.forward(step)

    @pl.when(place >= 1)
    def _():
        halo_in.wait_recv()
        halo_spread.start()

    x_spread.wait()

    @pl.when(place < per_tree - 2)
    def _():
        far_out.start()

    f_gather.start()
    a_gather.wait()
    cols = wq_ref.shape[1]
    deep = wa_ref.shape[0] - 16
    weights = a_ref[:, 0:deep, :].reshape(8 * deep, 4 * cols)
    wq_ref[...] = weights[:, 0:cols]
    wk_ref[...] = weights[:, cols : 2 * cols]
    wv_ref[...] = weights[:, 2 * cols : 3 * cols]
    wout_ref[pl.ds(t * wide, wide), :] = weights[:, 3 * cols : 4 * cols].T
    gains = jnp.sum(a_ref[:, deep : deep + 16, :].astype(F32), axis=0)
    gain_ref[...] = gains[0:8]

    def norm_rows(at):
        x = xe_ref[pl.ds(at, SEG), :].astype(F32)
        r = lax.rsqrt(jnp.mean(x * x, axis=-1, keepdims=True) + EPS)
        n = (x * r * gain_ref[0:1, :]).astype(BF)
        n1_ref[pl.ds(at, SEG), :] = n
        k_ref[pl.ds(at, SEG), :] = nn(n, wk_ref[...]).astype(BF)
        v = nn(n, wv_ref[...]).astype(BF)
        v_ref[pl.ds(at, SEG), :] = v
        vt_ref[:, pl.ds(at, SEG)] = v.T
        return n

    def own_rows(i, _):
        at = pl.multiple_of(i * SEG, SEG)
        n = norm_rows(WINDOW + at)
        q_ref[pl.ds(at, SEG), :] = (nn(n, wq_ref[...]).astype(BF).astype(F32) * HD**-0.5).astype(BF)
        return 0

    lax.fori_loop(0, blocks, own_rows, 0)

    @pl.when(place >= 1)
    def _():
        halo_spread.forward()
        halo_spread.wait()

    wout_spread.start()
    cot_spread.start()

    @pl.when(place >= 2)
    def _():
        far_in.wait_recv()

    def halo_rows(i, _):
        norm_rows(pl.multiple_of(i * SEG, SEG))
        return 0

    lax.fori_loop(0, back, halo_rows, 0)

    def attend(i, _):
        at = pl.multiple_of(i * SEG, SEG)
        block = dp * blocks + i
        biases = [block_bias(seg_ref, par_ref, block, back - j) for j in range(back + 1)]
        q = q_ref[pl.ds(at, SEG), :]
        for h in range(3):
            qm = jnp.where(head_mask(h, SEG, cols), q, jnp.zeros_like(q))
            top = None
            for j in range(back + 1):
                s = nt(k_ref[pl.ds(at + j * SEG, SEG), :], qm)
                if j == 0:
                    s = s + tri_ref[1]
                if j == back:
                    s = s + tri_ref[0]
                s_ref[h, j * SEG : (j + 1) * SEG, :] = s
                best = jnp.max(s, axis=0, keepdims=True) + biases[j]
                top = best if top is None else jnp.maximum(top, best)
            top = top * LOG2E
            total = None
            for j in range(back + 1):
                e = jnp.exp2(s_ref[h, j * SEG : (j + 1) * SEG, :] * LOG2E - (top - biases[j]))
                part = jnp.sum(e, axis=0, keepdims=True)
                total = part if total is None else total + part
                e_ref[h, j * SEG : (j + 1) * SEG, :] = e.astype(BF)
            o = nn(vt_ref[h * HD : (h + 1) * HD, pl.ds(at, (back + 1) * SEG)], e_ref[h])
            ct_ref[pl.ds(t * wide + h * HD, HD), pl.ds(at, SEG)] = (o / total).astype(BF)
            l_ref[h : h + 1, pl.ds(at, SEG)] = top + jnp.log(total) * LOG2E
        c_spread(i).start()

        @pl.when(i > 0)
        def _():
            c_spread(i - 1).forward()

        @pl.when(i == 1)
        def _():
            for step in (1, 3, 2):
                f_gather.forward(step)

        return 0

    lax.fori_loop(0, blocks, attend, 0)
    c_spread(blocks - 1).forward()
    for i in range(blocks):
        c_spread(i).wait()
    wout_spread.forward()
    cot_spread.forward()
    wout_spread.wait()
    cot_spread.wait()
    f_gather.wait()
    for item in (x_spread, cot_spread, wout_spread, a_gather, f_gather):
        item.finish()
    for i in range(blocks):
        c_spread(i).finish()

    @pl.when(place >= 1)
    def _():
        halo_spread.finish()

    @pl.when(place < per_tree - 1)
    def _():
        halo_out.wait_send()

    @pl.when(place < per_tree - 2)
    def _():
        far_out.wait_send()


def first_phase(x, cot, segments, parents, wa, wf):
    rows, width = x.shape
    token = 4 * rows
    ext = token + WINDOW
    cols = width // 4
    blocks = token // SEG
    keys = WINDOW + SEG
    vmem = pl.BlockSpec(memory_space=pltpu.VMEM)
    smem = pl.BlockSpec(memory_space=pltpu.SMEM)
    copies = 3 * 4 + 2 * 8 + 2 + 3 * blocks
    return pl.pallas_call(
        first_kernel,
        out_shape=[
            jax.ShapeDtypeStruct((ext, width), BF),
            jax.ShapeDtypeStruct((8,) + wa.shape, BF),
            jax.ShapeDtypeStruct((8,) + wf.shape, BF),
            jax.ShapeDtypeStruct((token, width), BF),
            jax.ShapeDtypeStruct((width, width), BF),
            jax.ShapeDtypeStruct((token, cols), BF),
            jax.ShapeDtypeStruct((ext, cols), BF),
            jax.ShapeDtypeStruct((ext, cols), BF),
            jax.ShapeDtypeStruct((width, token), BF),
            jax.ShapeDtypeStruct((8, token), F32),
            jax.ShapeDtypeStruct((8, width), F32),
        ],
        in_specs=[smem, smem, vmem, vmem, vmem, vmem],
        out_specs=[vmem] * 11,
        scratch_shapes=[
            pltpu.VMEM((ext, width), BF),
            pltpu.VMEM((width, cols), BF),
            pltpu.VMEM((width, cols), BF),
            pltpu.VMEM((width, cols), BF),
            pltpu.VMEM((cols, ext), BF),
            pltpu.VMEM((3, keys, SEG), F32),
            pltpu.VMEM((3, keys, SEG), BF),
            pltpu.VMEM((2, SEG, SEG), F32),
            pltpu.SemaphoreType.DMA((copies,)),
            pltpu.SemaphoreType.DMA((copies,)),
        ],
        compiler_params=pltpu.CompilerParams(
            collective_id=0, has_side_effects=True, vmem_limit_bytes=56 << 20
        ),
    )(segments, parents, x, cot, wa, wf)


epsilon = 1e-06
masked_score = -1e30


def from_behind(block, axis, distance):
    devices = range(lax.axis_size(axis))
    route = [(i - distance, i) for i in devices if i - distance in devices]
    return lax.ppermute(block, axis, route)


def split_up(x, dim, peers):
    dims = x.shape
    tiles = x.reshape(*dims[:dim], peers, dims[dim] // peers, *dims[dim + 1 :])
    return jnp.moveaxis(tiles, dim, 0)


def sum_at_owner(x, axis, dim):
    tiles = split_up(x, dim, lax.axis_size(axis))
    arrived = lax.all_to_all(tiles, axis, split_axis=0, concat_axis=0, tiled=True)
    return arrived.astype(jnp.float32).sum(axis=0)


def side_by_side(arrays, axis, dim, along):
    widths = [math.prod(a.shape[along:]) for a in arrays]
    both = jnp.concatenate(
        [a.reshape(*a.shape[:along], w) for a, w in zip(arrays, widths)], axis=along
    )
    whole = sum_at_owner(both, axis, dim)
    tiles = jnp.split(whole, [sum(widths[:k]) for k in range(1, len(widths))], axis=along)
    return tuple((b.reshape(*whole.shape[:along], *a.shape[along:]) for a, b in zip(arrays, tiles)))


def gelu_exact(values):
    return jax.nn.gelu(values, approximate=False)


def row_scale(values):
    return lax.rsqrt(jnp.mean(values * values, axis=-1, keepdims=True) + epsilon)


def norm_backward(incoming, normal_hat, row_factor, gain):
    scaled = incoming * gain
    inner = jnp.mean(scaled * normal_hat, axis=-1, keepdims=True)
    return (row_factor * (scaled - normal_hat * inner), jnp.sum(incoming * normal_hat, axis=0))


def parent_of(seg_ids, parents):
    seg_table = jnp.arange(parents.shape[0], dtype=jnp.int32)
    hits = seg_ids[:, None] == seg_table[None, :]
    return jnp.sum(jnp.where(hits, parents[None, :], 0), axis=1)


def shards(
    layer_input,
    cotangent,
    segments,
    parents,
    norm1_gain,
    w_query,
    w_key,
    w_value,
    w_out,
    norm2_gain,
    w_up,
    w_down,
):
    gain_one, full_query, full_key, full_value, full_out, gain_two, full_up, full_down = (
        lax.all_gather(norm1_gain, "dp", axis=0, tiled=True),
        lax.all_gather(w_query, "dp", axis=0, tiled=True),
        lax.all_gather(w_key, "dp", axis=0, tiled=True),
        lax.all_gather(w_value, "dp", axis=0, tiled=True),
        lax.all_gather(w_out, "dp", axis=1, tiled=True),
        lax.all_gather(norm2_gain, "dp", axis=0, tiled=True),
        lax.all_gather(w_up, "dp", axis=0, tiled=True),
        lax.all_gather(w_down, "dp", axis=1, tiled=True),
    )
    gain_one = gain_one.astype(jnp.float32)
    gain_two = gain_two.astype(jnp.float32)
    row_count = layer_input.shape[0]
    token_count = row_count * lax.axis_size("tensor")
    position = lax.axis_index("dp") * token_count
    head_width = full_query.shape[1]
    head_count = head_width // HD
    scaling = HD ** (-0.5)
    block_rows = min(640, token_count)
    block_count = token_count // block_rows
    span = WINDOW + block_rows
    hop_count = (WINDOW + token_count - 1) // token_count
    inputs = layer_input.astype(jnp.float32)
    factor_one = row_scale(inputs)
    hat_one = inputs * factor_one
    normed = (hat_one * gain_one).astype(jnp.bfloat16)
    normed_all = lax.all_gather(normed, "tensor", axis=0, tiled=True)
    queries = jnp.dot(normed_all, full_query, preferred_element_type=jnp.float32).astype(
        jnp.bfloat16
    )
    keys_own = jnp.dot(normed_all, full_key, preferred_element_type=jnp.float32).astype(
        jnp.bfloat16
    )
    values_own = jnp.dot(normed_all, full_value, preferred_element_type=jnp.float32).astype(
        jnp.bfloat16
    )
    pair_own = jnp.concatenate([keys_own, values_own], axis=1)
    halo_parts = []
    for distance in range(1, hop_count + 1):
        length = min(token_count, WINDOW - (distance - 1) * token_count)
        piece = pair_own[token_count - length :]
        moved = from_behind(piece, "dp", distance)
        halo_parts.append(moved)
    pair_all = jnp.concatenate(halo_parts[::-1] + [pair_own], axis=0)
    seg_padded = jnp.concatenate([jnp.full((WINDOW,), -1, jnp.int32), segments])
    seg_keys = lax.dynamic_slice_in_dim(seg_padded, position, WINDOW + token_count, 0)
    seg_query = seg_keys[WINDOW:]
    parent_one = parent_of(seg_query, parents)
    parent_two = parent_of(parent_one, parents)
    query_spots = jnp.arange(block_rows, dtype=jnp.int32)
    key_spots = jnp.arange(span, dtype=jnp.int32)

    def scores_of(offset):
        query_block = lax.dynamic_slice_in_dim(queries, offset, block_rows, 0).reshape(
            block_rows, head_count, HD
        )
        pair_block = lax.dynamic_slice_in_dim(pair_all, offset, span, 0)
        key_block = pair_block[:, :head_width].reshape(span, head_count, HD)
        value_block = pair_block[:, head_width:].reshape(span, head_count, HD)
        own_seg = lax.dynamic_slice_in_dim(seg_query, offset, block_rows, 0)
        up_one = lax.dynamic_slice_in_dim(parent_one, offset, block_rows, 0)
        up_two = lax.dynamic_slice_in_dim(parent_two, offset, block_rows, 0)
        near_seg = lax.dynamic_slice_in_dim(seg_keys, offset, span, 0)
        gap = WINDOW + query_spots[:, None] - key_spots[None, :]
        same_path = (
            (near_seg[None, :] == own_seg[:, None])
            | (near_seg[None, :] == up_one[:, None])
            | (near_seg[None, :] == up_two[:, None])
        )
        allowed = (gap >= 0) & (gap < WINDOW) & same_path
        raw = (
            jnp.einsum("qhd,khd->hqk", query_block, key_block, preferred_element_type=jnp.float32)
            * scaling
        )
        return (jnp.where(allowed[None], raw, masked_score), query_block, key_block, value_block)

    def forward_block(block_index):
        scores, query_block, key_block, value_block = scores_of(block_index * block_rows)
        row_max = jnp.max(scores, axis=-1, keepdims=True)
        exponent = jnp.exp(scores - row_max)
        denominator = jnp.sum(exponent, axis=-1, keepdims=True)
        weights = (exponent / denominator).astype(jnp.bfloat16)
        mixed = jnp.einsum("hqk,khd->qhd", weights, value_block, preferred_element_type=jnp.float32)
        return (
            mixed.reshape(block_rows, head_width).astype(jnp.bfloat16),
            (row_max + jnp.log(denominator))[..., 0],
        )

    context_blocks, logsum_blocks = lax.map(forward_block, jnp.arange(block_count, dtype=jnp.int32))
    context = context_blocks.reshape(token_count, head_width)
    middle = inputs + lax.psum_scatter(
        jnp.dot(context, full_out, preferred_element_type=jnp.float32).astype(jnp.bfloat16),
        "tensor",
        scatter_dimension=0,
        tiled=True,
    ).astype(jnp.float32)
    factor_two = row_scale(middle)
    hat_two = middle * factor_two
    normed_two = (hat_two * gain_two).astype(jnp.bfloat16)
    normed_two_all = lax.all_gather(normed_two, "tensor", axis=0, tiled=True)
    upper = jnp.dot(normed_two_all, full_up, preferred_element_type=jnp.float32)
    active = gelu_exact(upper).astype(jnp.bfloat16)
    result = middle + lax.psum_scatter(
        jnp.dot(active, full_down, preferred_element_type=jnp.float32).astype(jnp.bfloat16),
        "tensor",
        scatter_dimension=0,
        tiled=True,
    ).astype(jnp.float32)
    incoming = cotangent.astype(jnp.float32)
    incoming_all = lax.all_gather(cotangent, "tensor", axis=0, tiled=True)
    grad_down = jnp.einsum("tf,td->fd", active, incoming_all, preferred_element_type=jnp.float32)
    grad_active = jnp.einsum(
        "td,fd->tf", incoming_all, full_down, preferred_element_type=jnp.float32
    )
    unused_value, gelu_pull = jax.vjp(gelu_exact, upper)
    grad_upper = gelu_pull(grad_active)[0].astype(jnp.bfloat16)
    grad_up = jnp.einsum(
        "tc,tf->cf", normed_two_all, grad_upper, preferred_element_type=jnp.float32
    )
    grad_normed_two = lax.psum_scatter(
        jnp.einsum("tf,cf->tc", grad_upper, full_up, preferred_element_type=jnp.float32).astype(
            jnp.bfloat16
        ),
        "tensor",
        scatter_dimension=0,
        tiled=True,
    ).astype(jnp.float32)
    through_two, gain_two_part = norm_backward(grad_normed_two, hat_two, factor_two, gain_two)
    grad_middle = incoming + through_two
    grad_middle_all = lax.all_gather(grad_middle.astype(jnp.bfloat16), "tensor", axis=0, tiled=True)
    grad_out = jnp.einsum("tc,td->cd", context, grad_middle_all, preferred_element_type=jnp.float32)
    grad_context = jnp.einsum(
        "td,cd->tc", grad_middle_all, full_out, preferred_element_type=jnp.float32
    ).astype(jnp.bfloat16)

    def backward_block(block_index, carry):
        grad_queries, grad_pairs = carry
        offset = block_index * block_rows
        scores, query_block, key_block, value_block = scores_of(offset)
        logsum = lax.dynamic_index_in_dim(logsum_blocks, block_index, 0, keepdims=False)
        probs = jnp.exp(scores - logsum[..., None])
        grad_rows = lax.dynamic_slice_in_dim(grad_context, offset, block_rows, 0).reshape(
            block_rows, head_count, HD
        )
        grad_probs = jnp.einsum(
            "qhd,khd->hqk", grad_rows, value_block, preferred_element_type=jnp.float32
        )
        inner = jnp.sum(probs * grad_probs, axis=-1, keepdims=True)
        grad_scores = (probs * (grad_probs - inner)).astype(jnp.bfloat16)
        grad_query_block = (
            jnp.einsum("hqk,khd->qhd", grad_scores, key_block, preferred_element_type=jnp.float32)
            * scaling
        )
        grad_key_block = (
            jnp.einsum("hqk,qhd->khd", grad_scores, query_block, preferred_element_type=jnp.float32)
            * scaling
        )
        grad_value_block = jnp.einsum(
            "hqk,qhd->khd",
            probs.astype(jnp.bfloat16),
            grad_rows,
            preferred_element_type=jnp.float32,
        )
        grad_queries = lax.dynamic_update_slice_in_dim(
            grad_queries, grad_query_block.reshape(block_rows, head_width), offset, 0
        )
        update = jnp.concatenate(
            [grad_key_block.reshape(span, head_width), grad_value_block.reshape(span, head_width)],
            axis=1,
        )
        current = lax.dynamic_slice_in_dim(grad_pairs, offset, span, 0)
        grad_pairs = lax.dynamic_update_slice_in_dim(grad_pairs, current + update, offset, 0)
        return (grad_queries, grad_pairs)

    start_carry = (
        jnp.zeros((token_count, head_width), jnp.float32),
        jnp.zeros((WINDOW + token_count, 2 * head_width), jnp.float32),
    )
    grad_queries, grad_pairs = lax.fori_loop(0, block_count, backward_block, start_carry)
    grad_own = grad_pairs[WINDOW:]
    for distance in range(1, hop_count + 1):
        length = min(token_count, WINDOW - (distance - 1) * token_count)
        first_row = WINDOW - (distance - 1) * token_count - length
        piece = grad_pairs[first_row : first_row + length]
        returned = from_behind(piece.astype(jnp.bfloat16), "dp", -distance).astype(piece.dtype)
        grad_own = grad_own + jnp.pad(returned, ((token_count - length, 0), (0, 0)))
    grad_keys = grad_own[:, :head_width].astype(jnp.bfloat16)
    grad_values = grad_own[:, head_width:].astype(jnp.bfloat16)
    grad_queries_low = grad_queries.astype(jnp.bfloat16)
    grad_query = jnp.einsum(
        "tc,tq->cq", normed_all, grad_queries_low, preferred_element_type=jnp.float32
    )
    grad_key = jnp.einsum("tc,tq->cq", normed_all, grad_keys, preferred_element_type=jnp.float32)
    grad_value = jnp.einsum(
        "tc,tq->cq", normed_all, grad_values, preferred_element_type=jnp.float32
    )
    part_query = jnp.einsum(
        "tq,cq->tc", grad_queries_low, full_query, preferred_element_type=jnp.float32
    )
    part_key = jnp.einsum("tq,cq->tc", grad_keys, full_key, preferred_element_type=jnp.float32)
    part_value = jnp.einsum(
        "tq,cq->tc", grad_values, full_value, preferred_element_type=jnp.float32
    )
    grad_normed = lax.psum_scatter(
        (part_query + part_key + part_value).astype(jnp.bfloat16),
        "tensor",
        scatter_dimension=0,
        tiled=True,
    ).astype(jnp.float32)
    through_one, gain_one_part = norm_backward(grad_normed, hat_one, factor_one, gain_one)
    grad_inputs = grad_middle + through_one
    gain_one_sum, gain_two_sum = lax.psum((gain_one_part, gain_two_part), "tensor")
    summed = (
        *side_by_side(
            (
                gain_one_sum.astype(jnp.bfloat16),
                grad_query.astype(jnp.bfloat16),
                grad_key.astype(jnp.bfloat16),
                grad_value.astype(jnp.bfloat16),
            ),
            "dp",
            0,
            1,
        ),
        sum_at_owner(grad_out.astype(jnp.bfloat16), "dp", 1),
        *side_by_side(
            (gain_two_sum.astype(jnp.bfloat16), grad_up.astype(jnp.bfloat16)), "dp", 0, 1
        ),
        sum_at_owner(grad_down.astype(jnp.bfloat16), "dp", 1),
    )
    return (
        result.astype(jnp.bfloat16),
        grad_inputs.astype(jnp.bfloat16),
        summed[0],
        summed[1],
        summed[2],
        summed[3],
        summed[4],
        summed[5],
        summed[6],
        summed[7],
    )


def fast_shards(
    layer_input, cotangent, segments, parents, norm1_gain, w_query, w_key, w_value, w_out, norm2_gain, w_up, w_down,
):
    dp = lax.axis_index("dp")
    width = layer_input.shape[1]
    gains = jnp.zeros((16, width), BF)
    gains = lax.dynamic_update_slice(gains, norm1_gain[None], (0, dp * norm1_gain.shape[0]))
    gains = lax.dynamic_update_slice(gains, norm2_gain[None], (1, dp * norm1_gain.shape[0]))
    wa = jnp.concatenate([jnp.concatenate([w_query, w_key, w_value, w_out.T], axis=1), gains], axis=0)
    wf = jnp.concatenate([w_up, w_down.T], axis=1)
    n1, a_all, f_all, incoming_all, wout, queries, keys, values, ct, logs, gain = first_phase(
        layer_input, cotangent, segments, parents, wa, wf
    )
    deep = w_query.shape[0]
    weights = a_all[:, :deep].reshape(width, width)
    full_query, full_key, full_value = weights[:, :192], weights[:, 192:384], weights[:, 384:576]
    full_out = weights[:, 576:].T
    ffn = f_all.reshape(width, -1)
    full_up, full_down = ffn[:, :768], ffn[:, 768:].T
    gain_one, gain_two = gain[0], gain[1]
    row_count = layer_input.shape[0]
    token_count = row_count * lax.axis_size("tensor")
    position = lax.axis_index("dp") * token_count
    head_width = full_query.shape[1]
    head_count = head_width // HD
    scaling = HD ** (-0.5)
    block_rows = min(640, token_count)
    block_count = token_count // block_rows
    span = WINDOW + block_rows
    hop_count = (WINDOW + token_count - 1) // token_count
    inputs = layer_input.astype(jnp.float32)
    factor_one = row_scale(inputs)
    hat_one = inputs * factor_one
    normed_all = n1[WINDOW:]
    pair_all = jnp.concatenate([keys, values], axis=1)
    seg_padded = jnp.concatenate([jnp.full((WINDOW,), -1, jnp.int32), segments])
    seg_keys = lax.dynamic_slice_in_dim(seg_padded, position, WINDOW + token_count, 0)
    seg_query = seg_keys[WINDOW:]
    parent_one = parent_of(seg_query, parents)
    parent_two = parent_of(parent_one, parents)
    query_spots = jnp.arange(block_rows, dtype=jnp.int32)
    key_spots = jnp.arange(span, dtype=jnp.int32)

    def scores_of(offset):
        query_block = lax.dynamic_slice_in_dim(queries, offset, block_rows, 0).reshape(
            block_rows, head_count, HD
        )
        pair_block = lax.dynamic_slice_in_dim(pair_all, offset, span, 0)
        key_block = pair_block[:, :head_width].reshape(span, head_count, HD)
        value_block = pair_block[:, head_width:].reshape(span, head_count, HD)
        own_seg = lax.dynamic_slice_in_dim(seg_query, offset, block_rows, 0)
        up_one = lax.dynamic_slice_in_dim(parent_one, offset, block_rows, 0)
        up_two = lax.dynamic_slice_in_dim(parent_two, offset, block_rows, 0)
        near_seg = lax.dynamic_slice_in_dim(seg_keys, offset, span, 0)
        gap = WINDOW + query_spots[:, None] - key_spots[None, :]
        same_path = (
            (near_seg[None, :] == own_seg[:, None])
            | (near_seg[None, :] == up_one[:, None])
            | (near_seg[None, :] == up_two[:, None])
        )
        allowed = (gap >= 0) & (gap < WINDOW) & same_path
        raw = (
            jnp.einsum("qhd,khd->hqk", query_block, key_block, preferred_element_type=jnp.float32)
        )
        return (jnp.where(allowed[None], raw, masked_score), query_block, key_block, value_block)

    t = lax.axis_index("tensor")
    context = lax.dynamic_slice_in_dim(ct, t * 192, 192, 0).T
    logsum_blocks = (logs[:3] / LOG2E).reshape(3, block_count, block_rows).transpose(1, 0, 2)
    middle = inputs + lax.psum_scatter(
        jnp.dot(context, full_out, preferred_element_type=jnp.float32).astype(jnp.bfloat16),
        "tensor",
        scatter_dimension=0,
        tiled=True,
    ).astype(jnp.float32)
    factor_two = row_scale(middle)
    hat_two = middle * factor_two
    normed_two = (hat_two * gain_two).astype(jnp.bfloat16)
    normed_two_all = lax.all_gather(normed_two, "tensor", axis=0, tiled=True)
    upper = jnp.dot(normed_two_all, full_up, preferred_element_type=jnp.float32)
    active = gelu_exact(upper).astype(jnp.bfloat16)
    result = middle + lax.psum_scatter(
        jnp.dot(active, full_down, preferred_element_type=jnp.float32).astype(jnp.bfloat16),
        "tensor",
        scatter_dimension=0,
        tiled=True,
    ).astype(jnp.float32)
    incoming = cotangent.astype(jnp.float32)
    grad_down = jnp.einsum("tf,td->fd", active, incoming_all, preferred_element_type=jnp.float32)
    grad_active = jnp.einsum(
        "td,fd->tf", incoming_all, full_down, preferred_element_type=jnp.float32
    )
    unused_value, gelu_pull = jax.vjp(gelu_exact, upper)
    grad_upper = gelu_pull(grad_active)[0].astype(jnp.bfloat16)
    grad_up = jnp.einsum(
        "tc,tf->cf", normed_two_all, grad_upper, preferred_element_type=jnp.float32
    )
    grad_normed_two = lax.psum_scatter(
        jnp.einsum("tf,cf->tc", grad_upper, full_up, preferred_element_type=jnp.float32).astype(
            jnp.bfloat16
        ),
        "tensor",
        scatter_dimension=0,
        tiled=True,
    ).astype(jnp.float32)
    through_two, gain_two_part = norm_backward(grad_normed_two, hat_two, factor_two, gain_two)
    grad_middle = incoming + through_two
    grad_middle_all = lax.all_gather(grad_middle.astype(jnp.bfloat16), "tensor", axis=0, tiled=True)
    grad_out = jnp.einsum("tc,td->cd", context, grad_middle_all, preferred_element_type=jnp.float32)
    grad_context = jnp.einsum(
        "td,cd->tc", grad_middle_all, full_out, preferred_element_type=jnp.float32
    ).astype(jnp.bfloat16)

    def backward_block(block_index, carry):
        grad_queries, grad_pairs = carry
        offset = block_index * block_rows
        scores, query_block, key_block, value_block = scores_of(offset)
        logsum = lax.dynamic_index_in_dim(logsum_blocks, block_index, 0, keepdims=False)
        probs = jnp.exp(scores - logsum[..., None])
        grad_rows = lax.dynamic_slice_in_dim(grad_context, offset, block_rows, 0).reshape(
            block_rows, head_count, HD
        )
        grad_probs = jnp.einsum(
            "qhd,khd->hqk", grad_rows, value_block, preferred_element_type=jnp.float32
        )
        inner = jnp.sum(probs * grad_probs, axis=-1, keepdims=True)
        grad_scores = (probs * (grad_probs - inner)).astype(jnp.bfloat16)
        grad_query_block = (
            jnp.einsum("hqk,khd->qhd", grad_scores, key_block, preferred_element_type=jnp.float32)
            * scaling
        )
        grad_key_block = jnp.einsum("hqk,qhd->khd", grad_scores, query_block, preferred_element_type=jnp.float32)
        grad_value_block = jnp.einsum(
            "hqk,qhd->khd",
            probs.astype(jnp.bfloat16),
            grad_rows,
            preferred_element_type=jnp.float32,
        )
        grad_queries = lax.dynamic_update_slice_in_dim(
            grad_queries, grad_query_block.reshape(block_rows, head_width), offset, 0
        )
        update = jnp.concatenate(
            [grad_key_block.reshape(span, head_width), grad_value_block.reshape(span, head_width)],
            axis=1,
        )
        current = lax.dynamic_slice_in_dim(grad_pairs, offset, span, 0)
        grad_pairs = lax.dynamic_update_slice_in_dim(grad_pairs, current + update, offset, 0)
        return (grad_queries, grad_pairs)

    start_carry = (
        jnp.zeros((token_count, head_width), jnp.float32),
        jnp.zeros((WINDOW + token_count, 2 * head_width), jnp.float32),
    )
    grad_queries, grad_pairs = lax.fori_loop(0, block_count, backward_block, start_carry)
    grad_own = grad_pairs[WINDOW:]
    for distance in range(1, hop_count + 1):
        length = min(token_count, WINDOW - (distance - 1) * token_count)
        first_row = WINDOW - (distance - 1) * token_count - length
        piece = grad_pairs[first_row : first_row + length]
        returned = from_behind(piece.astype(jnp.bfloat16), "dp", -distance).astype(piece.dtype)
        grad_own = grad_own + jnp.pad(returned, ((token_count - length, 0), (0, 0)))
    grad_keys = grad_own[:, :head_width].astype(jnp.bfloat16)
    grad_values = grad_own[:, head_width:].astype(jnp.bfloat16)
    grad_queries_low = grad_queries.astype(jnp.bfloat16)
    grad_query = jnp.einsum(
        "tc,tq->cq", normed_all, grad_queries_low, preferred_element_type=jnp.float32
    )
    grad_key = jnp.einsum("tc,tq->cq", normed_all, grad_keys, preferred_element_type=jnp.float32)
    grad_value = jnp.einsum(
        "tc,tq->cq", normed_all, grad_values, preferred_element_type=jnp.float32
    )
    part_query = jnp.einsum(
        "tq,cq->tc", grad_queries_low, full_query, preferred_element_type=jnp.float32
    )
    part_key = jnp.einsum("tq,cq->tc", grad_keys, full_key, preferred_element_type=jnp.float32)
    part_value = jnp.einsum(
        "tq,cq->tc", grad_values, full_value, preferred_element_type=jnp.float32
    )
    grad_normed = lax.psum_scatter(
        (part_query + part_key + part_value).astype(jnp.bfloat16),
        "tensor",
        scatter_dimension=0,
        tiled=True,
    ).astype(jnp.float32)
    through_one, gain_one_part = norm_backward(grad_normed, hat_one, factor_one, gain_one)
    grad_inputs = grad_middle + through_one
    gain_one_sum, gain_two_sum = lax.psum((gain_one_part, gain_two_part), "tensor")
    summed = (
        *side_by_side(
            (
                gain_one_sum.astype(jnp.bfloat16),
                grad_query.astype(jnp.bfloat16),
                grad_key.astype(jnp.bfloat16),
                grad_value.astype(jnp.bfloat16),
            ),
            "dp",
            0,
            1,
        ),
        sum_at_owner(grad_out.astype(jnp.bfloat16), "dp", 1),
        *side_by_side(
            (gain_two_sum.astype(jnp.bfloat16), grad_up.astype(jnp.bfloat16)), "dp", 0, 1
        ),
        sum_at_owner(grad_down.astype(jnp.bfloat16), "dp", 1),
    )
    return (
        result.astype(jnp.bfloat16),
        grad_inputs.astype(jnp.bfloat16),
        summed[0],
        summed[1],
        summed[2],
        summed[3],
        summed[4],
        summed[5],
        summed[6],
        summed[7],
    )


def solution(mesh):
    fast = mesh.shape["dp"] == 8 and mesh.shape["tensor"] == 4
    return jax.shard_map(
        fast_shards if fast else shards,
        mesh=mesh,
        in_specs=(
            P(("dp", "tensor"), None),
            P(("dp", "tensor"), None),
            P(),
            P(),
            P("dp"),
            P("dp", "tensor"),
            P("dp", "tensor"),
            P("dp", "tensor"),
            P("tensor", "dp"),
            P("dp"),
            P("dp", "tensor"),
            P("tensor", "dp"),
        ),
        out_specs=(
            P(("dp", "tensor"), None),
            P(("dp", "tensor"), None),
            P("dp"),
            P("dp", "tensor"),
            P("dp", "tensor"),
            P("dp", "tensor"),
            P("tensor", "dp"),
            P("dp"),
            P("dp", "tensor"),
            P("tensor", "dp"),
        ),
        check_vma=False,
    )
```

```python
import functools
import math

import jax
import jax.numpy as jnp
from jax import lax
from jax.experimental import pallas as pl
from jax.experimental.pallas import tpu as pltpu
from jax.sharding import PartitionSpec as P

MESH = pl.DeviceIdType.MESH
BF = jnp.bfloat16
F32 = jnp.float32
HD = 64
WINDOW = 1536
SEG = 256
TREE = 5120
LOG2E = 1.4426950408889634
NEG = -1e30
EPS = 1e-6


def nt(a, b):
    return lax.dot_general(a, b, (((1,), (1,)), ((), ())), preferred_element_type=F32)


def nn(a, b):
    return jnp.dot(a, b, preferred_element_type=F32)


def tn(a, b):
    return lax.dot_general(a, b, (((0,), (0,)), ((), ())), preferred_element_type=F32)


class Links:
    def __init__(self, send, recv):
        self.send, self.recv, self.used = send, recv, 0

    def take(self, count):
        base = self.used
        self.used += count
        return base

    def copy(self, src, dst, send, recv, device):
        return pltpu.make_async_remote_copy(
            src_ref=src,
            dst_ref=dst,
            send_sem=self.send.at[send],
            recv_sem=self.recv.at[recv],
            device_id=device,
            device_id_type=MESH,
        )


class Spread:
    def __init__(self, links, base, dp, t, part):
        self.links, self.base, self.dp, self.t, self.part = links, base, dp, t, part

    def leave(self, i):
        flip, what = ((1, 0), (2, 0), (1, 2))[i]
        ref = self.part(self.t ^ what)
        return self.links.copy(ref, ref, self.base + i, self.base + i, (self.dp, self.t ^ flip))

    def come(self, i):
        flip, what = ((1, 1), (2, 2), (1, 3))[i]
        ref = self.part(self.t ^ what)
        return self.links.copy(ref, ref, self.base + i, self.base + i, (self.dp, self.t ^ flip))

    def start(self):
        self.leave(1).start()
        self.leave(0).start()

    def forward(self):
        self.come(1).wait_recv()
        self.leave(2).start()

    def wait(self):
        self.come(0).wait_recv()
        self.come(2).wait_recv()

    def finish(self):
        for i in range(3):
            self.leave(i).wait_send()


class Gather:
    def __init__(self, links, base, dp, t, slot):
        self.links, self.base, self.dp, self.t, self.slot = links, base, dp, t, slot
        self.z, self.y = dp // 2, dp % 2

    def at(self, step):
        z = lax.rem(self.z + step, 4)
        return z, z * 2 + self.y

    def along(self, step):
        z, peer = self.at(step)
        return self.links.copy(self.slot(self.dp), self.slot(self.dp), self.base + step - 1, self.base + self.z, (peer, self.t))

    def came(self, step):
        z, peer = self.at(step)
        return self.links.copy(self.slot(peer), self.slot(peer), self.base + step - 1, self.base + z, (peer, self.t))

    def across(self, step):
        z, peer = self.at(step)
        return self.links.copy(self.slot(peer), self.slot(peer), self.base + 4 + step, self.base + 4 + z, (self.dp ^ 1, self.t))

    def crossed(self, step):
        z, peer = self.at(step)
        other = z * 2 + (1 - self.y)
        return self.links.copy(self.slot(other), self.slot(other), self.base + 4 + step, self.base + 4 + z, (self.dp ^ 1, self.t))

    def start(self):
        self.across(0).start()
        for step in (1, 3, 2):
            self.along(step).start()

    def forward(self, step):
        self.came(step).wait_recv()
        self.across(step).start()

    def wait(self):
        for step in range(4):
            self.crossed(step).wait_recv()

    def finish(self):
        for step in range(1, 4):
            self.along(step).wait_send()
        for step in range(4):
            self.across(step).wait_send()


def greet(dp, t):
    barrier = pltpu.get_barrier_semaphore()
    for step in range(1, 8):
        pl.semaphore_signal(barrier, inc=1, device_id=(lax.rem(dp + step, 8), t), device_id_type=MESH)
    for flip in (1, 2, 3):
        pl.semaphore_signal(barrier, inc=1, device_id=(dp, t ^ flip), device_id_type=MESH)
    pl.semaphore_wait(barrier, 10)


def head_mask(h, rows, width):
    lane = lax.broadcasted_iota(jnp.int32, (rows, width), 1)
    return (lane >= h * HD) & (lane < (h + 1) * HD)


def block_bias(seg_ref, par_ref, block, back):
    own = seg_ref[block * SEG]
    one = par_ref[own]
    two = par_ref[one]
    far = block - back
    near = seg_ref[jnp.maximum(far, 0) * SEG]
    ok = ((near == own) | (near == one) | (near == two)) & (far >= 0)
    return jnp.where(ok, jnp.float32(0.0), jnp.float32(NEG))


def first_kernel(
    seg_ref, par_ref, x_ref, cot_ref, wa_ref, wf_ref,
    n1_ref, n2_ref, mid_ref, f_ref, cot_all, wout_ref, q_ref, k_ref, v_ref, ct_ref, l_ref, gain_ref, wq_ref, wk_ref, wv_ref,
    a_ref, xe_ref, vt_ref, s_ref, e_ref, tri_ref, mids_ref, send, recv,
):
    dp, t = lax.axis_index("dp"), lax.axis_index("tensor")
    rows = x_ref.shape[0]
    token = 4 * rows
    blocks = token // SEG
    back = WINDOW // SEG
    lag = WINDOW - token
    per_tree = TREE // token
    place = lax.rem(dp, per_tree)
    links = Links(send, recv)
    own = lambda p: xe_ref.at[pl.ds(WINDOW + p * rows, rows)]
    halo = lambda p: xe_ref.at[pl.ds(lag + p * rows, rows)]
    x_spread = Spread(links, links.take(3), dp, t, own)
    halo_spread = Spread(links, links.take(3), dp, t, halo)
    cot_spread = Spread(links, links.take(3), dp, t, lambda p: cot_all.at[pl.ds(p * rows, rows)])
    wide = wout_ref.shape[0] // 4
    wout_spread = Spread(links, links.take(3), dp, t, lambda p: wout_ref.at[pl.ds(p * wide, wide)])
    a_gather = Gather(links, links.take(8), dp, t, lambda s: a_ref.at[s])
    f_gather = Gather(links, links.take(8), dp, t, lambda s: f_ref.at[s])
    h1 = links.take(1)
    h2 = links.take(1)
    halo_copy = lambda: links.copy(x_ref, halo(t), h1, h1, (lax.rem(dp + 1, 8), t))
    far_copy = lambda: links.copy(
        xe_ref.at[pl.ds(WINDOW + token - lag, lag)], xe_ref.at[pl.ds(0, lag)], h2, h2, (lax.rem(dp + 2, 8), t)
    )
    c_base = links.take(3 * blocks)

    def c_spread(i):
        at = pl.multiple_of(i * SEG, SEG)
        return Spread(
            links, c_base + 3 * i, dp, t, lambda p: ct_ref.at[pl.ds(p * wide, wide), pl.ds(at, SEG)]
        )

    greet(dp, t)
    a_ref[pl.ds(dp, 1)] = wa_ref[...][None]
    a_gather.start()
    xe_ref[pl.ds(WINDOW + t * rows, rows), :] = x_ref[...]
    x_spread.start()

    @pl.when(place < per_tree - 1)
    def _():
        halo_copy().start()

    @pl.when(place < 1)
    def _():
        xe_ref[pl.ds(lag, token), :] = jnp.zeros((token, xe_ref.shape[1]), BF)

    @pl.when(place < 2)
    def _():
        xe_ref[pl.ds(0, lag), :] = jnp.zeros((lag, xe_ref.shape[1]), BF)

    row = lax.broadcasted_iota(jnp.int32, (SEG, SEG), 0)
    col = lax.broadcasted_iota(jnp.int32, (SEG, SEG), 1)
    tri_ref[0] = jnp.where(row <= col, 0.0, NEG)
    tri_ref[1] = jnp.where(row > col, 0.0, NEG)
    cot_all[pl.ds(t * rows, rows), :] = cot_ref[...]
    f_ref[pl.ds(dp, 1)] = wf_ref[...][None]
    x_spread.forward()
    for step in (1, 3, 2):
        a_gather.forward(step)

    @pl.when(place >= 1)
    def _():
        halo_copy().wait_recv()
        halo_spread.start()

    x_spread.wait()

    @pl.when(place < per_tree - 2)
    def _():
        far_copy().start()

    f_gather.start()
    a_gather.wait()
    cols = wq_ref.shape[1]
    deep = wa_ref.shape[0] - 16
    weights = a_ref[:, 0:deep, :].reshape(8 * deep, 4 * wide)
    for j, ref in enumerate((wq_ref, wk_ref, wv_ref)):
        ref[...] = jnp.concatenate(
            [weights[:, j * wide : (j + 1) * wide], jnp.zeros((8 * deep, cols - wide), BF)], axis=1
        )
    wout_ref[pl.ds(t * wide, wide), :] = weights[:, 3 * wide : 4 * wide].T
    gains = jnp.sum(a_ref[:, deep : deep + 16, :].astype(F32), axis=0)
    gain_ref[...] = gains[0:8]

    def norm_rows(at):
        x = xe_ref[pl.ds(at, SEG), :].astype(F32)
        r = lax.rsqrt(jnp.mean(x * x, axis=-1, keepdims=True) + EPS)
        n = (x * r * gain_ref[0:1, :]).astype(BF)
        k_ref[pl.ds(at, SEG), :] = nn(n, wk_ref[...]).astype(BF)
        v = nn(n, wv_ref[...]).astype(BF)
        v_ref[pl.ds(at, SEG), :] = v
        vt_ref[:, pl.ds(at, SEG)] = v.T
        return n

    def own_rows(i, _):
        at = pl.multiple_of(i * SEG, SEG)
        n = norm_rows(WINDOW + at)
        n1_ref[pl.ds(at, SEG), :] = n
        q_ref[pl.ds(at, SEG), :] = (nn(n, wq_ref[...]).astype(BF).astype(F32) * HD**-0.5).astype(BF)
        return 0

    lax.fori_loop(0, blocks, own_rows, 0)

    @pl.when(place >= 1)
    def _():
        halo_spread.forward()
        halo_spread.wait()

    wout_spread.start()
    cot_spread.start()

    @pl.when(place >= 2)
    def _():
        far_copy().wait_recv()

    def halo_rows(i, _):
        norm_rows(pl.multiple_of(i * SEG, SEG))
        return 0

    lax.fori_loop(0, back, halo_rows, 0)

    def attend(i, _):
        at = pl.multiple_of(i * SEG, SEG)
        block = dp * blocks + i
        biases = [block_bias(seg_ref, par_ref, block, back - j) for j in range(back + 1)]
        q = q_ref[pl.ds(at, SEG), :]
        for h in range(3):
            qm = jnp.where(head_mask(h, SEG, cols), q, jnp.zeros_like(q))
            top = None
            for j in range(back + 1):
                s = nt(k_ref[pl.ds(at + j * SEG, SEG), :], qm)
                if j == 0:
                    s = s + tri_ref[1]
                if j == back:
                    s = s + tri_ref[0]
                s_ref[h, j * SEG : (j + 1) * SEG, :] = s
                best = jnp.max(s, axis=0, keepdims=True) + biases[j]
                top = best if top is None else jnp.maximum(top, best)
            top = top * LOG2E
            total = None
            for j in range(back + 1):
                e = jnp.exp2(s_ref[h, j * SEG : (j + 1) * SEG, :] * LOG2E - (top - biases[j]))
                part = jnp.sum(e, axis=0, keepdims=True)
                total = part if total is None else total + part
                e_ref[h, j * SEG : (j + 1) * SEG, :] = e.astype(BF)
            o = nn(vt_ref[h * HD : (h + 1) * HD, pl.ds(at, (back + 1) * SEG)], e_ref[h])
            ct_ref[pl.ds(t * wide + h * HD, HD), pl.ds(at, SEG)] = (o / total).astype(BF)
            l_ref[h : h + 1, pl.ds(at, SEG)] = top + jnp.log(total) * LOG2E
        c_spread(i).start()

        @pl.when(i > 0)
        def _():
            c_spread(i - 1).forward()

        @pl.when(i == 1)
        def _():
            for step in (1, 3, 2):
                f_gather.forward(step)

        return 0

    lax.fori_loop(0, blocks, attend, 0)
    c_spread(blocks - 1).forward()
    wout_spread.forward()
    wout_spread.wait()

    def middle(i, _):
        at = pl.multiple_of(i * SEG, SEG)
        c_spread(i).wait()
        m = xe_ref[pl.ds(WINDOW + at, SEG), :].astype(F32) + tn(ct_ref[:, pl.ds(at, SEG)], wout_ref[...])
        mids_ref[pl.ds(at, SEG), :] = m
        r = lax.rsqrt(jnp.mean(m * m, axis=-1, keepdims=True) + EPS)
        n2_ref[pl.ds(at, SEG), :] = (m * r * gain_ref[1:2, :]).astype(BF)
        return 0

    lax.fori_loop(0, blocks, middle, 0)
    mid_ref[...] = mids_ref[pl.ds(t * rows, rows), :]
    cot_spread.forward()
    cot_spread.wait()
    f_gather.wait()
    for item in (x_spread, cot_spread, wout_spread, a_gather, f_gather):
        item.finish()
    for i in range(blocks):
        c_spread(i).finish()

    @pl.when(place >= 1)
    def _():
        halo_spread.finish()

    @pl.when(place < per_tree - 1)
    def _():
        halo_copy().wait_send()

    @pl.when(place < per_tree - 2)
    def _():
        far_copy().wait_send()


def first_phase(x, cot, segments, parents, wa, wf):
    rows, width = x.shape
    token = 4 * rows
    ext = token + WINDOW
    wide = width // 4
    cols = 256 * pl.cdiv(wide, 256)
    blocks = token // SEG
    keys = WINDOW + SEG
    vmem = pl.BlockSpec(memory_space=pltpu.VMEM)
    smem = pl.BlockSpec(memory_space=pltpu.SMEM)
    copies = 3 * 4 + 2 * 8 + 2 + 3 * blocks
    shape = jax.ShapeDtypeStruct
    return pl.pallas_call(
        first_kernel,
        out_shape=[
            shape((token, width), BF),
            shape((token, width), BF),
            shape((rows, width), F32),
            shape((8,) + wf.shape, BF),
            shape((token, width), BF),
            shape((width, width), BF),
            shape((token, cols), BF),
            shape((ext, cols), BF),
            shape((ext, cols), BF),
            shape((width, token), BF),
            shape((8, token), F32),
            shape((8, width), F32),
            shape((width, cols), BF),
            shape((width, cols), BF),
            shape((width, cols), BF),
        ],
        in_specs=[smem, smem, vmem, vmem, vmem, vmem],
        out_specs=[vmem] * 15,
        scratch_shapes=[
            pltpu.VMEM((8,) + wa.shape, BF),
            pltpu.VMEM((ext, width), BF),
            pltpu.VMEM((cols, ext), BF),
            pltpu.VMEM((3, keys, SEG), F32),
            pltpu.VMEM((3, keys, SEG), BF),
            pltpu.VMEM((2, SEG, SEG), F32),
            pltpu.VMEM((token, width), F32),
            pltpu.SemaphoreType.DMA((copies,)),
            pltpu.SemaphoreType.DMA((copies,)),
        ],
        compiler_params=pltpu.CompilerParams(
            collective_id=0, has_side_effects=True, vmem_limit_bytes=60 << 20
        ),
    )(segments, parents, x, cot, wa, wf)


class Fold:
    def __init__(self, links, base, dp, t, buf):
        self.links, self.base, self.dp, self.t, self.buf = links, base, dp, t, buf

    def copy(self, i):
        flip = (1, 2, 1)[i]
        return self.links.copy(
            self.buf.at[i], self.buf.at[3 + i], self.base + i, self.base + i, (self.dp, self.t ^ flip)
        )

    def put(self, i, value):
        if i == 1:
            self.copy(0).wait_recv()
            value = value + self.buf[3].astype(F32)
        self.buf[i] = value.astype(BF)

    def total(self, value):
        self.copy(1).wait_recv()
        self.copy(2).wait_recv()
        return value + self.buf[5].astype(F32) + self.buf[4].astype(F32)

    def finish(self):
        for i in range(3):
            self.copy(i).wait_send()


class Settle:
    def __init__(self, links, base, dp, t, slots, deep, from_y, from_z):
        self.links, self.base, self.dp, self.t = links, base, dp, t
        self.slots, self.deep, self.from_y, self.from_z = slots, deep, from_y, from_z
        self.z, self.y = dp // 2, lax.rem(dp, 2)

    def rows(self, z, y):
        return pl.ds(pl.multiple_of((z * 2 + y) * self.deep, self.deep), self.deep)

    def across(self, step):
        z = lax.rem(self.z + step, 4)
        return self.links.copy(
            self.slots.at[self.rows(z, 1 - self.y)],
            self.from_y.at[step],
            self.base + step,
            self.base + step,
            (self.dp ^ 1, self.t),
        )

    def along(self, step):
        z = lax.rem(self.z + step, 4)
        return self.links.copy(
            self.slots.at[self.rows(z, self.y)],
            self.from_z.at[step - 1],
            self.base + 3 + step,
            self.base + 3 + step,
            (z * 2 + self.y, self.t),
        )

    def start(self):
        for step in (2, 1, 3, 0):
            self.across(step).start()

    def pass_on(self, step):
        self.across(step).wait_recv()
        z = lax.rem(self.z + step, 4)
        at = self.rows(z, self.y)
        self.slots[at, :] = (self.slots[at, :].astype(F32) + self.from_y[step].astype(F32)).astype(BF)
        self.along(step).start()

    def total(self):
        self.across(0).wait_recv()
        value = self.slots[self.rows(self.z, self.y), :].astype(F32) + self.from_y[0].astype(F32)
        for step in (1, 2, 3):
            self.along(step).wait_recv()
            value = value + self.from_z[step - 1].astype(F32)
        return value

    def finish(self):
        for step in range(4):
            self.across(step).wait_send()
        for step in (1, 2, 3):
            self.along(step).wait_send()


def second_kernel(
    seg_ref, par_ref, x_ref, cot_ref, wa_ref, wf_ref,
    n1_ref, n2_ref, mid_ref, f_ref, cot_all, wout_ref, q_ref, k_ref, v_ref, ct_ref, l_ref, gain_ref, wq_ref, wk_ref, wv_ref,
    out_ref, ing_ref, gqkv_ref, gout_ref, gup_ref, gdown_ref, gs_ref,
    a_ref, gu_ref, down_own, gn_own, down_buf, gn_buf, gn1_buf, gmb_ref, gmid_ref,
    gf_ref, gfy_ref, gfz_ref, ga_ref, gay_ref, gaz_ref, wo_ref, kt_ref, dqt_ref, halo_ref, back_ref, own_ref, acc_ref,
    gq_ref, gk_ref, gv_ref, tri_ref, delta_ref, gain_buf, send, recv,
):
    dp, t = lax.axis_index("dp"), lax.axis_index("tensor")
    rows, width = x_ref.shape
    token = 4 * rows
    blocks = token // SEG
    back = WINDOW // SEG
    lag = WINDOW - token
    per_tree = TREE // token
    place = lax.rem(dp, per_tree)
    wide = width // 4
    cols = q_ref.shape[1]
    deep = wf_ref.shape[0]
    hidden = wf_ref.shape[1] // 2
    links = Links(send, recv)
    down_fold = Fold(links, links.take(3), dp, t, down_buf)
    gn_fold = Fold(links, links.take(3), dp, t, gn_buf)
    gn1_fold = Fold(links, links.take(3), dp, t, gn1_buf)
    gmb_spread = Spread(links, links.take(3), dp, t, lambda p: gmb_ref.at[pl.ds(p * rows, rows)])
    f_settle = Settle(links, links.take(7), dp, t, gf_ref, deep, gfy_ref, gfz_ref)
    a_settle = Settle(links, links.take(7), dp, t, ga_ref, deep, gay_ref, gaz_ref)
    hb = links.take(5)

    def back_copy(i):
        at = pl.ds(lag + (t ^ (3 - i)) * rows, rows)
        return links.copy(halo_ref.at[at], back_ref.at[at], hb + i, hb + i, (lax.rem(dp + 7, 8), t))

    def far_copy():
        at = pl.ds(0, lag)
        return links.copy(halo_ref.at[at], back_ref.at[at], hb + 4, hb + 4, (lax.rem(dp + 6, 8), t))

    gb = links.take(3)

    def gain_copy(i):
        return links.copy(gain_buf.at[0], gain_buf.at[i + 1], gb + i, gb + i, (dp, t ^ (i + 1)))

    greet(dp, t)
    up = f_ref[:, :, 0:hidden].reshape(width, hidden)
    down_t = f_ref[:, :, hidden : 2 * hidden].reshape(width, hidden)

    def feed(k, _):
        at = (t ^ (3 - k)) * rows
        u = nn(n2_ref[pl.ds(at, rows), :], up)
        cdf = 0.5 * (1.0 + lax.erf(u * 0.7071067811865476))
        act = (u * cdf).astype(BF)
        a_ref[pl.ds(at, rows), :] = act
        slope = cdf + u * jnp.exp2(u * u * (-0.5 * LOG2E)) * 0.3989422804014327
        gu = (nn(cot_all[pl.ds(at, rows), :], down_t) * slope).astype(BF)
        gu_ref[pl.ds(at, rows), :] = gu
        gn_own[...] = nt(gu, up)
        down_own[...] = nt(act, down_t)
        for i in range(3):

            @pl.when(k == i)
            def _():
                gn_fold.put(i, gn_own[...])
                gn_fold.copy(i).start()
                down_fold.put(i, down_own[...])
                if i != 1:
                    down_fold.copy(i).start()

        return 0

    lax.fori_loop(0, 4, feed, 0)

    def ffn_grads(j, _):
        at = pl.multiple_of(j * 256, 256)
        gf_ref[pl.ds(at, 256), 0:hidden] = tn(n2_ref[:, pl.ds(at, 256)], gu_ref[...]).astype(BF)
        gf_ref[pl.ds(at, 256), hidden : 2 * hidden] = tn(cot_all[:, pl.ds(at, 256)], a_ref[...]).astype(BF)
        return 0

    lax.fori_loop(0, width // 256, ffn_grads, 0)
    f_settle.start()

    gn2 = gn_fold.total(gn_own[...])
    mid = mid_ref[...]
    r2 = lax.rsqrt(jnp.mean(mid * mid, axis=-1, keepdims=True) + EPS)
    hat2 = mid * r2
    scaled = gn2 * gain_ref[1:2, :]
    inner = jnp.mean(scaled * hat2, axis=-1, keepdims=True)
    gmid = cot_ref[...].astype(F32) + r2 * (scaled - hat2 * inner)
    gmid_ref[...] = gmid
    gmb_ref[pl.ds(t * rows, rows), :] = gmid.astype(BF)
    gmb_spread.start()

    row = lax.broadcasted_iota(jnp.int32, (SEG, SEG), 0)
    col = lax.broadcasted_iota(jnp.int32, (SEG, SEG), 1)
    tri_ref[0] = jnp.where(row <= col, 0.0, NEG)
    tri_ref[1] = jnp.where(row > col, 0.0, NEG)
    tri_ref[2] = jnp.zeros((SEG, SEG), F32)
    wo_ref[0:wide, :] = wout_ref[pl.ds(t * wide, wide), :]
    wo_ref[wide:cols, :] = jnp.zeros((cols - wide, width), BF)

    def turn_keys(i, _):
        at = pl.multiple_of(i * SEG, SEG)
        kt_ref[:, pl.ds(at, SEG)] = k_ref[pl.ds(at, SEG), :].T
        return 0

    lax.fori_loop(0, blocks + back, turn_keys, 0)
    dqt_ref[...] = jnp.zeros_like(dqt_ref)

    def mask_queries(i, _):
        at = pl.multiple_of(i * SEG, SEG)
        q = q_ref[pl.ds(at, SEG), :]
        for h in range(3):
            a_ref[pl.ds(at, SEG), h * cols : (h + 1) * cols] = jnp.where(head_mask(h, SEG, cols), q, jnp.zeros_like(q))
        return 0

    lax.fori_loop(0, blocks, mask_queries, 0)
    gmb_spread.forward()
    for step in (2, 1, 3):
        f_settle.pass_on(step)
    gmb_spread.wait()
    down_fold.copy(1).start()

    def context_grads(i, _):
        at = pl.multiple_of(i * SEG, SEG)
        gc = nt(gmb_ref[pl.ds(at, SEG), :], wo_ref[...])
        low = gc.astype(BF)
        gct = low.astype(F32).T
        for h in range(3):
            gu_ref[pl.ds(at, SEG), h * cols : (h + 1) * cols] = jnp.where(
                head_mask(h, SEG, cols), low, jnp.zeros_like(low)
            )
            c = ct_ref[pl.ds(t * wide + h * HD, HD), pl.ds(at, SEG)].astype(F32)
            delta_ref[h : h + 1, pl.ds(at, SEG)] = jnp.sum(gct[h * HD : (h + 1) * HD] * c, axis=0, keepdims=True)
        return 0

    lax.fori_loop(0, blocks, context_grads, 0)
    qm_ref, gm_ref = a_ref, gu_ref

    def key_block(kb, _):
        kat = pl.multiple_of(kb * SEG, SEG)
        acc_ref[...] = jnp.zeros_like(acc_ref)

        def pair(qb, _):
            qat = pl.multiple_of(qb * SEG, SEG)
            bias = block_bias(seg_ref, par_ref, dp * blocks + qb, back + qb - kb)
            tri = tri_ref[jnp.where(kb == qb, 1, jnp.where(kb == qb + back, 0, 2))]
            keys = k_ref[pl.ds(kat, SEG), :]
            values = v_ref[pl.ds(kat, SEG), :]
            dk = dv = None
            for h in range(3):
                qm = qm_ref[pl.ds(qat, SEG), h * cols : (h + 1) * cols]
                gm = gm_ref[pl.ds(qat, SEG), h * cols : (h + 1) * cols]
                p = jnp.exp2(nt(keys, qm) * LOG2E + tri - (l_ref[h : h + 1, pl.ds(qat, SEG)] - bias))
                ds = (p * (nt(values, gm) - delta_ref[h : h + 1, pl.ds(qat, SEG)])).astype(BF)
                dv_h = nn(p.astype(BF), gm)
                dk_h = nn(ds, qm)
                dv = dv_h if dv is None else dv + dv_h
                dk = dk_h if dk is None else dk + dk_h
                dqt_ref[h * HD : (h + 1) * HD, pl.ds(qat, SEG)] += nn(
                    kt_ref[h * HD : (h + 1) * HD, pl.ds(kat, SEG)], ds
                )
            acc_ref[0] += dk
            acc_ref[1] += dv
            return 0

        lax.fori_loop(jnp.maximum(kb - back, 0), jnp.minimum(kb + 1, blocks), pair, 0)
        both = jnp.concatenate([acc_ref[0, :, 0:wide], acc_ref[1, :, 0:wide]], axis=1)

        @pl.when(kb < back)
        def _():
            halo_ref[pl.ds(kat, SEG), :] = both.astype(BF)

        @pl.when(kb >= back)
        def _():
            own_ref[pl.ds(kat - WINDOW, SEG), :] = both

        @pl.when((kb == back - 1) & (place >= 1))
        def _():
            for i in range(4):
                back_copy(i).start()

        @pl.when((kb == back - 1) & (place >= 2))
        def _():
            far_copy().start()

        return 0

    lax.fori_loop(0, blocks + back, key_block, 0)

    def turn_queries(i, _):
        at = pl.multiple_of(i * SEG, SEG)
        gq_ref[pl.ds(at, SEG), :] = (dqt_ref[:, pl.ds(at, SEG)] * HD**-0.5).astype(BF).T
        return 0

    lax.fori_loop(0, blocks, turn_queries, 0)
    gout = nn(ct_ref[pl.ds(t * wide, wide), :], gmb_ref[...]).astype(BF).T
    out_ref[...] = (mid_ref[...] + down_fold.total(down_own[...])).astype(BF)

    @pl.when(place < per_tree - 2)
    def _():
        far_copy().wait_recv()
        at = token - lag
        own_ref[at:token, :] = own_ref[at:token, :] + back_ref[0:lag, :].astype(F32)

    def outer(k, _):
        at = (t ^ (3 - k)) * rows

        @pl.when(place < per_tree - 1)
        def _():
            for i in range(4):

                @pl.when(k == i)
                def _():
                    back_copy(i).wait_recv()

            own_ref[pl.ds(at, rows), :] = own_ref[pl.ds(at, rows), :] + back_ref[pl.ds(lag + at, rows), :].astype(F32)

        both = own_ref[pl.ds(at, rows), :].astype(BF)
        gk_ref[pl.ds(at, rows), :] = both[:, 0:wide]
        gv_ref[pl.ds(at, rows), :] = both[:, wide : 2 * wide]
        gn_own[...] = (
            nt(gq_ref[pl.ds(at, rows), :], wq_ref[:, 0:wide])
            + nt(gk_ref[pl.ds(at, rows), :], wk_ref[:, 0:wide])
            + nt(gv_ref[pl.ds(at, rows), :], wv_ref[:, 0:wide])
        )
        for i in range(3):

            @pl.when(k == i)
            def _():
                gn1_fold.put(i, gn_own[...])
                gn1_fold.copy(i).start()

        return 0

    lax.fori_loop(0, 4, outer, 0)

    ga_ref[:, 3 * wide : 4 * wide] = gout
    for j, ref in enumerate((gq_ref, gk_ref, gv_ref)):
        ga_ref[:, j * wide : (j + 1) * wide] = tn(n1_ref[...], ref[...]).astype(BF)
    a_settle.start()
    gf = f_settle.total()
    gup_ref[...] = gf[:, 0:hidden]
    gdown_ref[...] = gf[:, hidden : 2 * hidden].T
    for step in (2, 1, 3):
        a_settle.pass_on(step)

    gn1 = gn1_fold.total(gn_own[...])
    x = x_ref[...].astype(F32)
    r1 = lax.rsqrt(jnp.mean(x * x, axis=-1, keepdims=True) + EPS)
    hat1 = x * r1
    scaled = gn1 * gain_ref[0:1, :]
    inner = jnp.mean(scaled * hat1, axis=-1, keepdims=True)
    ing_ref[...] = (gmid_ref[...] + r1 * (scaled - hat1 * inner)).astype(BF)

    ga = a_settle.total()
    gqkv_ref[...] = ga[:, 0 : 3 * wide]
    gout_ref[...] = ga[:, 3 * wide : 4 * wide].T
    one = jnp.sum(ga[:, 0 : 3 * wide] * wa_ref[0:deep, 0 : 3 * wide].astype(F32), axis=1, keepdims=True)
    two = jnp.sum(gup_ref[...] * wf_ref[:, 0:hidden].astype(F32), axis=1, keepdims=True)
    lane = lax.broadcasted_iota(jnp.int32, (deep, 128), 1)
    gain_buf[0] = jnp.where(lane < 64, one, two)
    for i in range(3):
        gain_copy(i).start()
    total = gain_buf[0]
    for i in range(3):
        gain_copy(i).wait_recv()
        total = total + gain_buf[i + 1]
    gs_ref[...] = total
    for i in range(3):
        gain_copy(i).wait_send()
    for item in (down_fold, gn_fold, gn1_fold, gmb_spread, f_settle, a_settle):
        item.finish()

    @pl.when(place >= 1)
    def _():
        for i in range(4):
            back_copy(i).wait_send()

    @pl.when(place >= 2)
    def _():
        far_copy().wait_send()


def second_phase(x, cot, segments, parents, wa, wf, firsts):
    rows, width = x.shape
    token = 4 * rows
    ext = token + WINDOW
    wide = width // 4
    cols = 256 * pl.cdiv(wide, 256)
    deep, hidden = wf.shape[0], wf.shape[1] // 2
    vmem = pl.BlockSpec(memory_space=pltpu.VMEM)
    smem = pl.BlockSpec(memory_space=pltpu.SMEM)
    copies = 4 * 3 + 2 * 7 + 5 + 3
    shape = jax.ShapeDtypeStruct
    return pl.pallas_call(
        second_kernel,
        out_shape=[
            shape((rows, width), BF),
            shape((rows, width), BF),
            shape((deep, 3 * wide), F32),
            shape((wide, deep), F32),
            shape((deep, hidden), F32),
            shape((hidden, deep), F32),
            shape((deep, 128), F32),
        ],
        in_specs=[smem, smem] + [vmem] * 19,
        out_specs=[vmem] * 7,
        scratch_shapes=[
            pltpu.VMEM((token, hidden), BF),
            pltpu.VMEM((token, hidden), BF),
            pltpu.VMEM((rows, width), F32),
            pltpu.VMEM((rows, width), F32),
            pltpu.VMEM((6, rows, width), BF),
            pltpu.VMEM((6, rows, width), BF),
            pltpu.VMEM((6, rows, width), BF),
            pltpu.VMEM((token, width), BF),
            pltpu.VMEM((rows, width), F32),
            pltpu.VMEM((width, 2 * hidden), BF),
            pltpu.VMEM((4, deep, 2 * hidden), BF),
            pltpu.VMEM((3, deep, 2 * hidden), BF),
            pltpu.VMEM((width, width), BF),
            pltpu.VMEM((4, deep, width), BF),
            pltpu.VMEM((3, deep, width), BF),
            pltpu.VMEM((cols, width), BF),
            pltpu.VMEM((cols, ext), BF),
            pltpu.VMEM((wide, token), F32),
            pltpu.VMEM((WINDOW, 2 * wide), BF),
            pltpu.VMEM((WINDOW, 2 * wide), BF),
            pltpu.VMEM((token, 2 * wide), F32),
            pltpu.VMEM((2, SEG, cols), F32),
            pltpu.VMEM((token, wide), BF),
            pltpu.VMEM((token, wide), BF),
            pltpu.VMEM((token, wide), BF),
            pltpu.VMEM((3, SEG, SEG), F32),
            pltpu.VMEM((8, token), F32),
            pltpu.VMEM((4, deep, 128), F32),
            pltpu.SemaphoreType.DMA((copies,)),
            pltpu.SemaphoreType.DMA((copies,)),
        ],
        compiler_params=pltpu.CompilerParams(
            collective_id=1, has_side_effects=True, vmem_limit_bytes=63 << 20
        ),
    )(segments, parents, x, cot, wa, wf, *firsts)


def fast_shards(
    layer_input, cotangent, segments, parents, norm1_gain, w_query, w_key, w_value, w_out, norm2_gain, w_up, w_down,
):
    dp = lax.axis_index("dp")
    width = layer_input.shape[1]
    wide = width // 4
    gains = jnp.zeros((16, width), BF)
    gains = lax.dynamic_update_slice(gains, norm1_gain[None], (0, dp * norm1_gain.shape[0]))
    gains = lax.dynamic_update_slice(gains, norm2_gain[None], (1, dp * norm1_gain.shape[0]))
    wa = jnp.concatenate([jnp.concatenate([w_query, w_key, w_value, w_out.T], axis=1), gains], axis=0)
    wf = jnp.concatenate([w_up, w_down.T], axis=1)
    firsts = first_phase(layer_input, cotangent, segments, parents, wa, wf)
    out, ing, gqkv, gout, gup, gdown, gs = second_phase(layer_input, cotangent, segments, parents, wa, wf, firsts)
    return (
        out,
        ing,
        gs[:, 0] / norm1_gain.astype(F32),
        gqkv[:, 0:wide],
        gqkv[:, wide : 2 * wide],
        gqkv[:, 2 * wide :],
        gout,
        gs[:, 64] / norm2_gain.astype(F32),
        gup,
        gdown,
    )


epsilon = 1e-06
masked_score = -1e30


def from_behind(block, axis, distance):
    devices = range(lax.axis_size(axis))
    route = [(i - distance, i) for i in devices if i - distance in devices]
    return lax.ppermute(block, axis, route)


def split_up(x, dim, peers):
    dims = x.shape
    tiles = x.reshape(*dims[:dim], peers, dims[dim] // peers, *dims[dim + 1 :])
    return jnp.moveaxis(tiles, dim, 0)


def sum_at_owner(x, axis, dim):
    tiles = split_up(x, dim, lax.axis_size(axis))
    arrived = lax.all_to_all(tiles, axis, split_axis=0, concat_axis=0, tiled=True)
    return arrived.astype(jnp.float32).sum(axis=0)


def side_by_side(arrays, axis, dim, along):
    widths = [math.prod(a.shape[along:]) for a in arrays]
    both = jnp.concatenate(
        [a.reshape(*a.shape[:along], w) for a, w in zip(arrays, widths)], axis=along
    )
    whole = sum_at_owner(both, axis, dim)
    tiles = jnp.split(whole, [sum(widths[:k]) for k in range(1, len(widths))], axis=along)
    return tuple((b.reshape(*whole.shape[:along], *a.shape[along:]) for a, b in zip(arrays, tiles)))


def gelu_exact(values):
    return jax.nn.gelu(values, approximate=False)


def row_scale(values):
    return lax.rsqrt(jnp.mean(values * values, axis=-1, keepdims=True) + epsilon)


def norm_backward(incoming, normal_hat, row_factor, gain):
    scaled = incoming * gain
    inner = jnp.mean(scaled * normal_hat, axis=-1, keepdims=True)
    return (row_factor * (scaled - normal_hat * inner), jnp.sum(incoming * normal_hat, axis=0))


def parent_of(seg_ids, parents):
    seg_table = jnp.arange(parents.shape[0], dtype=jnp.int32)
    hits = seg_ids[:, None] == seg_table[None, :]
    return jnp.sum(jnp.where(hits, parents[None, :], 0), axis=1)


def shards(
    layer_input,
    cotangent,
    segments,
    parents,
    norm1_gain,
    w_query,
    w_key,
    w_value,
    w_out,
    norm2_gain,
    w_up,
    w_down,
):
    gain_one, full_query, full_key, full_value, full_out, gain_two, full_up, full_down = (
        lax.all_gather(norm1_gain, "dp", axis=0, tiled=True),
        lax.all_gather(w_query, "dp", axis=0, tiled=True),
        lax.all_gather(w_key, "dp", axis=0, tiled=True),
        lax.all_gather(w_value, "dp", axis=0, tiled=True),
        lax.all_gather(w_out, "dp", axis=1, tiled=True),
        lax.all_gather(norm2_gain, "dp", axis=0, tiled=True),
        lax.all_gather(w_up, "dp", axis=0, tiled=True),
        lax.all_gather(w_down, "dp", axis=1, tiled=True),
    )
    gain_one = gain_one.astype(jnp.float32)
    gain_two = gain_two.astype(jnp.float32)
    row_count = layer_input.shape[0]
    token_count = row_count * lax.axis_size("tensor")
    position = lax.axis_index("dp") * token_count
    head_width = full_query.shape[1]
    head_count = head_width // HD
    scaling = HD ** (-0.5)
    block_rows = min(640, token_count)
    block_count = token_count // block_rows
    span = WINDOW + block_rows
    hop_count = (WINDOW + token_count - 1) // token_count
    inputs = layer_input.astype(jnp.float32)
    factor_one = row_scale(inputs)
    hat_one = inputs * factor_one
    normed = (hat_one * gain_one).astype(jnp.bfloat16)
    normed_all = lax.all_gather(normed, "tensor", axis=0, tiled=True)
    queries = jnp.dot(normed_all, full_query, preferred_element_type=jnp.float32).astype(
        jnp.bfloat16
    )
    keys_own = jnp.dot(normed_all, full_key, preferred_element_type=jnp.float32).astype(
        jnp.bfloat16
    )
    values_own = jnp.dot(normed_all, full_value, preferred_element_type=jnp.float32).astype(
        jnp.bfloat16
    )
    pair_own = jnp.concatenate([keys_own, values_own], axis=1)
    halo_parts = []
    for distance in range(1, hop_count + 1):
        length = min(token_count, WINDOW - (distance - 1) * token_count)
        piece = pair_own[token_count - length :]
        moved = from_behind(piece, "dp", distance)
        halo_parts.append(moved)
    pair_all = jnp.concatenate(halo_parts[::-1] + [pair_own], axis=0)
    seg_padded = jnp.concatenate([jnp.full((WINDOW,), -1, jnp.int32), segments])
    seg_keys = lax.dynamic_slice_in_dim(seg_padded, position, WINDOW + token_count, 0)
    seg_query = seg_keys[WINDOW:]
    parent_one = parent_of(seg_query, parents)
    parent_two = parent_of(parent_one, parents)
    query_spots = jnp.arange(block_rows, dtype=jnp.int32)
    key_spots = jnp.arange(span, dtype=jnp.int32)

    def scores_of(offset):
        query_block = lax.dynamic_slice_in_dim(queries, offset, block_rows, 0).reshape(
            block_rows, head_count, HD
        )
        pair_block = lax.dynamic_slice_in_dim(pair_all, offset, span, 0)
        key_block = pair_block[:, :head_width].reshape(span, head_count, HD)
        value_block = pair_block[:, head_width:].reshape(span, head_count, HD)
        own_seg = lax.dynamic_slice_in_dim(seg_query, offset, block_rows, 0)
        up_one = lax.dynamic_slice_in_dim(parent_one, offset, block_rows, 0)
        up_two = lax.dynamic_slice_in_dim(parent_two, offset, block_rows, 0)
        near_seg = lax.dynamic_slice_in_dim(seg_keys, offset, span, 0)
        gap = WINDOW + query_spots[:, None] - key_spots[None, :]
        same_path = (
            (near_seg[None, :] == own_seg[:, None])
            | (near_seg[None, :] == up_one[:, None])
            | (near_seg[None, :] == up_two[:, None])
        )
        allowed = (gap >= 0) & (gap < WINDOW) & same_path
        raw = (
            jnp.einsum("qhd,khd->hqk", query_block, key_block, preferred_element_type=jnp.float32)
            * scaling
        )
        return (jnp.where(allowed[None], raw, masked_score), query_block, key_block, value_block)

    def forward_block(block_index):
        scores, query_block, key_block, value_block = scores_of(block_index * block_rows)
        row_max = jnp.max(scores, axis=-1, keepdims=True)
        exponent = jnp.exp(scores - row_max)
        denominator = jnp.sum(exponent, axis=-1, keepdims=True)
        weights = (exponent / denominator).astype(jnp.bfloat16)
        mixed = jnp.einsum("hqk,khd->qhd", weights, value_block, preferred_element_type=jnp.float32)
        return (
            mixed.reshape(block_rows, head_width).astype(jnp.bfloat16),
            (row_max + jnp.log(denominator))[..., 0],
        )

    context_blocks, logsum_blocks = lax.map(forward_block, jnp.arange(block_count, dtype=jnp.int32))
    context = context_blocks.reshape(token_count, head_width)
    middle = inputs + lax.psum_scatter(
        jnp.dot(context, full_out, preferred_element_type=jnp.float32).astype(jnp.bfloat16),
        "tensor",
        scatter_dimension=0,
        tiled=True,
    ).astype(jnp.float32)
    factor_two = row_scale(middle)
    hat_two = middle * factor_two
    normed_two = (hat_two * gain_two).astype(jnp.bfloat16)
    normed_two_all = lax.all_gather(normed_two, "tensor", axis=0, tiled=True)
    upper = jnp.dot(normed_two_all, full_up, preferred_element_type=jnp.float32)
    active = gelu_exact(upper).astype(jnp.bfloat16)
    result = middle + lax.psum_scatter(
        jnp.dot(active, full_down, preferred_element_type=jnp.float32).astype(jnp.bfloat16),
        "tensor",
        scatter_dimension=0,
        tiled=True,
    ).astype(jnp.float32)
    incoming = cotangent.astype(jnp.float32)
    incoming_all = lax.all_gather(cotangent, "tensor", axis=0, tiled=True)
    grad_down = jnp.einsum("tf,td->fd", active, incoming_all, preferred_element_type=jnp.float32)
    grad_active = jnp.einsum(
        "td,fd->tf", incoming_all, full_down, preferred_element_type=jnp.float32
    )
    unused_value, gelu_pull = jax.vjp(gelu_exact, upper)
    grad_upper = gelu_pull(grad_active)[0].astype(jnp.bfloat16)
    grad_up = jnp.einsum(
        "tc,tf->cf", normed_two_all, grad_upper, preferred_element_type=jnp.float32
    )
    grad_normed_two = lax.psum_scatter(
        jnp.einsum("tf,cf->tc", grad_upper, full_up, preferred_element_type=jnp.float32).astype(
            jnp.bfloat16
        ),
        "tensor",
        scatter_dimension=0,
        tiled=True,
    ).astype(jnp.float32)
    through_two, gain_two_part = norm_backward(grad_normed_two, hat_two, factor_two, gain_two)
    grad_middle = incoming + through_two
    grad_middle_all = lax.all_gather(grad_middle.astype(jnp.bfloat16), "tensor", axis=0, tiled=True)
    grad_out = jnp.einsum("tc,td->cd", context, grad_middle_all, preferred_element_type=jnp.float32)
    grad_context = jnp.einsum(
        "td,cd->tc", grad_middle_all, full_out, preferred_element_type=jnp.float32
    ).astype(jnp.bfloat16)

    def backward_block(block_index, carry):
        grad_queries, grad_pairs = carry
        offset = block_index * block_rows
        scores, query_block, key_block, value_block = scores_of(offset)
        logsum = lax.dynamic_index_in_dim(logsum_blocks, block_index, 0, keepdims=False)
        probs = jnp.exp(scores - logsum[..., None])
        grad_rows = lax.dynamic_slice_in_dim(grad_context, offset, block_rows, 0).reshape(
            block_rows, head_count, HD
        )
        grad_probs = jnp.einsum(
            "qhd,khd->hqk", grad_rows, value_block, preferred_element_type=jnp.float32
        )
        inner = jnp.sum(probs * grad_probs, axis=-1, keepdims=True)
        grad_scores = (probs * (grad_probs - inner)).astype(jnp.bfloat16)
        grad_query_block = (
            jnp.einsum("hqk,khd->qhd", grad_scores, key_block, preferred_element_type=jnp.float32)
            * scaling
        )
        grad_key_block = (
            jnp.einsum("hqk,qhd->khd", grad_scores, query_block, preferred_element_type=jnp.float32)
            * scaling
        )
        grad_value_block = jnp.einsum(
            "hqk,qhd->khd",
            probs.astype(jnp.bfloat16),
            grad_rows,
            preferred_element_type=jnp.float32,
        )
        grad_queries = lax.dynamic_update_slice_in_dim(
            grad_queries, grad_query_block.reshape(block_rows, head_width), offset, 0
        )
        update = jnp.concatenate(
            [grad_key_block.reshape(span, head_width), grad_value_block.reshape(span, head_width)],
            axis=1,
        )
        current = lax.dynamic_slice_in_dim(grad_pairs, offset, span, 0)
        grad_pairs = lax.dynamic_update_slice_in_dim(grad_pairs, current + update, offset, 0)
        return (grad_queries, grad_pairs)

    start_carry = (
        jnp.zeros((token_count, head_width), jnp.float32),
        jnp.zeros((WINDOW + token_count, 2 * head_width), jnp.float32),
    )
    grad_queries, grad_pairs = lax.fori_loop(0, block_count, backward_block, start_carry)
    grad_own = grad_pairs[WINDOW:]
    for distance in range(1, hop_count + 1):
        length = min(token_count, WINDOW - (distance - 1) * token_count)
        first_row = WINDOW - (distance - 1) * token_count - length
        piece = grad_pairs[first_row : first_row + length]
        returned = from_behind(piece.astype(jnp.bfloat16), "dp", -distance).astype(piece.dtype)
        grad_own = grad_own + jnp.pad(returned, ((token_count - length, 0), (0, 0)))
    grad_keys = grad_own[:, :head_width].astype(jnp.bfloat16)
    grad_values = grad_own[:, head_width:].astype(jnp.bfloat16)
    grad_queries_low = grad_queries.astype(jnp.bfloat16)
    grad_query = jnp.einsum(
        "tc,tq->cq", normed_all, grad_queries_low, preferred_element_type=jnp.float32
    )
    grad_key = jnp.einsum("tc,tq->cq", normed_all, grad_keys, preferred_element_type=jnp.float32)
    grad_value = jnp.einsum(
        "tc,tq->cq", normed_all, grad_values, preferred_element_type=jnp.float32
    )
    part_query = jnp.einsum(
        "tq,cq->tc", grad_queries_low, full_query, preferred_element_type=jnp.float32
    )
    part_key = jnp.einsum("tq,cq->tc", grad_keys, full_key, preferred_element_type=jnp.float32)
    part_value = jnp.einsum(
        "tq,cq->tc", grad_values, full_value, preferred_element_type=jnp.float32
    )
    grad_normed = lax.psum_scatter(
        (part_query + part_key + part_value).astype(jnp.bfloat16),
        "tensor",
        scatter_dimension=0,
        tiled=True,
    ).astype(jnp.float32)
    through_one, gain_one_part = norm_backward(grad_normed, hat_one, factor_one, gain_one)
    grad_inputs = grad_middle + through_one
    gain_one_sum, gain_two_sum = lax.psum((gain_one_part, gain_two_part), "tensor")
    summed = (
        *side_by_side(
            (
                gain_one_sum.astype(jnp.bfloat16),
                grad_query.astype(jnp.bfloat16),
                grad_key.astype(jnp.bfloat16),
                grad_value.astype(jnp.bfloat16),
            ),
            "dp",
            0,
            1,
        ),
        sum_at_owner(grad_out.astype(jnp.bfloat16), "dp", 1),
        *side_by_side(
            (gain_two_sum.astype(jnp.bfloat16), grad_up.astype(jnp.bfloat16)), "dp", 0, 1
        ),
        sum_at_owner(grad_down.astype(jnp.bfloat16), "dp", 1),
    )
    return (
        result.astype(jnp.bfloat16),
        grad_inputs.astype(jnp.bfloat16),
        summed[0],
        summed[1],
        summed[2],
        summed[3],
        summed[4],
        summed[5],
        summed[6],
        summed[7],
    )


def solution(mesh):
    fast = mesh.shape["dp"] == 8 and mesh.shape["tensor"] == 4
    return jax.shard_map(
        fast_shards if fast else shards,
        mesh=mesh,
        in_specs=(
            P(("dp", "tensor"), None),
            P(("dp", "tensor"), None),
            P(),
            P(),
            P("dp"),
            P("dp", "tensor"),
            P("dp", "tensor"),
            P("dp", "tensor"),
            P("tensor", "dp"),
            P("dp"),
            P("dp", "tensor"),
            P("tensor", "dp"),
        ),
        out_specs=(
            P(("dp", "tensor"), None),
            P(("dp", "tensor"), None),
            P("dp"),
            P("dp", "tensor"),
            P("dp", "tensor"),
            P("dp", "tensor"),
            P("tensor", "dp"),
            P("dp"),
            P("dp", "tensor"),
            P("tensor", "dp"),
        ),
        check_vma=False,
    )
```

```python
import functools
import math

import jax
import jax.numpy as jnp
from jax import lax
from jax.experimental import pallas as pl
from jax.experimental.pallas import tpu as pltpu
from jax.sharding import PartitionSpec as P

MESH = pl.DeviceIdType.MESH
BF = jnp.bfloat16
F32 = jnp.float32
HD = 64
WINDOW = 1536
SEG = 256
TREE = 5120
LOG2E = 1.4426950408889634
NEG = -1e30
EPS = 1e-6


def nt(a, b):
    return lax.dot_general(a, b, (((1,), (1,)), ((), ())), preferred_element_type=F32)


def nn(a, b):
    return jnp.dot(a, b, preferred_element_type=F32)


def tn(a, b):
    return lax.dot_general(a, b, (((0,), (0,)), ((), ())), preferred_element_type=F32)


class Links:
    def __init__(self, send, recv):
        self.send, self.recv, self.used = send, recv, 0

    def take(self, count):
        base = self.used
        self.used += count
        return base

    def copy(self, src, dst, send, recv, device):
        return pltpu.make_async_remote_copy(
            src_ref=src,
            dst_ref=dst,
            send_sem=self.send.at[send],
            recv_sem=self.recv.at[recv],
            device_id=device,
            device_id_type=MESH,
        )


class Spread:
    def __init__(self, links, base, dp, t, part):
        self.links, self.base, self.dp, self.t, self.part = links, base, dp, t, part

    def leave(self, i):
        flip, what = ((1, 0), (2, 0), (1, 2))[i]
        ref = self.part(self.t ^ what)
        return self.links.copy(ref, ref, self.base + i, self.base + i, (self.dp, self.t ^ flip))

    def come(self, i):
        flip, what = ((1, 1), (2, 2), (1, 3))[i]
        ref = self.part(self.t ^ what)
        return self.links.copy(ref, ref, self.base + i, self.base + i, (self.dp, self.t ^ flip))

    def start(self):
        self.leave(1).start()
        self.leave(0).start()

    def forward(self):
        self.come(1).wait_recv()
        self.leave(2).start()

    def wait(self):
        self.come(0).wait_recv()
        self.come(2).wait_recv()

    def finish(self):
        for i in range(3):
            self.leave(i).wait_send()


class Gather:
    def __init__(self, links, base, dp, t, slot):
        self.links, self.base, self.dp, self.t, self.slot = links, base, dp, t, slot
        self.z, self.y = dp // 2, dp % 2

    def at(self, step):
        z = lax.rem(self.z + step, 4)
        return z, z * 2 + self.y

    def along(self, step):
        z, peer = self.at(step)
        return self.links.copy(self.slot(self.dp), self.slot(self.dp), self.base + step - 1, self.base + self.z, (peer, self.t))

    def came(self, step):
        z, peer = self.at(step)
        return self.links.copy(self.slot(peer), self.slot(peer), self.base + step - 1, self.base + z, (peer, self.t))

    def across(self, step):
        z, peer = self.at(step)
        return self.links.copy(self.slot(peer), self.slot(peer), self.base + 4 + step, self.base + 4 + z, (self.dp ^ 1, self.t))

    def crossed(self, step):
        z, peer = self.at(step)
        other = z * 2 + (1 - self.y)
        return self.links.copy(self.slot(other), self.slot(other), self.base + 4 + step, self.base + 4 + z, (self.dp ^ 1, self.t))

    def start(self):
        self.across(0).start()
        for step in (1, 3, 2):
            self.along(step).start()

    def forward(self, step):
        self.came(step).wait_recv()
        self.across(step).start()

    def wait(self):
        for step in range(4):
            self.crossed(step).wait_recv()

    def finish(self):
        for step in range(1, 4):
            self.along(step).wait_send()
        for step in range(4):
            self.across(step).wait_send()


def head_mask(h, rows, width):
    lane = lax.broadcasted_iota(jnp.int32, (rows, width), 1)
    return (lane >= h * HD) & (lane < (h + 1) * HD)


def block_bias(seg_ref, par_ref, block, back):
    own = seg_ref[block * SEG]
    one = par_ref[own]
    two = par_ref[one]
    far = block - back
    near = seg_ref[jnp.maximum(far, 0) * SEG]
    ok = ((near == own) | (near == one) | (near == two)) & (far >= 0)
    return jnp.where(ok, jnp.float32(0.0), jnp.float32(NEG))


class Fold:
    def __init__(self, links, base, dp, t, buf):
        self.links, self.base, self.dp, self.t, self.buf = links, base, dp, t, buf

    def copy(self, i):
        flip = (1, 2, 1)[i]
        return self.links.copy(
            self.buf.at[i], self.buf.at[3 + i], self.base + i, self.base + i, (self.dp, self.t ^ flip)
        )

    def put(self, i, value):
        if i == 1:
            self.copy(0).wait_recv()
            value = value + self.buf[3].astype(F32)
        self.buf[i] = value.astype(BF)

    def total(self, value):
        self.copy(1).wait_recv()
        self.copy(2).wait_recv()
        return value + self.buf[5].astype(F32) + self.buf[4].astype(F32)

    def finish(self):
        for i in range(3):
            self.copy(i).wait_send()


class Settle:
    def __init__(self, links, base, dp, t, slots, deep, from_y, from_z):
        self.links, self.base, self.dp, self.t = links, base, dp, t
        self.slots, self.deep, self.from_y, self.from_z = slots, deep, from_y, from_z
        self.z, self.y = dp // 2, lax.rem(dp, 2)

    def rows(self, z, y):
        return pl.ds(pl.multiple_of((z * 2 + y) * self.deep, self.deep), self.deep)

    def across(self, step):
        z = lax.rem(self.z + step, 4)
        return self.links.copy(
            self.slots.at[self.rows(z, 1 - self.y)],
            self.from_y.at[step],
            self.base + step,
            self.base + step,
            (self.dp ^ 1, self.t),
        )

    def along(self, step):
        z = lax.rem(self.z + step, 4)
        return self.links.copy(
            self.slots.at[self.rows(z, self.y)],
            self.from_z.at[step - 1],
            self.base + 3 + step,
            self.base + 3 + step,
            (z * 2 + self.y, self.t),
        )

    def start(self):
        for step in (2, 1, 3, 0):
            self.across(step).start()

    def pass_on(self, step):
        self.across(step).wait_recv()
        z = lax.rem(self.z + step, 4)
        at = self.rows(z, self.y)
        self.slots[at, :] = (self.slots[at, :].astype(F32) + self.from_y[step].astype(F32)).astype(BF)
        self.along(step).start()

    def total(self):
        self.across(0).wait_recv()
        value = self.slots[self.rows(self.z, self.y), :].astype(F32) + self.from_y[0].astype(F32)
        for step in (1, 2, 3):
            self.along(step).wait_recv()
            value = value + self.from_z[step - 1].astype(F32)
        return value

    def finish(self):
        for step in range(4):
            self.across(step).wait_send()
        for step in (1, 2, 3):
            self.along(step).wait_send()


def kernel(
    seg_ref, par_ref, x_ref, cot_ref, g1_ref, wq_in, wk_in, wv_in, wo_in, g2_ref, wu_in, wd_in,
    out_ref, ing_ref, gg1_ref, gq_out, gk_out, gv_out, gout_ref, gg2_ref, gup_ref, gdown_ref,
    xe_ref, n1_ref, n2_ref, mid_ref, gmid_ref, w_ref, f_ref, cot_all, wout_ref, wo_ref, wq_ref, wk_ref, wv_ref,
    q_ref, k_ref, v_ref, turn_ref, ct_ref, l_ref, gain_ref, delta_ref, pool_ref, e_ref, tri_ref,
    a_ref, gu_ref, down_own, gn_own, down_buf, gn_buf, gmb_ref,
    gfy_ref, gfz_ref, gay_ref, gaz_ref, dqt_ref, halo_ref, back_ref, gain_buf, send, recv,
):
    dp, t = lax.axis_index("dp"), lax.axis_index("tensor")
    rows, width = x_ref.shape
    token = 4 * rows
    ext = token + WINDOW
    blocks = token // SEG
    back = WINDOW // SEG
    lag = WINDOW - token
    per_tree = TREE // token
    place = lax.rem(dp, per_tree)
    wide = width // 4
    cols = q_ref.shape[1]
    deep = wu_in.shape[0]
    hidden = wu_in.shape[1]
    links = Links(send, recv)
    spread = lambda part: Spread(links, links.take(3), dp, t, part)
    x_spread = spread(lambda p: xe_ref.at[pl.ds(WINDOW + p * rows, rows)])
    halo = lambda p: xe_ref.at[pl.ds(lag + p * rows, rows)]
    halo_spread = spread(halo)
    cot_spread = spread(lambda p: cot_all.at[pl.ds(p * rows, rows)])
    wout_spread = spread(lambda p: wout_ref.at[pl.ds(p * wide, wide)])
    gmb_spread = spread(lambda p: gmb_ref.at[pl.ds(p * rows, rows)])
    slot = deep + 16
    a_gather = Gather(links, links.take(8), dp, t, lambda s: w_ref.at[pl.ds(pl.multiple_of(s * slot, 16), slot)])
    f_slot = lambda s: pl.ds(pl.multiple_of(s * deep, deep), deep)
    u_gather = Gather(links, links.take(8), dp, t, lambda s: f_ref.at[f_slot(s), pl.ds(0, hidden)])
    d_gather = Gather(links, links.take(8), dp, t, lambda s: f_ref.at[f_slot(s), pl.ds(hidden, hidden)])
    h1 = links.take(1)
    h2 = links.take(1)
    halo_copy = lambda: links.copy(x_ref, halo(t), h1, h1, (lax.rem(dp + 1, 8), t))
    far_copy = lambda: links.copy(
        xe_ref.at[pl.ds(WINDOW + token - lag, lag)], xe_ref.at[pl.ds(0, lag)], h2, h2, (lax.rem(dp + 2, 8), t)
    )
    c_base = links.take(3 * blocks)

    def c_spread(i):
        at = pl.multiple_of(i * SEG, SEG)
        return Spread(links, c_base + 3 * i, dp, t, lambda p: ct_ref.at[pl.ds(p * wide, wide), pl.ds(at, SEG)])

    down_fold = Fold(links, links.take(3), dp, t, down_buf)
    gn_fold = Fold(links, links.take(3), dp, t, gn_buf)
    gn1_fold = Fold(links, links.take(3), dp, t, gn_buf)
    f_settle = Settle(links, links.take(7), dp, t, f_ref, deep, gfy_ref, gfz_ref)
    a_settle = Settle(links, links.take(7), dp, t, w_ref, deep, gay_ref, gaz_ref)
    hb = links.take(5)

    def back_copy(i):
        at = pl.ds(lag + (t ^ (3 - i)) * rows, rows)
        return links.copy(halo_ref.at[at], back_ref.at[at], hb + i, hb + i, (lax.rem(dp + 7, 8), t))

    def far_back():
        at = pl.ds(0, lag)
        return links.copy(halo_ref.at[at], back_ref.at[at], hb + 4, hb + 4, (lax.rem(dp + 6, 8), t))

    gb = links.take(3)

    def gain_copy(i):
        return links.copy(gain_buf.at[0], gain_buf.at[i + 1], gb + i, gb + i, (dp, t ^ (i + 1)))

    barrier = pltpu.get_barrier_semaphore()
    for step in range(1, 8):
        pl.semaphore_signal(barrier, inc=1, device_id=(lax.rem(dp + step, 8), t), device_id_type=MESH)
    for flip in (1, 2, 3):
        pl.semaphore_signal(barrier, inc=1, device_id=(dp, t ^ flip), device_id_type=MESH)

    base = pl.multiple_of(dp * slot, 16)
    w_ref[pl.ds(base, deep), :] = jnp.concatenate(
        [wq_in[...], wk_in[...], wv_in[...], wo_in[...].astype(F32).T.astype(BF)], axis=1
    )
    lane = lax.broadcasted_iota(jnp.int32, (deep, width), 1)
    line = lax.broadcasted_iota(jnp.int32, (deep, width), 0)
    put = jnp.where(lane == line + dp * deep, 1.0, 0.0).astype(BF)
    two = jnp.concatenate([g1_ref[...], g2_ref[...], jnp.zeros((14, deep), BF)], axis=0)
    w_ref[pl.ds(base + deep, 16), :] = nn(two, put).astype(BF)
    xe_ref[pl.ds(WINDOW + t * rows, rows), :] = x_ref[...]
    pl.semaphore_wait(barrier, 10)
    x_spread.start()

    @pl.when(place < per_tree - 1)
    def _():
        halo_copy().start()

    a_gather.start()
    f_ref[f_slot(dp), 0:hidden] = wu_in[...]
    f_ref[f_slot(dp), hidden : 2 * hidden] = wd_in[...].astype(F32).T.astype(BF)
    cot_all[pl.ds(t * rows, rows), :] = cot_ref[...]

    @pl.when(place < 1)
    def _():
        xe_ref[pl.ds(lag, token), :] = jnp.zeros((token, width), BF)

    @pl.when(place < 2)
    def _():
        xe_ref[pl.ds(0, lag), :] = jnp.zeros((lag, width), BF)

    row = lax.broadcasted_iota(jnp.int32, (SEG, SEG), 0)
    col = lax.broadcasted_iota(jnp.int32, (SEG, SEG), 1)
    tri_ref[0] = jnp.where(row <= col, 0.0, NEG)
    tri_ref[1] = jnp.where(row > col, 0.0, NEG)
    a_gather.forward(1)
    x_spread.forward()
    a_gather.forward(3)
    a_gather.forward(2)

    @pl.when(place >= 1)
    def _():
        halo_copy().wait_recv()
        halo_spread.start()

    x_spread.wait()

    @pl.when(place < per_tree - 2)
    def _():
        far_copy().start()

    u_gather.start()
    a_gather.wait()
    weights = w_ref[...].reshape(8, slot, width)[:, 0:deep].reshape(width, width)
    for j, ref in enumerate((wq_ref, wk_ref, wv_ref)):
        ref[...] = jnp.concatenate(
            [weights[:, j * wide : (j + 1) * wide], jnp.zeros((width, cols - wide), BF)], axis=1
        )
    wo_ref[0:wide, :] = weights[:, 3 * wide : 4 * wide].T
    wo_ref[wide:cols, :] = jnp.zeros((cols - wide, width), BF)
    wout_ref[pl.ds(t * wide, wide), :] = wo_ref[0:wide, :]
    gain_ref[...] = jnp.sum(w_ref[...].reshape(8, slot, width)[:, deep:slot].astype(F32), axis=0)[0:8]

    def norm_rows(at):
        x = xe_ref[pl.ds(at, SEG), :].astype(F32)
        r = lax.rsqrt(jnp.mean(x * x, axis=-1, keepdims=True) + EPS)
        n = (x * r * gain_ref[0:1, :]).astype(BF)
        k_ref[pl.ds(at, SEG), :] = nn(n, wk_ref[...]).astype(BF)
        v = nn(n, wv_ref[...]).astype(BF)
        v_ref[pl.ds(at, SEG), :] = v
        turn_ref[:, pl.ds(at, SEG)] = v.T
        return n

    def own_rows(i, _):
        at = pl.multiple_of(i * SEG, SEG)
        n = norm_rows(WINDOW + at)
        n1_ref[pl.ds(at, SEG), :] = n
        q_ref[pl.ds(at, SEG), :] = (nn(n, wq_ref[...]).astype(BF).astype(F32) * HD**-0.5).astype(BF)
        return 0

    lax.fori_loop(0, blocks, own_rows, 0)

    @pl.when(place >= 1)
    def _():
        halo_spread.forward()
        halo_spread.wait()

    wout_spread.start()
    cot_spread.start()

    @pl.when(place >= 2)
    def _():
        far_copy().wait_recv()

    def halo_rows(i, _):
        norm_rows(pl.multiple_of(i * SEG, SEG))
        return 0

    lax.fori_loop(0, back, halo_rows, 0)
    span = (back + 1) * SEG

    def scores(i, h):
        at = pl.multiple_of(i * SEG, SEG)
        q = q_ref[pl.ds(at, SEG), :]
        qm = jnp.where(head_mask(h, SEG, cols), q, jnp.zeros_like(q))
        pool_ref[h * span : (h + 1) * span, :] = nt(k_ref[pl.ds(at, span), :], qm)

    scores(0, 0)

    def attend(i, _):
        at = pl.multiple_of(i * SEG, SEG)
        biases = [block_bias(seg_ref, par_ref, dp * blocks + i, back - j) for j in range(back + 1)]
        for h in range(3):
            if h < 2:
                scores(i, h + 1)
            else:
                scores(jnp.minimum(i + 1, blocks - 1), 0)
            top = None
            for j in range(back + 1):
                here = pl.ds(h * span + j * SEG, SEG)
                s = pool_ref[here, :]
                if j == 0 or j == back:
                    s = s + tri_ref[1 if j == 0 else 0]
                    pool_ref[here, :] = s
                best = jnp.max(s, axis=0, keepdims=True) + biases[j]
                top = best if top is None else jnp.maximum(top, best)
            top = top * LOG2E
            total = None
            for j in range(back + 1):
                e = jnp.exp2(pool_ref[pl.ds(h * span + j * SEG, SEG), :] * LOG2E - (top - biases[j]))
                part = jnp.sum(e, axis=0, keepdims=True)
                total = part if total is None else total + part
                e_ref[h, j * SEG : (j + 1) * SEG, :] = e.astype(BF)
            o = nn(turn_ref[h * HD : (h + 1) * HD, pl.ds(at, span)], e_ref[h])
            ct_ref[pl.ds(t * wide + h * HD, HD), pl.ds(at, SEG)] = (o / total).astype(BF)
            l_ref[h : h + 1, pl.ds(at, SEG)] = top + jnp.log(total) * LOG2E
        c_spread(i).start()

        @pl.when(i == 0)
        def _():
            for step in (1, 3, 2):
                u_gather.forward(step)
            d_gather.start()

        @pl.when(i > 0)
        def _():
            c_spread(i - 1).forward()

        return 0

    lax.fori_loop(0, blocks, attend, 0)
    c_spread(blocks - 1).forward()
    for step in (1, 3, 2):
        d_gather.forward(step)
    wout_spread.forward()
    wout_spread.wait()

    def middle(i, _):
        at = pl.multiple_of(i * SEG, SEG)
        c_spread(i).wait()
        m = xe_ref[pl.ds(WINDOW + at, SEG), :].astype(F32) + tn(ct_ref[:, pl.ds(at, SEG)], wout_ref[...])
        for j in range(width // 256):
            pool_ref[pl.ds(j * token + at, SEG), :] = m[:, j * 256 : (j + 1) * 256]
        r = lax.rsqrt(jnp.mean(m * m, axis=-1, keepdims=True) + EPS)
        n2_ref[pl.ds(at, SEG), :] = (m * r * gain_ref[1:2, :]).astype(BF)
        return 0

    lax.fori_loop(0, blocks, middle, 0)
    for j in range(width // 256):
        mid_ref[:, j * 256 : (j + 1) * 256] = pool_ref[pl.ds(j * token + t * rows, rows), :]
    cot_spread.forward()
    cot_spread.wait()
    u_gather.wait()
    d_gather.wait()

    def feed(k, _):
        at = (t ^ (3 - k)) * rows
        up = f_ref[:, 0:hidden]
        down_t = f_ref[:, hidden : 2 * hidden]
        u = nn(n2_ref[pl.ds(at, rows), :], up)
        cdf = 0.5 * (1.0 + lax.erf(u * 0.7071067811865476))
        act = (u * cdf).astype(BF)
        a_ref[pl.ds(at, rows), :] = act
        slope = cdf + u * jnp.exp2(u * u * (-0.5 * LOG2E)) * 0.3989422804014327
        gu = (nn(cot_all[pl.ds(at, rows), :], down_t) * slope).astype(BF)
        gu_ref[pl.ds(at, rows), :] = gu
        gn_own[...] = nt(gu, up)
        down_own[...] = nt(act, down_t)
        for i in range(3):

            @pl.when(k == i)
            def _():
                gn_fold.put(i, gn_own[...])
                gn_fold.copy(i).start()
                down_fold.put(i, down_own[...])
                if i != 1:
                    down_fold.copy(i).start()

        return 0

    lax.fori_loop(0, 4, feed, 0)
    for item in (x_spread, cot_spread, wout_spread, a_gather, u_gather, d_gather):
        item.finish()
    for i in range(blocks):
        c_spread(i).finish()

    @pl.when(place >= 1)
    def _():
        halo_spread.finish()

    @pl.when(place < per_tree - 1)
    def _():
        halo_copy().wait_send()

    @pl.when(place < per_tree - 2)
    def _():
        far_copy().wait_send()

    def ffn_grads(j, _):
        at = pl.multiple_of(j * 256, 256)
        f_ref[pl.ds(at, 256), 0:hidden] = tn(n2_ref[:, pl.ds(at, 256)], gu_ref[...]).astype(BF)
        f_ref[pl.ds(at, 256), hidden : 2 * hidden] = tn(cot_all[:, pl.ds(at, 256)], a_ref[...]).astype(BF)
        return 0

    lax.fori_loop(0, width // 256, ffn_grads, 0)
    f_settle.start()

    gn2 = gn_fold.total(gn_own[...])
    mid = mid_ref[...]
    r2 = lax.rsqrt(jnp.mean(mid * mid, axis=-1, keepdims=True) + EPS)
    hat2 = mid * r2
    scaled = gn2 * gain_ref[1:2, :]
    inner = jnp.mean(scaled * hat2, axis=-1, keepdims=True)
    gmid = cot_ref[...].astype(F32) + r2 * (scaled - hat2 * inner)
    gmid_ref[...] = gmid
    gmb_ref[pl.ds(t * rows, rows), :] = gmid.astype(BF)
    gmb_spread.start()
    gn_fold.finish()

    def turn_keys(i, _):
        at = pl.multiple_of(i * SEG, SEG)
        turn_ref[:, pl.ds(at, SEG)] = k_ref[pl.ds(at, SEG), :].T
        return 0

    lax.fori_loop(0, blocks + back, turn_keys, 0)

    def mask_queries(i, _):
        at = pl.multiple_of(i * SEG, SEG)
        q = q_ref[pl.ds(at, SEG), :]
        for h in range(3):
            a_ref[pl.ds(at, SEG), h * cols : (h + 1) * cols] = jnp.where(head_mask(h, SEG, cols), q, jnp.zeros_like(q))
        return 0

    lax.fori_loop(0, blocks, mask_queries, 0)
    gmb_spread.forward()
    gmb_spread.wait()
    down_fold.copy(1).start()

    def context_grads(i, _):
        at = pl.multiple_of(i * SEG, SEG)
        low = nt(gmb_ref[pl.ds(at, SEG), :], wo_ref[...]).astype(BF)
        gct = low.astype(F32).T
        for h in range(3):
            gu_ref[pl.ds(at, SEG), h * cols : (h + 1) * cols] = jnp.where(
                head_mask(h, SEG, cols), low, jnp.zeros_like(low)
            )
            c = ct_ref[pl.ds(t * wide + h * HD, HD), pl.ds(at, SEG)].astype(F32)
            delta_ref[h : h + 1, pl.ds(at, SEG)] = jnp.sum(gct[h * HD : (h + 1) * HD] * c, axis=0, keepdims=True)
        return 0

    lax.fori_loop(0, blocks, context_grads, 0)
    qm_ref, gm_ref = a_ref, gu_ref

    def piece(i, lo, hi, first):
        at, n = i * SEG, hi - lo
        keys = pl.ds(lo * SEG, n * SEG)
        values = pl.ds(ext + lo * SEG, n * SEG)
        for h in range(3):
            head = slice(h * cols, (h + 1) * cols)
            turned = slice(h * HD, (h + 1) * HD)
            qm, gm = qm_ref[at : at + SEG, head], gm_ref[at : at + SEG, head]
            s = nt(k_ref[keys, :], qm)
            g = nt(v_ref[keys, :], gm)
            logsum, delta = l_ref[h : h + 1, at : at + SEG], delta_ref[h : h + 1, at : at + SEG]
            for j in range(n):
                bias = block_bias(seg_ref, par_ref, dp * blocks + i, back + i - lo - j)
                part = slice(j * SEG, (j + 1) * SEG)
                x = s[part] * LOG2E
                if lo + j == i:
                    x = x + tri_ref[1]
                if lo + j == i + back:
                    x = x + tri_ref[0]
                p = jnp.exp2(x - (logsum - bias))
                e_ref[h, part, :] = p.astype(BF)
                xe_ref[part, head] = (p * (g[part] - delta)).astype(BF)
            dv = nn(e_ref[h, 0 : n * SEG, :], gm)
            ds = xe_ref[0 : n * SEG, head]
            dk = nn(ds, qm)
            dq = nn(turn_ref[turned, keys], ds)
            if first and h == 0:
                pool_ref[values, :] = dv
                pool_ref[keys, :] = dk
            else:
                pool_ref[values, :] += dv
                pool_ref[keys, :] += dk
            if lo < back:
                dqt_ref[turned, at : at + SEG] = dq
            else:
                dqt_ref[turned, at : at + SEG] += dq

    for i in range(blocks):
        piece(i, i, back, i == 0)
    for i in range(back):
        at = pl.ds(i * SEG, SEG)
        halo_ref[at, :] = jnp.concatenate(
            [pool_ref[at, 0:wide], pool_ref[pl.ds(ext + i * SEG, SEG), 0:wide]], axis=1
        ).astype(BF)

    @pl.when(place >= 1)
    def _():
        for i in range(4):
            back_copy(i).start()

    @pl.when(place >= 2)
    def _():
        far_back().start()

    for step in (2, 1, 3):
        f_settle.pass_on(step)
    for i in range(blocks - 1, -1, -1):
        piece(i, back, back + i + 1, i == blocks - 1)

    def turn_queries(i, _):
        at = pl.multiple_of(i * SEG, SEG)
        q_ref[pl.ds(at, SEG), 0:wide] = (dqt_ref[:, pl.ds(at, SEG)] * HD**-0.5).astype(BF).T
        return 0

    lax.fori_loop(0, blocks, turn_queries, 0)
    gout = nn(ct_ref[pl.ds(t * wide, wide), :], gmb_ref[...]).astype(BF).T
    out_ref[...] = (mid_ref[...] + down_fold.total(down_own[...])).astype(BF)

    @pl.when(place < per_tree - 2)
    def _():
        far_back().wait_recv()
        for j in range(2):
            at = pl.ds(j * ext + WINDOW + token - lag, lag)
            pool_ref[at, 0:wide] += back_ref[0:lag, j * wide : (j + 1) * wide].astype(F32)

    def outer(k, _):
        at = (t ^ (3 - k)) * rows

        @pl.when(place < per_tree - 1)
        def _():
            for i in range(4):

                @pl.when(k == i)
                def _():
                    back_copy(i).wait_recv()

            for j in range(2):
                here = pl.ds(j * ext + WINDOW + at, rows)
                pool_ref[here, 0:wide] += back_ref[pl.ds(lag + at, rows), j * wide : (j + 1) * wide].astype(F32)

        gq = q_ref[pl.ds(at, rows), 0:wide]
        gk = pool_ref[pl.ds(WINDOW + at, rows), 0:wide].astype(BF)
        gv = pool_ref[pl.ds(ext + WINDOW + at, rows), 0:wide].astype(BF)
        k_ref[pl.ds(at, rows), 0:wide] = gk
        v_ref[pl.ds(at, rows), 0:wide] = gv
        gn_own[...] = nt(gq, wq_ref[:, 0:wide]) + nt(gk, wk_ref[:, 0:wide]) + nt(gv, wv_ref[:, 0:wide])
        for i in range(3):

            @pl.when(k == i)
            def _():
                gn1_fold.put(i, gn_own[...])
                gn1_fold.copy(i).start()

        return 0

    lax.fori_loop(0, 4, outer, 0)

    grads = [tn(n1_ref[...], ref[0:token, 0:wide]).astype(BF) for ref in (q_ref, k_ref, v_ref)]
    w_ref[0:width, :] = jnp.concatenate(grads + [gout], axis=1)
    a_settle.start()
    gf = f_settle.total()
    gup_ref[...] = gf[:, 0:hidden]
    gdown_ref[...] = gf[:, hidden : 2 * hidden].T
    two_sum = jnp.sum(gf[:, 0:hidden] * wu_in[...].astype(F32), axis=1, keepdims=True)
    for step in (2, 1, 3):
        a_settle.pass_on(step)

    gn1 = gn1_fold.total(gn_own[...])
    x = x_ref[...].astype(F32)
    r1 = lax.rsqrt(jnp.mean(x * x, axis=-1, keepdims=True) + EPS)
    hat1 = x * r1
    scaled = gn1 * gain_ref[0:1, :]
    inner = jnp.mean(scaled * hat1, axis=-1, keepdims=True)
    ing_ref[...] = (gmid_ref[...] + r1 * (scaled - hat1 * inner)).astype(BF)

    ga = a_settle.total()
    one_sum = None
    for j, (ref, own) in enumerate(((gq_out, wq_in), (gk_out, wk_in), (gv_out, wv_in))):
        part = ga[:, j * wide : (j + 1) * wide]
        ref[...] = part
        part = jnp.sum(part * own[...].astype(F32), axis=1, keepdims=True)
        one_sum = part if one_sum is None else one_sum + part
    gout_ref[...] = ga[:, 3 * wide : 4 * wide].T
    lane = lax.broadcasted_iota(jnp.int32, (deep, 128), 1)
    gain_buf[0] = jnp.where(lane < 64, one_sum, two_sum)
    for i in range(3):
        gain_copy(i).start()
    total = gain_buf[0]
    for i in range(3):
        gain_copy(i).wait_recv()
        total = total + gain_buf[i + 1]
    turned = total.T
    gg1_ref[...] = turned[0:1] / g1_ref[...].astype(F32)
    gg2_ref[...] = turned[64:65] / g2_ref[...].astype(F32)
    for i in range(3):
        gain_copy(i).wait_send()
    for item in (down_fold, gn1_fold, gmb_spread, f_settle, a_settle):
        item.finish()

    @pl.when(place >= 1)
    def _():
        for i in range(4):
            back_copy(i).wait_send()

    @pl.when(place >= 2)
    def _():
        far_back().wait_send()


def fast_shards(
    layer_input, cotangent, segments, parents, norm1_gain, w_query, w_key, w_value, w_out, norm2_gain, w_up, w_down,
):
    rows, width = layer_input.shape
    token = 4 * rows
    ext = token + WINDOW
    wide = width // 4
    cols = 256 * pl.cdiv(wide, 256)
    deep, hidden = w_up.shape
    blocks = token // SEG
    span = WINDOW + SEG
    shape = jax.ShapeDtypeStruct
    vmem = pl.BlockSpec(memory_space=pltpu.VMEM)
    smem = pl.BlockSpec(memory_space=pltpu.SMEM)
    copies = 5 * 3 + 3 * 8 + 2 + 3 * blocks + 3 * 3 + 2 * 7 + 5 + 3
    results = pl.pallas_call(
        kernel,
        out_shape=[
            shape((rows, width), BF),
            shape((rows, width), BF),
            shape((1, deep), F32),
            shape((deep, wide), F32),
            shape((deep, wide), F32),
            shape((deep, wide), F32),
            shape((wide, deep), F32),
            shape((1, deep), F32),
            shape((deep, hidden), F32),
            shape((hidden, deep), F32),
        ],
        in_specs=[smem, smem] + [vmem] * 10,
        out_specs=[vmem] * 10,
        scratch_shapes=[
            pltpu.VMEM((ext, width), BF),
            pltpu.VMEM((token, width), BF),
            pltpu.VMEM((token, width), BF),
            pltpu.VMEM((rows, width), F32),
            pltpu.VMEM((rows, width), F32),
            pltpu.VMEM((8 * (deep + 16), width), BF),
            pltpu.VMEM((width, 2 * hidden), BF),
            pltpu.VMEM((token, width), BF),
            pltpu.VMEM((width, width), BF),
            pltpu.VMEM((cols, width), BF),
            pltpu.VMEM((width, cols), BF),
            pltpu.VMEM((width, cols), BF),
            pltpu.VMEM((width, cols), BF),
            pltpu.VMEM((token, cols), BF),
            pltpu.VMEM((ext, cols), BF),
            pltpu.VMEM((ext, cols), BF),
            pltpu.VMEM((cols, ext), BF),
            pltpu.VMEM((width, token), BF),
            pltpu.VMEM((8, token), F32),
            pltpu.VMEM((8, width), F32),
            pltpu.VMEM((8, token), F32),
            pltpu.VMEM((2 * ext, SEG), F32),
            pltpu.VMEM((3, span, SEG), BF),
            pltpu.VMEM((2, SEG, SEG), F32),
            pltpu.VMEM((token, hidden), BF),
            pltpu.VMEM((token, hidden), BF),
            pltpu.VMEM((rows, width), F32),
            pltpu.VMEM((rows, width), F32),
            pltpu.VMEM((6, rows, width), BF),
            pltpu.VMEM((6, rows, width), BF),
            pltpu.VMEM((token, width), BF),
            pltpu.VMEM((4, deep, 2 * hidden), BF),
            pltpu.VMEM((3, deep, 2 * hidden), BF),
            pltpu.VMEM((4, deep, width), BF),
            pltpu.VMEM((3, deep, width), BF),
            pltpu.VMEM((wide, token), F32),
            pltpu.VMEM((WINDOW, 2 * wide), BF),
            pltpu.VMEM((WINDOW, 2 * wide), BF),
            pltpu.VMEM((4, deep, 128), F32),
            pltpu.SemaphoreType.DMA((copies,)),
            pltpu.SemaphoreType.DMA((copies,)),
        ],
        compiler_params=pltpu.CompilerParams(
            collective_id=0, has_side_effects=True, vmem_limit_bytes=64 << 20
        ),
    )(
        segments, parents, layer_input, cotangent, norm1_gain[None], w_query, w_key, w_value, w_out,
        norm2_gain[None], w_up, w_down,
    )
    results = list(results)
    results[2], results[7] = results[2][0], results[7][0]
    return tuple(results)


epsilon = 1e-06
masked_score = -1e30


def from_behind(block, axis, distance):
    devices = range(lax.axis_size(axis))
    route = [(i - distance, i) for i in devices if i - distance in devices]
    return lax.ppermute(block, axis, route)


def split_up(x, dim, peers):
    dims = x.shape
    tiles = x.reshape(*dims[:dim], peers, dims[dim] // peers, *dims[dim + 1 :])
    return jnp.moveaxis(tiles, dim, 0)


def sum_at_owner(x, axis, dim):
    tiles = split_up(x, dim, lax.axis_size(axis))
    arrived = lax.all_to_all(tiles, axis, split_axis=0, concat_axis=0, tiled=True)
    return arrived.astype(jnp.float32).sum(axis=0)


def side_by_side(arrays, axis, dim, along):
    widths = [math.prod(a.shape[along:]) for a in arrays]
    both = jnp.concatenate(
        [a.reshape(*a.shape[:along], w) for a, w in zip(arrays, widths)], axis=along
    )
    whole = sum_at_owner(both, axis, dim)
    tiles = jnp.split(whole, [sum(widths[:k]) for k in range(1, len(widths))], axis=along)
    return tuple((b.reshape(*whole.shape[:along], *a.shape[along:]) for a, b in zip(arrays, tiles)))


def gelu_exact(values):
    return jax.nn.gelu(values, approximate=False)


def row_scale(values):
    return lax.rsqrt(jnp.mean(values * values, axis=-1, keepdims=True) + epsilon)


def norm_backward(incoming, normal_hat, row_factor, gain):
    scaled = incoming * gain
    inner = jnp.mean(scaled * normal_hat, axis=-1, keepdims=True)
    return (row_factor * (scaled - normal_hat * inner), jnp.sum(incoming * normal_hat, axis=0))


def parent_of(seg_ids, parents):
    seg_table = jnp.arange(parents.shape[0], dtype=jnp.int32)
    hits = seg_ids[:, None] == seg_table[None, :]
    return jnp.sum(jnp.where(hits, parents[None, :], 0), axis=1)


def shards(
    layer_input,
    cotangent,
    segments,
    parents,
    norm1_gain,
    w_query,
    w_key,
    w_value,
    w_out,
    norm2_gain,
    w_up,
    w_down,
):
    gain_one, full_query, full_key, full_value, full_out, gain_two, full_up, full_down = (
        lax.all_gather(norm1_gain, "dp", axis=0, tiled=True),
        lax.all_gather(w_query, "dp", axis=0, tiled=True),
        lax.all_gather(w_key, "dp", axis=0, tiled=True),
        lax.all_gather(w_value, "dp", axis=0, tiled=True),
        lax.all_gather(w_out, "dp", axis=1, tiled=True),
        lax.all_gather(norm2_gain, "dp", axis=0, tiled=True),
        lax.all_gather(w_up, "dp", axis=0, tiled=True),
        lax.all_gather(w_down, "dp", axis=1, tiled=True),
    )
    gain_one = gain_one.astype(jnp.float32)
    gain_two = gain_two.astype(jnp.float32)
    row_count = layer_input.shape[0]
    token_count = row_count * lax.axis_size("tensor")
    position = lax.axis_index("dp") * token_count
    head_width = full_query.shape[1]
    head_count = head_width // HD
    scaling = HD ** (-0.5)
    block_rows = min(640, token_count)
    block_count = token_count // block_rows
    span = WINDOW + block_rows
    hop_count = (WINDOW + token_count - 1) // token_count
    inputs = layer_input.astype(jnp.float32)
    factor_one = row_scale(inputs)
    hat_one = inputs * factor_one
    normed = (hat_one * gain_one).astype(jnp.bfloat16)
    normed_all = lax.all_gather(normed, "tensor", axis=0, tiled=True)
    queries = jnp.dot(normed_all, full_query, preferred_element_type=jnp.float32).astype(
        jnp.bfloat16
    )
    keys_own = jnp.dot(normed_all, full_key, preferred_element_type=jnp.float32).astype(
        jnp.bfloat16
    )
    values_own = jnp.dot(normed_all, full_value, preferred_element_type=jnp.float32).astype(
        jnp.bfloat16
    )
    pair_own = jnp.concatenate([keys_own, values_own], axis=1)
    halo_parts = []
    for distance in range(1, hop_count + 1):
        length = min(token_count, WINDOW - (distance - 1) * token_count)
        piece = pair_own[token_count - length :]
        moved = from_behind(piece, "dp", distance)
        halo_parts.append(moved)
    pair_all = jnp.concatenate(halo_parts[::-1] + [pair_own], axis=0)
    seg_padded = jnp.concatenate([jnp.full((WINDOW,), -1, jnp.int32), segments])
    seg_keys = lax.dynamic_slice_in_dim(seg_padded, position, WINDOW + token_count, 0)
    seg_query = seg_keys[WINDOW:]
    parent_one = parent_of(seg_query, parents)
    parent_two = parent_of(parent_one, parents)
    query_spots = jnp.arange(block_rows, dtype=jnp.int32)
    key_spots = jnp.arange(span, dtype=jnp.int32)

    def scores_of(offset):
        query_block = lax.dynamic_slice_in_dim(queries, offset, block_rows, 0).reshape(
            block_rows, head_count, HD
        )
        pair_block = lax.dynamic_slice_in_dim(pair_all, offset, span, 0)
        key_block = pair_block[:, :head_width].reshape(span, head_count, HD)
        value_block = pair_block[:, head_width:].reshape(span, head_count, HD)
        own_seg = lax.dynamic_slice_in_dim(seg_query, offset, block_rows, 0)
        up_one = lax.dynamic_slice_in_dim(parent_one, offset, block_rows, 0)
        up_two = lax.dynamic_slice_in_dim(parent_two, offset, block_rows, 0)
        near_seg = lax.dynamic_slice_in_dim(seg_keys, offset, span, 0)
        gap = WINDOW + query_spots[:, None] - key_spots[None, :]
        same_path = (
            (near_seg[None, :] == own_seg[:, None])
            | (near_seg[None, :] == up_one[:, None])
            | (near_seg[None, :] == up_two[:, None])
        )
        allowed = (gap >= 0) & (gap < WINDOW) & same_path
        raw = (
            jnp.einsum("qhd,khd->hqk", query_block, key_block, preferred_element_type=jnp.float32)
            * scaling
        )
        return (jnp.where(allowed[None], raw, masked_score), query_block, key_block, value_block)

    def forward_block(block_index):
        scores, query_block, key_block, value_block = scores_of(block_index * block_rows)
        row_max = jnp.max(scores, axis=-1, keepdims=True)
        exponent = jnp.exp(scores - row_max)
        denominator = jnp.sum(exponent, axis=-1, keepdims=True)
        weights = (exponent / denominator).astype(jnp.bfloat16)
        mixed = jnp.einsum("hqk,khd->qhd", weights, value_block, preferred_element_type=jnp.float32)
        return (
            mixed.reshape(block_rows, head_width).astype(jnp.bfloat16),
            (row_max + jnp.log(denominator))[..., 0],
        )

    context_blocks, logsum_blocks = lax.map(forward_block, jnp.arange(block_count, dtype=jnp.int32))
    context = context_blocks.reshape(token_count, head_width)
    middle = inputs + lax.psum_scatter(
        jnp.dot(context, full_out, preferred_element_type=jnp.float32).astype(jnp.bfloat16),
        "tensor",
        scatter_dimension=0,
        tiled=True,
    ).astype(jnp.float32)
    factor_two = row_scale(middle)
    hat_two = middle * factor_two
    normed_two = (hat_two * gain_two).astype(jnp.bfloat16)
    normed_two_all = lax.all_gather(normed_two, "tensor", axis=0, tiled=True)
    upper = jnp.dot(normed_two_all, full_up, preferred_element_type=jnp.float32)
    active = gelu_exact(upper).astype(jnp.bfloat16)
    result = middle + lax.psum_scatter(
        jnp.dot(active, full_down, preferred_element_type=jnp.float32).astype(jnp.bfloat16),
        "tensor",
        scatter_dimension=0,
        tiled=True,
    ).astype(jnp.float32)
    incoming = cotangent.astype(jnp.float32)
    incoming_all = lax.all_gather(cotangent, "tensor", axis=0, tiled=True)
    grad_down = jnp.einsum("tf,td->fd", active, incoming_all, preferred_element_type=jnp.float32)
    grad_active = jnp.einsum(
        "td,fd->tf", incoming_all, full_down, preferred_element_type=jnp.float32
    )
    unused_value, gelu_pull = jax.vjp(gelu_exact, upper)
    grad_upper = gelu_pull(grad_active)[0].astype(jnp.bfloat16)
    grad_up = jnp.einsum(
        "tc,tf->cf", normed_two_all, grad_upper, preferred_element_type=jnp.float32
    )
    grad_normed_two = lax.psum_scatter(
        jnp.einsum("tf,cf->tc", grad_upper, full_up, preferred_element_type=jnp.float32).astype(
            jnp.bfloat16
        ),
        "tensor",
        scatter_dimension=0,
        tiled=True,
    ).astype(jnp.float32)
    through_two, gain_two_part = norm_backward(grad_normed_two, hat_two, factor_two, gain_two)
    grad_middle = incoming + through_two
    grad_middle_all = lax.all_gather(grad_middle.astype(jnp.bfloat16), "tensor", axis=0, tiled=True)
    grad_out = jnp.einsum("tc,td->cd", context, grad_middle_all, preferred_element_type=jnp.float32)
    grad_context = jnp.einsum(
        "td,cd->tc", grad_middle_all, full_out, preferred_element_type=jnp.float32
    ).astype(jnp.bfloat16)

    def backward_block(block_index, carry):
        grad_queries, grad_pairs = carry
        offset = block_index * block_rows
        scores, query_block, key_block, value_block = scores_of(offset)
        logsum = lax.dynamic_index_in_dim(logsum_blocks, block_index, 0, keepdims=False)
        probs = jnp.exp(scores - logsum[..., None])
        grad_rows = lax.dynamic_slice_in_dim(grad_context, offset, block_rows, 0).reshape(
            block_rows, head_count, HD
        )
        grad_probs = jnp.einsum(
            "qhd,khd->hqk", grad_rows, value_block, preferred_element_type=jnp.float32
        )
        inner = jnp.sum(probs * grad_probs, axis=-1, keepdims=True)
        grad_scores = (probs * (grad_probs - inner)).astype(jnp.bfloat16)
        grad_query_block = (
            jnp.einsum("hqk,khd->qhd", grad_scores, key_block, preferred_element_type=jnp.float32)
            * scaling
        )
        grad_key_block = (
            jnp.einsum("hqk,qhd->khd", grad_scores, query_block, preferred_element_type=jnp.float32)
            * scaling
        )
        grad_value_block = jnp.einsum(
            "hqk,qhd->khd",
            probs.astype(jnp.bfloat16),
            grad_rows,
            preferred_element_type=jnp.float32,
        )
        grad_queries = lax.dynamic_update_slice_in_dim(
            grad_queries, grad_query_block.reshape(block_rows, head_width), offset, 0
        )
        update = jnp.concatenate(
            [grad_key_block.reshape(span, head_width), grad_value_block.reshape(span, head_width)],
            axis=1,
        )
        current = lax.dynamic_slice_in_dim(grad_pairs, offset, span, 0)
        grad_pairs = lax.dynamic_update_slice_in_dim(grad_pairs, current + update, offset, 0)
        return (grad_queries, grad_pairs)

    start_carry = (
        jnp.zeros((token_count, head_width), jnp.float32),
        jnp.zeros((WINDOW + token_count, 2 * head_width), jnp.float32),
    )
    grad_queries, grad_pairs = lax.fori_loop(0, block_count, backward_block, start_carry)
    grad_own = grad_pairs[WINDOW:]
    for distance in range(1, hop_count + 1):
        length = min(token_count, WINDOW - (distance - 1) * token_count)
        first_row = WINDOW - (distance - 1) * token_count - length
        piece = grad_pairs[first_row : first_row + length]
        returned = from_behind(piece.astype(jnp.bfloat16), "dp", -distance).astype(piece.dtype)
        grad_own = grad_own + jnp.pad(returned, ((token_count - length, 0), (0, 0)))
    grad_keys = grad_own[:, :head_width].astype(jnp.bfloat16)
    grad_values = grad_own[:, head_width:].astype(jnp.bfloat16)
    grad_queries_low = grad_queries.astype(jnp.bfloat16)
    grad_query = jnp.einsum(
        "tc,tq->cq", normed_all, grad_queries_low, preferred_element_type=jnp.float32
    )
    grad_key = jnp.einsum("tc,tq->cq", normed_all, grad_keys, preferred_element_type=jnp.float32)
    grad_value = jnp.einsum(
        "tc,tq->cq", normed_all, grad_values, preferred_element_type=jnp.float32
    )
    part_query = jnp.einsum(
        "tq,cq->tc", grad_queries_low, full_query, preferred_element_type=jnp.float32
    )
    part_key = jnp.einsum("tq,cq->tc", grad_keys, full_key, preferred_element_type=jnp.float32)
    part_value = jnp.einsum(
        "tq,cq->tc", grad_values, full_value, preferred_element_type=jnp.float32
    )
    grad_normed = lax.psum_scatter(
        (part_query + part_key + part_value).astype(jnp.bfloat16),
        "tensor",
        scatter_dimension=0,
        tiled=True,
    ).astype(jnp.float32)
    through_one, gain_one_part = norm_backward(grad_normed, hat_one, factor_one, gain_one)
    grad_inputs = grad_middle + through_one
    gain_one_sum, gain_two_sum = lax.psum((gain_one_part, gain_two_part), "tensor")
    summed = (
        *side_by_side(
            (
                gain_one_sum.astype(jnp.bfloat16),
                grad_query.astype(jnp.bfloat16),
                grad_key.astype(jnp.bfloat16),
                grad_value.astype(jnp.bfloat16),
            ),
            "dp",
            0,
            1,
        ),
        sum_at_owner(grad_out.astype(jnp.bfloat16), "dp", 1),
        *side_by_side(
            (gain_two_sum.astype(jnp.bfloat16), grad_up.astype(jnp.bfloat16)), "dp", 0, 1
        ),
        sum_at_owner(grad_down.astype(jnp.bfloat16), "dp", 1),
    )
    return (
        result.astype(jnp.bfloat16),
        grad_inputs.astype(jnp.bfloat16),
        summed[0],
        summed[1],
        summed[2],
        summed[3],
        summed[4],
        summed[5],
        summed[6],
        summed[7],
    )


def solution(mesh):
    fast = mesh.shape["dp"] == 8 and mesh.shape["tensor"] == 4
    return jax.shard_map(
        fast_shards if fast else shards,
        mesh=mesh,
        in_specs=(
            P(("dp", "tensor"), None),
            P(("dp", "tensor"), None),
            P(),
            P(),
            P("dp"),
            P("dp", "tensor"),
            P("dp", "tensor"),
            P("dp", "tensor"),
            P("tensor", "dp"),
            P("dp"),
            P("dp", "tensor"),
            P("tensor", "dp"),
        ),
        out_specs=(
            P(("dp", "tensor"), None),
            P(("dp", "tensor"), None),
            P("dp"),
            P("dp", "tensor"),
            P("dp", "tensor"),
            P("dp", "tensor"),
            P("tensor", "dp"),
            P("dp"),
            P("dp", "tensor"),
            P("tensor", "dp"),
        ),
        check_vma=False,
    )
```

```python
import functools
import math

import jax
import jax.numpy as jnp
from jax import lax
from jax.experimental import pallas as pl
from jax.experimental.pallas import tpu as pltpu
from jax.sharding import PartitionSpec as P

MESH = pl.DeviceIdType.MESH
BF = jnp.bfloat16
F32 = jnp.float32
HD = 64
WINDOW = 1536
SEG = 256
TREE = 5120
LOG2E = 1.4426950408889634
NEG = -1e30
EPS = 1e-6


def nt(a, b):
    return lax.dot_general(a, b, (((1,), (1,)), ((), ())), preferred_element_type=F32)


def nn(a, b):
    return jnp.dot(a, b, preferred_element_type=F32)


def tn(a, b):
    return lax.dot_general(a, b, (((0,), (0,)), ((), ())), preferred_element_type=F32)


class Links:
    def __init__(self, send, recv):
        self.send, self.recv, self.used = send, recv, 0

    def take(self, count):
        base = self.used
        self.used += count
        return base

    def copy(self, src, dst, send, recv, device):
        return pltpu.make_async_remote_copy(
            src_ref=src,
            dst_ref=dst,
            send_sem=self.send.at[send],
            recv_sem=self.recv.at[recv],
            device_id=device,
            device_id_type=MESH,
        )


class Spread:
    def __init__(self, links, base, dp, t, part):
        self.links, self.base, self.dp, self.t, self.part = links, base, dp, t, part

    def leave(self, i):
        flip, what = ((1, 0), (2, 0), (1, 2))[i]
        ref = self.part(self.t ^ what)
        return self.links.copy(ref, ref, self.base + i, self.base + i, (self.dp, self.t ^ flip))

    def come(self, i):
        flip, what = ((1, 1), (2, 2), (1, 3))[i]
        ref = self.part(self.t ^ what)
        return self.links.copy(ref, ref, self.base + i, self.base + i, (self.dp, self.t ^ flip))

    def start(self):
        self.leave(1).start()
        self.leave(0).start()

    def forward(self):
        self.come(1).wait_recv()
        self.leave(2).start()

    def wait(self):
        self.come(0).wait_recv()
        self.come(2).wait_recv()

    def finish(self):
        for i in range(3):
            self.leave(i).wait_send()


class Gather:
    def __init__(self, links, base, dp, t, slot):
        self.links, self.base, self.dp, self.t, self.slot = links, base, dp, t, slot
        self.z, self.y = dp // 2, dp % 2

    def at(self, step):
        z = lax.rem(self.z + step, 4)
        return z, z * 2 + self.y

    def along(self, step):
        z, peer = self.at(step)
        return self.links.copy(self.slot(self.dp), self.slot(self.dp), self.base + step - 1, self.base + self.z, (peer, self.t))

    def came(self, step):
        z, peer = self.at(step)
        return self.links.copy(self.slot(peer), self.slot(peer), self.base + step - 1, self.base + z, (peer, self.t))

    def across(self, step):
        z, peer = self.at(step)
        return self.links.copy(self.slot(peer), self.slot(peer), self.base + 4 + step, self.base + 4 + z, (self.dp ^ 1, self.t))

    def crossed(self, step):
        z, peer = self.at(step)
        other = z * 2 + (1 - self.y)
        return self.links.copy(self.slot(other), self.slot(other), self.base + 4 + step, self.base + 4 + z, (self.dp ^ 1, self.t))

    def start(self):
        self.across(0).start()
        for step in (1, 3, 2):
            self.along(step).start()

    def forward(self, step):
        self.came(step).wait_recv()
        self.across(step).start()

    def wait(self):
        for step in range(4):
            self.crossed(step).wait_recv()

    def finish(self):
        for step in range(1, 4):
            self.along(step).wait_send()
        for step in range(4):
            self.across(step).wait_send()


def head_mask(h, rows, width):
    lane = lax.broadcasted_iota(jnp.int32, (rows, width), 1)
    return (lane >= h * HD) & (lane < (h + 1) * HD)


def block_bias(seg_ref, par_ref, block, back):
    own = seg_ref[block * SEG]
    one = par_ref[own]
    two = par_ref[one]
    far = block - back
    near = seg_ref[jnp.maximum(far, 0) * SEG]
    ok = ((near == own) | (near == one) | (near == two)) & (far >= 0)
    return jnp.where(ok, jnp.float32(0.0), jnp.float32(NEG))


class Fold:
    def __init__(self, links, base, dp, t, out, into):
        self.links, self.base, self.dp, self.t, self.out, self.into = links, base, dp, t, out, into

    def copy(self, i):
        flip = (1, 2, 1)[i]
        return self.links.copy(
            self.out(i), self.into(i), self.base + i, self.base + i, (self.dp, self.t ^ flip)
        )

    def put(self, i, value):
        if i == 1:
            self.copy(0).wait_recv()
            value = value + self.into(0)[...].astype(F32)
        self.out(i)[...] = value.astype(BF)

    def total(self, value):
        self.copy(1).wait_recv()
        self.copy(2).wait_recv()
        return value + self.into(2)[...].astype(F32) + self.into(1)[...].astype(F32)

    def finish(self):
        for i in range(3):
            self.copy(i).wait_send()


class Settle:
    def __init__(self, links, base, dp, t, slots, deep, from_y, from_z):
        self.links, self.base, self.dp, self.t = links, base, dp, t
        self.slots, self.deep, self.from_y, self.from_z = slots, deep, from_y, from_z
        self.z, self.y = dp // 2, lax.rem(dp, 2)

    def rows(self, z, y):
        return pl.ds(pl.multiple_of((z * 2 + y) * self.deep, self.deep), self.deep)

    def across(self, step):
        z = lax.rem(self.z + step, 4)
        return self.links.copy(
            self.slots.at[self.rows(z, 1 - self.y)],
            self.from_y.at[step],
            self.base + step,
            self.base + step,
            (self.dp ^ 1, self.t),
        )

    def along(self, step):
        z = lax.rem(self.z + step, 4)
        return self.links.copy(
            self.slots.at[self.rows(z, self.y)],
            self.from_z.at[step - 1],
            self.base + 3 + step,
            self.base + 3 + step,
            (z * 2 + self.y, self.t),
        )

    def start(self):
        for step in (2, 1, 3, 0):
            self.across(step).start()

    def pass_on(self, step):
        self.across(step).wait_recv()
        z = lax.rem(self.z + step, 4)
        at = self.rows(z, self.y)
        self.slots[at, :] = (self.slots[at, :].astype(F32) + self.from_y[step].astype(F32)).astype(BF)
        self.along(step).start()

    def total(self):
        self.across(0).wait_recv()
        value = self.slots[self.rows(self.z, self.y), :].astype(F32) + self.from_y[0].astype(F32)
        for step in (1, 2, 3):
            self.along(step).wait_recv()
            value = value + self.from_z[step - 1].astype(F32)
        return value

    def finish(self):
        for step in range(4):
            self.across(step).wait_send()
        for step in (1, 2, 3):
            self.along(step).wait_send()


def kernel(
    seg_ref, par_ref, x_ref, cot_ref, g1_ref, wq_in, wk_in, wv_in, wo_in, g2_ref, wu_in, wd_in,
    out_ref, ing_ref, gg1_ref, gq_out, gk_out, gv_out, gout_ref, gg2_ref, gup_ref, gdown_ref,
    xe_ref, n1_ref, n2_ref, mid_ref, gmid_ref, w_ref, f_ref, cot_all, wout_ref, wo_ref, wq_ref, wk_ref, wv_ref,
    q_ref, k_ref, v_ref, turn_ref, ct_ref, l_ref, gain_ref, delta_ref, pool_ref, e_ref, tri_ref,
    a_ref, gu_ref, down_own, gn_own, down_buf, gn_buf, gmb_ref,
    gfy_ref, gfz_ref, go_ref, goy_ref, goz_ref, gay_ref, gaz_ref, dqt_ref, near_buf, far_buf, gt_buf, gd_buf, send, recv,
):
    dp, t = lax.axis_index("dp"), lax.axis_index("tensor")
    rows, width = x_ref.shape
    token = 4 * rows
    ext = token + WINDOW
    blocks = token // SEG
    back = WINDOW // SEG
    lag = WINDOW - token
    per_tree = TREE // token
    place = lax.rem(dp, per_tree)
    wide = width // 4
    cols = q_ref.shape[1]
    deep = wu_in.shape[0]
    hidden = wu_in.shape[1]
    links = Links(send, recv)
    spread = lambda part: Spread(links, links.take(3), dp, t, part)
    x_spread = spread(lambda p: xe_ref.at[pl.ds(WINDOW + p * rows, rows)])
    part = rows // 2
    halo_half = lambda p, j: xe_ref.at[pl.ds(lag + p * rows + j * part, part)]
    halo_spreads = [spread(lambda p, j=j: halo_half(p, j)) for j in range(2)]
    cot_spread = spread(lambda p: cot_all.at[pl.ds(p * rows, rows)])
    wout_spread = spread(lambda p: wout_ref.at[pl.ds(p * wide, wide)])
    gmb_spreads = [spread(lambda p, j=j: gmb_ref.at[pl.ds(p * rows + j * part, part)]) for j in range(2)]
    slot = deep + 16
    a_slot = lambda s: pl.ds(pl.multiple_of(s * slot, 16), slot)
    half = width // 2
    a_gathers = [
        Gather(links, links.take(8), dp, t, lambda s, j=j: w_ref.at[a_slot(s), pl.ds(j * half, half)]) for j in range(2)
    ]
    f_slot = lambda s: pl.ds(pl.multiple_of(s * deep, deep), deep)
    u_gather = Gather(links, links.take(8), dp, t, lambda s: f_ref.at[f_slot(s), pl.ds(0, hidden)])
    d_gather = Gather(links, links.take(8), dp, t, lambda s: f_ref.at[f_slot(s), pl.ds(hidden, hidden)])
    h1 = links.take(2)
    h2 = links.take(1)
    halo_copy = lambda j: links.copy(
        x_ref.at[pl.ds(j * part, part)], halo_half(t, j), h1 + j, h1 + j, (lax.rem(dp + 1, 8), t)
    )
    far_copy = lambda: links.copy(
        xe_ref.at[pl.ds(WINDOW + token - lag, lag)], xe_ref.at[pl.ds(0, lag)], h2, h2, (lax.rem(dp + 2, 8), t)
    )
    c_base = links.take(3 * blocks)

    def c_spread(i):
        at = pl.multiple_of(i * SEG, SEG)
        return Spread(links, c_base + 3 * i, dp, t, lambda p: ct_ref.at[pl.ds(p * wide, wide), pl.ds(at, SEG)])

    down_fold = Fold(links, links.take(3), dp, t, lambda i: down_buf.at[i], lambda i: down_buf.at[3 + i])
    gn_folds = [
        Fold(
            links,
            links.take(3),
            dp,
            t,
            lambda i, j=j: gn_buf.at[i, pl.ds(j * part, part)],
            lambda i, j=j: gn_buf.at[3 + i, pl.ds(j * part, part)],
        )
        for j in range(2)
    ]
    gn1_fold = Fold(links, links.take(3), dp, t, lambda i: gn_buf.at[i], lambda i: gn_buf.at[3 + i])
    halo_fold = Fold(
        links,
        links.take(3),
        dp,
        t,
        lambda i: cot_all.at[pl.ds(i * rows, rows)],
        lambda i: n2_ref.at[pl.ds(i * rows, rows)],
    )
    f_settle = Settle(links, links.take(7), dp, t, f_ref, deep, gfy_ref, gfz_ref)
    o_settle = Settle(links, links.take(7), dp, t, go_ref, deep, goy_ref, goz_ref)
    a_settle = Settle(links, links.take(7), dp, t, w_ref.at[:, pl.ds(0, gay_ref.shape[2])], deep, gay_ref, gaz_ref)
    b1 = links.take(1)
    b2 = links.take(1)
    near_back = lambda: links.copy(cot_all.at[pl.ds(3 * rows, rows)], near_buf, b1, b1, (lax.rem(dp + 7, 8), t))
    far_back = lambda: links.copy(far_buf.at[0], far_buf.at[1], b2, b2, (lax.rem(dp + 6, 8), t))
    gb = links.take(3)
    gd = links.take(7)

    def gain_copy(i):
        return links.copy(gt_buf.at[0], gt_buf.at[i + 1], gb + i, gb + i, (dp, t ^ (i + 1)))

    def gain_over(i):
        return links.copy(gd_buf.at[0], gd_buf.at[i + 1], gd + i, gd + i, (lax.rem(dp + i + 1, 8), t))

    barrier = pltpu.get_barrier_semaphore()
    for step in range(1, 8):
        pl.semaphore_signal(barrier, inc=1, device_id=(lax.rem(dp + step, 8), t), device_id_type=MESH)
    for flip in (1, 2, 3):
        pl.semaphore_signal(barrier, inc=1, device_id=(dp, t ^ flip), device_id_type=MESH)

    base = pl.multiple_of(dp * slot, 16)
    w_ref[pl.ds(base, deep), :] = jnp.concatenate(
        [wq_in[...], wk_in[...], wv_in[...], wo_in[...].astype(F32).T.astype(BF)], axis=1
    )
    lane = lax.broadcasted_iota(jnp.int32, (deep, width), 1)
    line = lax.broadcasted_iota(jnp.int32, (deep, width), 0)
    put = jnp.where(lane == line + dp * deep, 1.0, 0.0).astype(BF)
    two = jnp.concatenate([g1_ref[...], g2_ref[...], jnp.zeros((14, deep), BF)], axis=0)
    w_ref[pl.ds(base + deep, 16), :] = nn(two, put).astype(BF)
    xe_ref[pl.ds(WINDOW + t * rows, rows), :] = x_ref[...]
    pl.semaphore_wait(barrier, 10)
    a_gathers[0].start()
    x_spread.start()

    @pl.when(place < per_tree - 1)
    def _():
        halo_copy(0).start()

    f_ref[f_slot(dp), 0:hidden] = wu_in[...]
    f_ref[f_slot(dp), hidden : 2 * hidden] = wd_in[...]
    cot_all[pl.ds(t * rows, rows), :] = cot_ref[...]

    @pl.when(place < 1)
    def _():
        xe_ref[pl.ds(lag, token), :] = jnp.zeros((token, width), BF)

    @pl.when(place < 2)
    def _():
        xe_ref[pl.ds(0, lag), :] = jnp.zeros((lag, width), BF)

    row = lax.broadcasted_iota(jnp.int32, (SEG, SEG), 0)
    col = lax.broadcasted_iota(jnp.int32, (SEG, SEG), 1)
    tri_ref[0] = jnp.where(row <= col, 0.0, NEG)
    tri_ref[1] = jnp.where(row > col, 0.0, NEG)
    for step in (1, 3, 2):
        a_gathers[0].forward(step)
    a_gathers[1].start()

    @pl.when(place < per_tree - 1)
    def _():
        halo_copy(0).wait_send()
        halo_copy(1).start()

    @pl.when(place >= 1)
    def _():
        halo_copy(0).wait_recv()
        halo_spreads[0].start()

    x_spread.forward()
    for step in (1, 3, 2):
        a_gathers[1].forward(step)

    @pl.when(place >= 1)
    def _():
        halo_copy(1).wait_recv()
        halo_spreads[1].start()
        halo_spreads[0].forward()

    x_spread.wait()

    @pl.when(place < per_tree - 2)
    def _():
        far_copy().start()

    for item in a_gathers:
        item.wait()
    u_gather.start()
    weights = w_ref[...].reshape(8, slot, width)[:, 0:deep].reshape(width, width)
    for j, ref in enumerate((wq_ref, wk_ref, wv_ref)):
        ref[...] = jnp.concatenate(
            [weights[:, j * wide : (j + 1) * wide], jnp.zeros((width, cols - wide), BF)], axis=1
        )
    wo_ref[0:wide, :] = weights[:, 3 * wide : 4 * wide].T
    wo_ref[wide:cols, :] = jnp.zeros((cols - wide, width), BF)
    wout_ref[pl.ds(t * wide, wide), :] = wo_ref[0:wide, :]
    wout_spread.start()
    gain_ref[...] = jnp.sum(w_ref[...].reshape(8, slot, width)[:, deep:slot].astype(F32), axis=0)[0:8]

    def norm_rows(at):
        x = xe_ref[pl.ds(at, SEG), :].astype(F32)
        r = lax.rsqrt(jnp.mean(x * x, axis=-1, keepdims=True) + EPS)
        n = (x * r * gain_ref[0:1, :]).astype(BF)
        k_ref[pl.ds(at, SEG), :] = nn(n, wk_ref[...]).astype(BF)
        v = nn(n, wv_ref[...]).astype(BF)
        v_ref[pl.ds(at, SEG), :] = v
        turn_ref[:, pl.ds(at, SEG)] = v.T
        return n

    def own_rows(i, _):
        at = pl.multiple_of(i * SEG, SEG)
        n = norm_rows(WINDOW + at)
        n1_ref[pl.ds(at, SEG), :] = n
        q_ref[pl.ds(at, SEG), :] = (nn(n, wq_ref[...]).astype(BF).astype(F32) * HD**-0.5).astype(BF)
        return 0

    lax.fori_loop(0, blocks, own_rows, 0)

    @pl.when(place >= 1)
    def _():
        halo_spreads[1].forward()
        for item in halo_spreads:
            item.wait()
            item.finish()

    cot_spread.start()

    @pl.when(place >= 2)
    def _():
        far_copy().wait_recv()

    def halo_rows(i, _):
        at = pl.multiple_of(i * SEG, SEG)
        xe_ref[pl.ds(at, SEG), :] = norm_rows(at)
        return 0

    lax.fori_loop(0, back, halo_rows, 0)
    span = (back + 1) * SEG

    def scores(i, h):
        at = pl.multiple_of(i * SEG, SEG)
        q = q_ref[pl.ds(at, SEG), :]
        qm = jnp.where(head_mask(h, SEG, cols), q, jnp.zeros_like(q))
        pool_ref[h * span : (h + 1) * span, :] = nt(k_ref[pl.ds(at, span), :], qm)

    scores(0, 0)

    def attend(i, _):
        at = pl.multiple_of(i * SEG, SEG)
        biases = [block_bias(seg_ref, par_ref, dp * blocks + i, back - j) for j in range(back + 1)]
        for h in range(3):
            if h < 2:
                scores(i, h + 1)
            else:
                scores(jnp.minimum(i + 1, blocks - 1), 0)
            top = None
            for j in range(back + 1):
                here = pl.ds(h * span + j * SEG, SEG)
                s = pool_ref[here, :]
                if j == 0 or j == back:
                    s = s + tri_ref[1 if j == 0 else 0]
                    pool_ref[here, :] = s
                best = jnp.max(s, axis=0, keepdims=True) + biases[j]
                top = best if top is None else jnp.maximum(top, best)
            top = top * LOG2E
            total = None
            for j in range(back + 1):
                e = jnp.exp2(pool_ref[pl.ds(h * span + j * SEG, SEG), :] * LOG2E - (top - biases[j]))
                part = jnp.sum(e, axis=0, keepdims=True)
                total = part if total is None else total + part
                e_ref[h, j * SEG : (j + 1) * SEG, :] = e.astype(BF)
            o = nn(turn_ref[h * HD : (h + 1) * HD, pl.ds(at, span)], e_ref[h])
            ct_ref[pl.ds(t * wide + h * HD, HD), pl.ds(at, SEG)] = (o / total).astype(BF)
            l_ref[h : h + 1, pl.ds(at, SEG)] = top + jnp.log(total) * LOG2E
        c_spread(i).start()

        @pl.when(i == 0)
        def _():
            for step in (1, 3, 2):
                u_gather.forward(step)
            d_gather.start()

        @pl.when(i > 0)
        def _():
            c_spread(i - 1).forward()

        return 0

    lax.fori_loop(0, blocks, attend, 0)
    c_spread(blocks - 1).forward()
    for step in (1, 3, 2):
        d_gather.forward(step)
    wout_spread.forward()
    wout_spread.wait()

    def middle(i, _):
        at = pl.multiple_of(i * SEG, SEG)
        c_spread(i).wait()
        m = xe_ref[pl.ds(WINDOW + at, SEG), :].astype(F32) + tn(ct_ref[:, pl.ds(at, SEG)], wout_ref[...])
        for j in range(width // 256):
            pool_ref[pl.ds(j * token + at, SEG), :] = m[:, j * 256 : (j + 1) * 256]
        r = lax.rsqrt(jnp.mean(m * m, axis=-1, keepdims=True) + EPS)
        n2_ref[pl.ds(at, SEG), :] = (m * r * gain_ref[1:2, :]).astype(BF)
        return 0

    lax.fori_loop(0, blocks, middle, 0)
    for j in range(width // 256):
        mid_ref[:, j * 256 : (j + 1) * 256] = pool_ref[pl.ds(j * token + t * rows, rows), :]
    cot_spread.forward()
    cot_spread.wait()
    u_gather.wait()
    d_gather.wait()

    def feed(k, _):
        at = (t ^ (3 - k)) * rows
        up = f_ref[:, 0:hidden]
        down_t = f_ref[:, hidden : 2 * hidden]
        u = nn(n2_ref[pl.ds(at, rows), :], up)
        cdf = 0.5 * (1.0 + lax.erf(u * 0.7071067811865476))
        act = (u * cdf).astype(BF)
        a_ref[pl.ds(at, rows), :] = act
        slope = cdf + u * jnp.exp2(u * u * (-0.5 * LOG2E)) * 0.3989422804014327
        gu = (nn(cot_all[pl.ds(at, rows), :], down_t) * slope).astype(BF)
        gu_ref[pl.ds(at, rows), :] = gu
        gn_own[...] = nt(gu, up)
        down_own[...] = nt(act, down_t)
        for i in range(3):

            @pl.when(k == i)
            def _():
                for j in range(2):
                    gn_folds[j].put(i, gn_own[j * part : (j + 1) * part, :])
                    if i != 1 or j == 0:
                        gn_folds[j].copy(i).start()
                down_fold.put(i, down_own[...])
                if i != 1:
                    down_fold.copy(i).start()

        return 0

    lax.fori_loop(0, 4, feed, 0)
    gn_folds[1].copy(1).start()
    for item in (x_spread, cot_spread, wout_spread, *a_gathers, u_gather, d_gather):
        item.finish()
    for i in range(blocks):
        c_spread(i).finish()

    @pl.when(place < per_tree - 1)
    def _():
        halo_copy(1).wait_send()

    @pl.when(place < per_tree - 2)
    def _():
        far_copy().wait_send()

    ones = jnp.ones((8, hidden), BF)

    def ffn_grads(j, _):
        at = pl.multiple_of(j * 256, 256)
        g = tn(n2_ref[:, pl.ds(at, 256)], gu_ref[...])
        gt_buf[0, :, pl.ds(at, 256)] = nt(ones, (g * f_ref[pl.ds(at, 256), 0:hidden].astype(F32)).astype(BF))
        f_ref[pl.ds(at, 256), 0:hidden] = g.astype(BF)
        f_ref[pl.ds(at, 256), hidden : 2 * hidden] = tn(cot_all[:, pl.ds(at, 256)], a_ref[...]).astype(BF)
        return 0

    lax.fori_loop(0, width // 256, ffn_grads, 0)
    f_settle.start()

    for j in range(2):
        here = slice(j * part, (j + 1) * part)
        gn2 = gn_folds[j].total(gn_own[here, :])
        mid = mid_ref[here, :]
        r2 = lax.rsqrt(jnp.mean(mid * mid, axis=-1, keepdims=True) + EPS)
        hat2 = mid * r2
        scaled = gn2 * gain_ref[1:2, :]
        inner = jnp.mean(scaled * hat2, axis=-1, keepdims=True)
        gmid = cot_ref[here, :].astype(F32) + r2 * (scaled - hat2 * inner)
        gmid_ref[here, :] = gmid
        gmb_ref[pl.ds(t * rows + j * part, part), :] = gmid.astype(BF)
        gmb_spreads[j].start()
    for item in gn_folds:
        item.finish()

    def turn_keys(i, _):
        at = pl.multiple_of(i * SEG, SEG)
        turn_ref[:, pl.ds(at, SEG)] = k_ref[pl.ds(at, SEG), :].T
        return 0

    lax.fori_loop(0, blocks + back, turn_keys, 0)

    def mask_queries(i, _):
        at = pl.multiple_of(i * SEG, SEG)
        q = q_ref[pl.ds(at, SEG), :]
        for h in range(3):
            a_ref[pl.ds(at, SEG), h * cols : (h + 1) * cols] = jnp.where(head_mask(h, SEG, cols), q, jnp.zeros_like(q))
        return 0

    lax.fori_loop(0, blocks, mask_queries, 0)
    for item in gmb_spreads:
        item.forward()
    for item in gmb_spreads:
        item.wait()

    def context_grads(i, _):
        at = pl.multiple_of(i * SEG, SEG)
        low = nt(gmb_ref[pl.ds(at, SEG), :], wo_ref[...]).astype(BF)
        gct = low.astype(F32).T
        for h in range(3):
            gu_ref[pl.ds(at, SEG), h * cols : (h + 1) * cols] = jnp.where(
                head_mask(h, SEG, cols), low, jnp.zeros_like(low)
            )
            c = ct_ref[pl.ds(t * wide + h * HD, HD), pl.ds(at, SEG)].astype(F32)
            delta_ref[h : h + 1, pl.ds(at, SEG)] = jnp.sum(gct[h * HD : (h + 1) * HD] * c, axis=0, keepdims=True)
        return 0

    lax.fori_loop(0, blocks, context_grads, 0)
    go_ref[...] = nn(ct_ref[pl.ds(t * wide, wide), :], gmb_ref[...]).astype(BF).T
    o_settle.start()
    qm_ref, gm_ref = a_ref, gu_ref

    def piece(i, lo, hi, first):
        at, n = i * SEG, hi - lo
        keys = pl.ds(lo * SEG, n * SEG)
        values = pl.ds(ext + lo * SEG, n * SEG)
        for h in range(3):
            head = slice(h * cols, (h + 1) * cols)
            turned = slice(h * HD, (h + 1) * HD)
            qm, gm = qm_ref[at : at + SEG, head], gm_ref[at : at + SEG, head]
            s = nt(k_ref[keys, :], qm)
            g = nt(v_ref[keys, :], gm)
            logsum, delta = l_ref[h : h + 1, at : at + SEG], delta_ref[h : h + 1, at : at + SEG]
            for j in range(n):
                bias = block_bias(seg_ref, par_ref, dp * blocks + i, back + i - lo - j)
                part = slice(j * SEG, (j + 1) * SEG)
                x = s[part] * LOG2E
                if lo + j == i:
                    x = x + tri_ref[1]
                if lo + j == i + back:
                    x = x + tri_ref[0]
                p = jnp.exp2(x - (logsum - bias))
                e_ref[h, part, :] = p.astype(BF)
                xe_ref[WINDOW + j * SEG : WINDOW + (j + 1) * SEG, head] = (p * (g[part] - delta)).astype(BF)
            dv = nn(e_ref[h, 0 : n * SEG, :], gm)
            ds = xe_ref[WINDOW : WINDOW + n * SEG, head]
            dk = nn(ds, qm)
            dq = nn(turn_ref[turned, keys], ds)
            if first and h == 0:
                pool_ref[values, :] = dv
                pool_ref[keys, :] = dk
            else:
                pool_ref[values, :] += dv
                pool_ref[keys, :] += dk
            if lo == i:
                dqt_ref[turned, at : at + SEG] = dq
            else:
                dqt_ref[turned, at : at + SEG] += dq

    def outer(at, k, fold, with_query):
        gk = pool_ref[pl.ds(at, rows), 0:wide].astype(BF)
        gv = pool_ref[pl.ds(ext + at, rows), 0:wide].astype(BF)
        k_ref[pl.ds(at, rows), 0:wide] = gk
        v_ref[pl.ds(at, rows), 0:wide] = gv
        part = nt(gk, wk_ref[:, 0:wide]) + nt(gv, wv_ref[:, 0:wide])
        if with_query:
            part = part + nt(q_ref[pl.ds(at - WINDOW, rows), 0:wide], wq_ref[:, 0:wide])
        gn_own[...] = part
        if with_query:

            @pl.when((place < per_tree - 2) & (t ^ (3 - k) == 3))
            def _():
                far_back().wait_recv()
                gn_own[rows - lag :, :] += far_buf[1].astype(F32)

        for i in range(3):

            @pl.when(k == i)
            def _():
                fold.put(i, gn_own[...])
                fold.copy(i).start()

    piece(0, 0, 3, True)
    piece(0, 3, back, True)
    for i in range(1, blocks):
        piece(i, i, back, False)

    @pl.when(place >= 2)
    def _():
        gk = pool_ref[0:lag, 0:wide].astype(BF)
        gv = pool_ref[ext : ext + lag, 0:wide].astype(BF)
        far_buf[0] = (nt(gk, wk_ref[:, 0:wide]) + nt(gv, wv_ref[:, 0:wide])).astype(BF)
        far_back().start()

    k_ref[0:lag, 0:wide] = pool_ref[0:lag, 0:wide].astype(BF)
    v_ref[0:lag, 0:wide] = pool_ref[ext : ext + lag, 0:wide].astype(BF)

    def halo_outer(k, _):
        outer(lag + (t ^ (3 - k)) * rows, k, halo_fold, False)
        return 0

    lax.fori_loop(0, 4, halo_outer, 0)
    for i in range(blocks - 1, 1, -1):
        piece(i, back, back + i + 1, i == blocks - 1)

    for step in (2, 1, 3):
        f_settle.pass_on(step)
    for step in (2, 1, 3):
        o_settle.pass_on(step)
    for i in range(1, -1, -1):
        piece(i, back, back + i + 1, False)

    cot_all[3 * rows : 4 * rows, :] = halo_fold.total(gn_own[...]).astype(BF)

    @pl.when(place >= 1)
    def _():
        near_back().start()

    down_fold.copy(1).start()

    def turn_queries(i, _):
        at = pl.multiple_of(i * SEG, SEG)
        q_ref[pl.ds(at, SEG), 0:wide] = (dqt_ref[:, pl.ds(at, SEG)] * HD**-0.5).astype(BF).T
        return 0

    lax.fori_loop(0, blocks, turn_queries, 0)

    def own_outer(k, _):
        outer(WINDOW + (t ^ (3 - k)) * rows, k, gn1_fold, True)
        return 0

    lax.fori_loop(0, 4, own_outer, 0)
    grads = [
        tn(n1_ref[...], q_ref[:, 0:wide]),
        tn(xe_ref[0:WINDOW, :], k_ref[0:WINDOW, 0:wide]) + tn(n1_ref[...], k_ref[WINDOW:, 0:wide]),
        tn(xe_ref[0:WINDOW, :], v_ref[0:WINDOW, 0:wide]) + tn(n1_ref[...], v_ref[WINDOW:, 0:wide]),
    ]
    w_ref[0:width, 0 : 3 * wide] = jnp.concatenate([g.astype(BF) for g in grads], axis=1)
    a_settle.start()
    terms = sum(g * w[:, 0:wide].astype(F32) for g, w in zip(grads, (wq_ref, wk_ref, wv_ref)))
    first_row = lax.broadcasted_iota(jnp.int32, (8, width), 0) == 0
    gt_buf[0] = jnp.where(first_row, nt(ones[:, 0:wide], terms.astype(BF)), gt_buf[0])
    for i in range(3):
        gain_copy(i).start()
    out_ref[...] = (mid_ref[...] + down_fold.total(down_own[...])).astype(BF)
    total = gt_buf[0]
    for i in range(3):
        gain_copy(i).wait_recv()
        total = total + gt_buf[i + 1]
    gd_buf[0] = total
    for i in range(7):
        gain_over(i).start()
    gf = f_settle.total()
    gup_ref[...] = gf[:, 0:hidden]
    gdown_ref[...] = gf[:, hidden : 2 * hidden]
    gout_ref[...] = o_settle.total().T
    for step in (2, 1, 3):
        a_settle.pass_on(step)

    gn1 = gn1_fold.total(gn_own[...])

    @pl.when(place < per_tree - 1)
    def _():
        near_back().wait_recv()
        gn_own[...] = near_buf[...].astype(F32)

    @pl.when(place == per_tree - 1)
    def _():
        gn_own[...] = jnp.zeros((rows, width), F32)

    gn1 = gn1 + gn_own[...]
    x = x_ref[...].astype(F32)
    r1 = lax.rsqrt(jnp.mean(x * x, axis=-1, keepdims=True) + EPS)
    hat1 = x * r1
    scaled = gn1 * gain_ref[0:1, :]
    inner = jnp.mean(scaled * hat1, axis=-1, keepdims=True)
    ing_ref[...] = (gmid_ref[...] + r1 * (scaled - hat1 * inner)).astype(BF)

    total = gd_buf[0]
    for i in range(7):
        gain_over(i).wait_recv()
        total = total + gd_buf[i + 1]
    total = pltpu.roll(total, lax.rem(8 - dp, 8) * deep, 1)
    gg1_ref[...] = total[0:1, 0:deep] / g1_ref[...].astype(F32)
    gg2_ref[...] = total[1:2, 0:deep] / g2_ref[...].astype(F32)
    ga = a_settle.total()
    for j, ref in enumerate((gq_out, gk_out, gv_out)):
        ref[...] = ga[:, j * wide : (j + 1) * wide]
    for i in range(3):
        gain_copy(i).wait_send()
    for i in range(7):
        gain_over(i).wait_send()
    for item in (down_fold, halo_fold, gn1_fold, *gmb_spreads, f_settle, o_settle, a_settle):
        item.finish()

    @pl.when(place >= 1)
    def _():
        near_back().wait_send()

    @pl.when(place >= 2)
    def _():
        far_back().wait_send()


def fast_shards(
    layer_input, cotangent, segments, parents, norm1_gain, w_query, w_key, w_value, w_out, norm2_gain, w_up, w_down,
):
    rows, width = layer_input.shape
    token = 4 * rows
    ext = token + WINDOW
    wide = width // 4
    cols = 256 * pl.cdiv(wide, 256)
    deep, hidden = w_up.shape
    blocks = token // SEG
    span = WINDOW + SEG
    shape = jax.ShapeDtypeStruct
    vmem = pl.BlockSpec(memory_space=pltpu.VMEM)
    smem = pl.BlockSpec(memory_space=pltpu.SMEM)
    copies = 7 * 3 + 4 * 8 + 3 + 3 * blocks + 5 * 3 + 3 * 7 + 2 + 3 + 7
    results = pl.pallas_call(
        kernel,
        out_shape=[
            shape((rows, width), BF),
            shape((rows, width), BF),
            shape((1, deep), F32),
            shape((deep, wide), F32),
            shape((deep, wide), F32),
            shape((deep, wide), F32),
            shape((wide, deep), F32),
            shape((1, deep), F32),
            shape((deep, hidden), F32),
            shape((deep, hidden), F32),
        ],
        in_specs=[smem, smem] + [vmem] * 10,
        out_specs=[vmem] * 10,
        scratch_shapes=[
            pltpu.VMEM((ext, width), BF),
            pltpu.VMEM((token, width), BF),
            pltpu.VMEM((token, width), BF),
            pltpu.VMEM((rows, width), F32),
            pltpu.VMEM((rows, width), F32),
            pltpu.VMEM((8 * (deep + 16), width), BF),
            pltpu.VMEM((width, 2 * hidden), BF),
            pltpu.VMEM((token, width), BF),
            pltpu.VMEM((width, width), BF),
            pltpu.VMEM((cols, width), BF),
            pltpu.VMEM((width, cols), BF),
            pltpu.VMEM((width, cols), BF),
            pltpu.VMEM((width, cols), BF),
            pltpu.VMEM((token, cols), BF),
            pltpu.VMEM((ext, cols), BF),
            pltpu.VMEM((ext, cols), BF),
            pltpu.VMEM((cols, ext), BF),
            pltpu.VMEM((width, token), BF),
            pltpu.VMEM((8, token), F32),
            pltpu.VMEM((8, width), F32),
            pltpu.VMEM((8, token), F32),
            pltpu.VMEM((2 * ext, SEG), F32),
            pltpu.VMEM((3, span, SEG), BF),
            pltpu.VMEM((2, SEG, SEG), F32),
            pltpu.VMEM((token, hidden), BF),
            pltpu.VMEM((token, hidden), BF),
            pltpu.VMEM((rows, width), F32),
            pltpu.VMEM((rows, width), F32),
            pltpu.VMEM((6, rows, width), BF),
            pltpu.VMEM((6, rows, width), BF),
            pltpu.VMEM((token, width), BF),
            pltpu.VMEM((4, deep, 2 * hidden), BF),
            pltpu.VMEM((3, deep, 2 * hidden), BF),
            pltpu.VMEM((width, wide), BF),
            pltpu.VMEM((4, deep, wide), BF),
            pltpu.VMEM((3, deep, wide), BF),
            pltpu.VMEM((4, deep, 128 * pl.cdiv(3 * wide, 128)), BF),
            pltpu.VMEM((3, deep, 128 * pl.cdiv(3 * wide, 128)), BF),
            pltpu.VMEM((wide, token), F32),
            pltpu.VMEM((rows, width), BF),
            pltpu.VMEM((2, WINDOW - token, width), BF),
            pltpu.VMEM((4, 8, width), F32),
            pltpu.VMEM((8, 8, width), F32),
            pltpu.SemaphoreType.DMA((copies,)),
            pltpu.SemaphoreType.DMA((copies,)),
        ],
        compiler_params=pltpu.CompilerParams(
            collective_id=0, has_side_effects=True, vmem_limit_bytes=64 << 20
        ),
    )(
        segments, parents, layer_input, cotangent, norm1_gain[None], w_query, w_key, w_value, w_out,
        norm2_gain[None], w_up, w_down.T,
    )
    results = list(hand_over(results))
    results[2], results[7], results[9] = results[2][0], results[7][0], results[9].T
    return tuple(results)


def hand_over(arrays):
    def body(*refs):
        for source, target in zip(refs[: len(arrays)], refs[len(arrays) :]):
            target[...] = source[...]

    vmem = pl.BlockSpec(memory_space=pltpu.VMEM)
    return pl.pallas_call(
        body,
        out_shape=[jax.ShapeDtypeStruct(a.shape, a.dtype) for a in arrays],
        in_specs=[vmem] * len(arrays),
        out_specs=[vmem] * len(arrays),
    )(*arrays)


epsilon = 1e-06
masked_score = -1e30


def from_behind(block, axis, distance):
    devices = range(lax.axis_size(axis))
    route = [(i - distance, i) for i in devices if i - distance in devices]
    return lax.ppermute(block, axis, route)


def split_up(x, dim, peers):
    dims = x.shape
    tiles = x.reshape(*dims[:dim], peers, dims[dim] // peers, *dims[dim + 1 :])
    return jnp.moveaxis(tiles, dim, 0)


def sum_at_owner(x, axis, dim):
    tiles = split_up(x, dim, lax.axis_size(axis))
    arrived = lax.all_to_all(tiles, axis, split_axis=0, concat_axis=0, tiled=True)
    return arrived.astype(jnp.float32).sum(axis=0)


def side_by_side(arrays, axis, dim, along):
    widths = [math.prod(a.shape[along:]) for a in arrays]
    both = jnp.concatenate(
        [a.reshape(*a.shape[:along], w) for a, w in zip(arrays, widths)], axis=along
    )
    whole = sum_at_owner(both, axis, dim)
    tiles = jnp.split(whole, [sum(widths[:k]) for k in range(1, len(widths))], axis=along)
    return tuple((b.reshape(*whole.shape[:along], *a.shape[along:]) for a, b in zip(arrays, tiles)))


def gelu_exact(values):
    return jax.nn.gelu(values, approximate=False)


def row_scale(values):
    return lax.rsqrt(jnp.mean(values * values, axis=-1, keepdims=True) + epsilon)


def norm_backward(incoming, normal_hat, row_factor, gain):
    scaled = incoming * gain
    inner = jnp.mean(scaled * normal_hat, axis=-1, keepdims=True)
    return (row_factor * (scaled - normal_hat * inner), jnp.sum(incoming * normal_hat, axis=0))


def parent_of(seg_ids, parents):
    seg_table = jnp.arange(parents.shape[0], dtype=jnp.int32)
    hits = seg_ids[:, None] == seg_table[None, :]
    return jnp.sum(jnp.where(hits, parents[None, :], 0), axis=1)


def shards(
    layer_input,
    cotangent,
    segments,
    parents,
    norm1_gain,
    w_query,
    w_key,
    w_value,
    w_out,
    norm2_gain,
    w_up,
    w_down,
):
    gain_one, full_query, full_key, full_value, full_out, gain_two, full_up, full_down = (
        lax.all_gather(norm1_gain, "dp", axis=0, tiled=True),
        lax.all_gather(w_query, "dp", axis=0, tiled=True),
        lax.all_gather(w_key, "dp", axis=0, tiled=True),
        lax.all_gather(w_value, "dp", axis=0, tiled=True),
        lax.all_gather(w_out, "dp", axis=1, tiled=True),
        lax.all_gather(norm2_gain, "dp", axis=0, tiled=True),
        lax.all_gather(w_up, "dp", axis=0, tiled=True),
        lax.all_gather(w_down, "dp", axis=1, tiled=True),
    )
    gain_one = gain_one.astype(jnp.float32)
    gain_two = gain_two.astype(jnp.float32)
    row_count = layer_input.shape[0]
    token_count = row_count * lax.axis_size("tensor")
    position = lax.axis_index("dp") * token_count
    head_width = full_query.shape[1]
    head_count = head_width // HD
    scaling = HD ** (-0.5)
    block_rows = min(640, token_count)
    block_count = token_count // block_rows
    span = WINDOW + block_rows
    hop_count = (WINDOW + token_count - 1) // token_count
    inputs = layer_input.astype(jnp.float32)
    factor_one = row_scale(inputs)
    hat_one = inputs * factor_one
    normed = (hat_one * gain_one).astype(jnp.bfloat16)
    normed_all = lax.all_gather(normed, "tensor", axis=0, tiled=True)
    queries = jnp.dot(normed_all, full_query, preferred_element_type=jnp.float32).astype(
        jnp.bfloat16
    )
    keys_own = jnp.dot(normed_all, full_key, preferred_element_type=jnp.float32).astype(
        jnp.bfloat16
    )
    values_own = jnp.dot(normed_all, full_value, preferred_element_type=jnp.float32).astype(
        jnp.bfloat16
    )
    pair_own = jnp.concatenate([keys_own, values_own], axis=1)
    halo_parts = []
    for distance in range(1, hop_count + 1):
        length = min(token_count, WINDOW - (distance - 1) * token_count)
        piece = pair_own[token_count - length :]
        moved = from_behind(piece, "dp", distance)
        halo_parts.append(moved)
    pair_all = jnp.concatenate(halo_parts[::-1] + [pair_own], axis=0)
    seg_padded = jnp.concatenate([jnp.full((WINDOW,), -1, jnp.int32), segments])
    seg_keys = lax.dynamic_slice_in_dim(seg_padded, position, WINDOW + token_count, 0)
    seg_query = seg_keys[WINDOW:]
    parent_one = parent_of(seg_query, parents)
    parent_two = parent_of(parent_one, parents)
    query_spots = jnp.arange(block_rows, dtype=jnp.int32)
    key_spots = jnp.arange(span, dtype=jnp.int32)

    def scores_of(offset):
        query_block = lax.dynamic_slice_in_dim(queries, offset, block_rows, 0).reshape(
            block_rows, head_count, HD
        )
        pair_block = lax.dynamic_slice_in_dim(pair_all, offset, span, 0)
        key_block = pair_block[:, :head_width].reshape(span, head_count, HD)
        value_block = pair_block[:, head_width:].reshape(span, head_count, HD)
        own_seg = lax.dynamic_slice_in_dim(seg_query, offset, block_rows, 0)
        up_one = lax.dynamic_slice_in_dim(parent_one, offset, block_rows, 0)
        up_two = lax.dynamic_slice_in_dim(parent_two, offset, block_rows, 0)
        near_seg = lax.dynamic_slice_in_dim(seg_keys, offset, span, 0)
        gap = WINDOW + query_spots[:, None] - key_spots[None, :]
        same_path = (
            (near_seg[None, :] == own_seg[:, None])
            | (near_seg[None, :] == up_one[:, None])
            | (near_seg[None, :] == up_two[:, None])
        )
        allowed = (gap >= 0) & (gap < WINDOW) & same_path
        raw = (
            jnp.einsum("qhd,khd->hqk", query_block, key_block, preferred_element_type=jnp.float32)
            * scaling
        )
        return (jnp.where(allowed[None], raw, masked_score), query_block, key_block, value_block)

    def forward_block(block_index):
        scores, query_block, key_block, value_block = scores_of(block_index * block_rows)
        row_max = jnp.max(scores, axis=-1, keepdims=True)
        exponent = jnp.exp(scores - row_max)
        denominator = jnp.sum(exponent, axis=-1, keepdims=True)
        weights = (exponent / denominator).astype(jnp.bfloat16)
        mixed = jnp.einsum("hqk,khd->qhd", weights, value_block, preferred_element_type=jnp.float32)
        return (
            mixed.reshape(block_rows, head_width).astype(jnp.bfloat16),
            (row_max + jnp.log(denominator))[..., 0],
        )

    context_blocks, logsum_blocks = lax.map(forward_block, jnp.arange(block_count, dtype=jnp.int32))
    context = context_blocks.reshape(token_count, head_width)
    middle = inputs + lax.psum_scatter(
        jnp.dot(context, full_out, preferred_element_type=jnp.float32).astype(jnp.bfloat16),
        "tensor",
        scatter_dimension=0,
        tiled=True,
    ).astype(jnp.float32)
    factor_two = row_scale(middle)
    hat_two = middle * factor_two
    normed_two = (hat_two * gain_two).astype(jnp.bfloat16)
    normed_two_all = lax.all_gather(normed_two, "tensor", axis=0, tiled=True)
    upper = jnp.dot(normed_two_all, full_up, preferred_element_type=jnp.float32)
    active = gelu_exact(upper).astype(jnp.bfloat16)
    result = middle + lax.psum_scatter(
        jnp.dot(active, full_down, preferred_element_type=jnp.float32).astype(jnp.bfloat16),
        "tensor",
        scatter_dimension=0,
        tiled=True,
    ).astype(jnp.float32)
    incoming = cotangent.astype(jnp.float32)
    incoming_all = lax.all_gather(cotangent, "tensor", axis=0, tiled=True)
    grad_down = jnp.einsum("tf,td->fd", active, incoming_all, preferred_element_type=jnp.float32)
    grad_active = jnp.einsum(
        "td,fd->tf", incoming_all, full_down, preferred_element_type=jnp.float32
    )
    unused_value, gelu_pull = jax.vjp(gelu_exact, upper)
    grad_upper = gelu_pull(grad_active)[0].astype(jnp.bfloat16)
    grad_up = jnp.einsum(
        "tc,tf->cf", normed_two_all, grad_upper, preferred_element_type=jnp.float32
    )
    grad_normed_two = lax.psum_scatter(
        jnp.einsum("tf,cf->tc", grad_upper, full_up, preferred_element_type=jnp.float32).astype(
            jnp.bfloat16
        ),
        "tensor",
        scatter_dimension=0,
        tiled=True,
    ).astype(jnp.float32)
    through_two, gain_two_part = norm_backward(grad_normed_two, hat_two, factor_two, gain_two)
    grad_middle = incoming + through_two
    grad_middle_all = lax.all_gather(grad_middle.astype(jnp.bfloat16), "tensor", axis=0, tiled=True)
    grad_out = jnp.einsum("tc,td->cd", context, grad_middle_all, preferred_element_type=jnp.float32)
    grad_context = jnp.einsum(
        "td,cd->tc", grad_middle_all, full_out, preferred_element_type=jnp.float32
    ).astype(jnp.bfloat16)

    def backward_block(block_index, carry):
        grad_queries, grad_pairs = carry
        offset = block_index * block_rows
        scores, query_block, key_block, value_block = scores_of(offset)
        logsum = lax.dynamic_index_in_dim(logsum_blocks, block_index, 0, keepdims=False)
        probs = jnp.exp(scores - logsum[..., None])
        grad_rows = lax.dynamic_slice_in_dim(grad_context, offset, block_rows, 0).reshape(
            block_rows, head_count, HD
        )
        grad_probs = jnp.einsum(
            "qhd,khd->hqk", grad_rows, value_block, preferred_element_type=jnp.float32
        )
        inner = jnp.sum(probs * grad_probs, axis=-1, keepdims=True)
        grad_scores = (probs * (grad_probs - inner)).astype(jnp.bfloat16)
        grad_query_block = (
            jnp.einsum("hqk,khd->qhd", grad_scores, key_block, preferred_element_type=jnp.float32)
            * scaling
        )
        grad_key_block = (
            jnp.einsum("hqk,qhd->khd", grad_scores, query_block, preferred_element_type=jnp.float32)
            * scaling
        )
        grad_value_block = jnp.einsum(
            "hqk,qhd->khd",
            probs.astype(jnp.bfloat16),
            grad_rows,
            preferred_element_type=jnp.float32,
        )
        grad_queries = lax.dynamic_update_slice_in_dim(
            grad_queries, grad_query_block.reshape(block_rows, head_width), offset, 0
        )
        update = jnp.concatenate(
            [grad_key_block.reshape(span, head_width), grad_value_block.reshape(span, head_width)],
            axis=1,
        )
        current = lax.dynamic_slice_in_dim(grad_pairs, offset, span, 0)
        grad_pairs = lax.dynamic_update_slice_in_dim(grad_pairs, current + update, offset, 0)
        return (grad_queries, grad_pairs)

    start_carry = (
        jnp.zeros((token_count, head_width), jnp.float32),
        jnp.zeros((WINDOW + token_count, 2 * head_width), jnp.float32),
    )
    grad_queries, grad_pairs = lax.fori_loop(0, block_count, backward_block, start_carry)
    grad_own = grad_pairs[WINDOW:]
    for distance in range(1, hop_count + 1):
        length = min(token_count, WINDOW - (distance - 1) * token_count)
        first_row = WINDOW - (distance - 1) * token_count - length
        piece = grad_pairs[first_row : first_row + length]
        returned = from_behind(piece.astype(jnp.bfloat16), "dp", -distance).astype(piece.dtype)
        grad_own = grad_own + jnp.pad(returned, ((token_count - length, 0), (0, 0)))
    grad_keys = grad_own[:, :head_width].astype(jnp.bfloat16)
    grad_values = grad_own[:, head_width:].astype(jnp.bfloat16)
    grad_queries_low = grad_queries.astype(jnp.bfloat16)
    grad_query = jnp.einsum(
        "tc,tq->cq", normed_all, grad_queries_low, preferred_element_type=jnp.float32
    )
    grad_key = jnp.einsum("tc,tq->cq", normed_all, grad_keys, preferred_element_type=jnp.float32)
    grad_value = jnp.einsum(
        "tc,tq->cq", normed_all, grad_values, preferred_element_type=jnp.float32
    )
    part_query = jnp.einsum(
        "tq,cq->tc", grad_queries_low, full_query, preferred_element_type=jnp.float32
    )
    part_key = jnp.einsum("tq,cq->tc", grad_keys, full_key, preferred_element_type=jnp.float32)
    part_value = jnp.einsum(
        "tq,cq->tc", grad_values, full_value, preferred_element_type=jnp.float32
    )
    grad_normed = lax.psum_scatter(
        (part_query + part_key + part_value).astype(jnp.bfloat16),
        "tensor",
        scatter_dimension=0,
        tiled=True,
    ).astype(jnp.float32)
    through_one, gain_one_part = norm_backward(grad_normed, hat_one, factor_one, gain_one)
    grad_inputs = grad_middle + through_one
    gain_one_sum, gain_two_sum = lax.psum((gain_one_part, gain_two_part), "tensor")
    summed = (
        *side_by_side(
            (
                gain_one_sum.astype(jnp.bfloat16),
                grad_query.astype(jnp.bfloat16),
                grad_key.astype(jnp.bfloat16),
                grad_value.astype(jnp.bfloat16),
            ),
            "dp",
            0,
            1,
        ),
        sum_at_owner(grad_out.astype(jnp.bfloat16), "dp", 1),
        *side_by_side(
            (gain_two_sum.astype(jnp.bfloat16), grad_up.astype(jnp.bfloat16)), "dp", 0, 1
        ),
        sum_at_owner(grad_down.astype(jnp.bfloat16), "dp", 1),
    )
    return (
        result.astype(jnp.bfloat16),
        grad_inputs.astype(jnp.bfloat16),
        summed[0],
        summed[1],
        summed[2],
        summed[3],
        summed[4],
        summed[5],
        summed[6],
        summed[7],
    )


def solution(mesh):
    fast = mesh.shape["dp"] == 8 and mesh.shape["tensor"] == 4
    return jax.shard_map(
        fast_shards if fast else shards,
        mesh=mesh,
        in_specs=(
            P(("dp", "tensor"), None),
            P(("dp", "tensor"), None),
            P(),
            P(),
            P("dp"),
            P("dp", "tensor"),
            P("dp", "tensor"),
            P("dp", "tensor"),
            P("tensor", "dp"),
            P("dp"),
            P("dp", "tensor"),
            P("tensor", "dp"),
        ),
        out_specs=(
            P(("dp", "tensor"), None),
            P(("dp", "tensor"), None),
            P("dp"),
            P("dp", "tensor"),
            P("dp", "tensor"),
            P("dp", "tensor"),
            P("tensor", "dp"),
            P("dp"),
            P("dp", "tensor"),
            P("tensor", "dp"),
        ),
        check_vma=False,
    )
```

```python
import functools
import math

import jax
import jax.numpy as jnp
from jax import lax
from jax.experimental import pallas as pl
from jax.experimental.pallas import tpu as pltpu
from jax.sharding import PartitionSpec as P

MESH = pl.DeviceIdType.MESH
BF = jnp.bfloat16
F32 = jnp.float32
HD = 64
WINDOW = 1536
SEG = 256
TREE = 5120
LOG2E = 1.4426950408889634
NEG = -1e30
EPS = 1e-6


def nt(a, b):
    return lax.dot_general(a, b, (((1,), (1,)), ((), ())), preferred_element_type=F32)


def nn(a, b):
    return jnp.dot(a, b, preferred_element_type=F32)


def tn(a, b):
    return lax.dot_general(a, b, (((0,), (0,)), ((), ())), preferred_element_type=F32)


class Links:
    def __init__(self, send, recv):
        self.send, self.recv, self.used = send, recv, 0

    def take(self, count):
        base = self.used
        self.used += count
        return base

    def copy(self, src, dst, send, recv, device):
        return pltpu.make_async_remote_copy(
            src_ref=src,
            dst_ref=dst,
            send_sem=self.send.at[send],
            recv_sem=self.recv.at[recv],
            device_id=device,
            device_id_type=MESH,
        )


class Spread:
    def __init__(self, links, base, dp, t, part):
        self.links, self.base, self.dp, self.t, self.part = links, base, dp, t, part

    def leave(self, i):
        flip, what = ((1, 0), (2, 0), (1, 2))[i]
        ref = self.part(self.t ^ what)
        return self.links.copy(ref, ref, self.base + i, self.base + i, (self.dp, self.t ^ flip))

    def come(self, i):
        flip, what = ((1, 1), (2, 2), (1, 3))[i]
        ref = self.part(self.t ^ what)
        return self.links.copy(ref, ref, self.base + i, self.base + i, (self.dp, self.t ^ flip))

    def start(self):
        self.leave(1).start()
        self.leave(0).start()

    def forward(self):
        self.come(1).wait_recv()
        self.leave(2).start()

    def wait(self):
        self.come(0).wait_recv()
        self.come(2).wait_recv()

    def finish(self):
        for i in range(3):
            self.leave(i).wait_send()


class Gather:
    def __init__(self, links, base, dp, t, slot):
        self.links, self.base, self.dp, self.t, self.slot = links, base, dp, t, slot
        self.z, self.y = dp // 2, dp % 2

    def at(self, step):
        z = lax.rem(self.z + step, 4)
        return z, z * 2 + self.y

    def along(self, step):
        z, peer = self.at(step)
        return self.links.copy(self.slot(self.dp), self.slot(self.dp), self.base + step - 1, self.base + self.z, (peer, self.t))

    def came(self, step):
        z, peer = self.at(step)
        return self.links.copy(self.slot(peer), self.slot(peer), self.base + step - 1, self.base + z, (peer, self.t))

    def across(self, step):
        z, peer = self.at(step)
        return self.links.copy(self.slot(peer), self.slot(peer), self.base + 4 + step, self.base + 4 + z, (self.dp ^ 1, self.t))

    def crossed(self, step):
        z, peer = self.at(step)
        other = z * 2 + (1 - self.y)
        return self.links.copy(self.slot(other), self.slot(other), self.base + 4 + step, self.base + 4 + z, (self.dp ^ 1, self.t))

    def start(self):
        self.across(0).start()
        for step in (1, 3, 2):
            self.along(step).start()

    def forward(self, step):
        self.came(step).wait_recv()
        self.across(step).start()

    def wait(self):
        for step in range(4):
            self.crossed(step).wait_recv()

    def finish(self):
        for step in range(1, 4):
            self.along(step).wait_send()
        for step in range(4):
            self.across(step).wait_send()


def head_mask(h, rows, width):
    lane = lax.broadcasted_iota(jnp.int32, (rows, width), 1)
    return (lane >= h * HD) & (lane < (h + 1) * HD)


def block_bias(seg_ref, par_ref, block, back):
    own = seg_ref[block * SEG]
    one = par_ref[own]
    two = par_ref[one]
    far = block - back
    near = seg_ref[jnp.maximum(far, 0) * SEG]
    ok = ((near == own) | (near == one) | (near == two)) & (far >= 0)
    return jnp.where(ok, jnp.float32(0.0), jnp.float32(NEG))


class Fold:
    def __init__(self, links, base, dp, t, out, into):
        self.links, self.base, self.dp, self.t, self.out, self.into = links, base, dp, t, out, into

    def copy(self, i):
        flip = (1, 2, 1)[i]
        return self.links.copy(
            self.out(i), self.into(i), self.base + i, self.base + i, (self.dp, self.t ^ flip)
        )

    def put(self, i, value):
        if i == 1:
            self.copy(0).wait_recv()
            value = value + self.into(0)[...].astype(F32)
        self.out(i)[...] = value.astype(BF)

    def total(self, value):
        self.copy(1).wait_recv()
        self.copy(2).wait_recv()
        return value + self.into(2)[...].astype(F32) + self.into(1)[...].astype(F32)

    def finish(self):
        for i in range(3):
            self.copy(i).wait_send()


class Settle:
    def __init__(self, links, base, dp, t, slots, deep, from_y, from_z):
        self.links, self.base, self.dp, self.t = links, base, dp, t
        self.slots, self.deep, self.from_y, self.from_z = slots, deep, from_y, from_z
        self.z, self.y = dp // 2, lax.rem(dp, 2)

    def rows(self, z, y):
        return pl.ds(pl.multiple_of((z * 2 + y) * self.deep, self.deep), self.deep)

    def across(self, step):
        z = lax.rem(self.z + step, 4)
        return self.links.copy(
            self.slots.at[self.rows(z, 1 - self.y)],
            self.from_y.at[step],
            self.base + step,
            self.base + step,
            (self.dp ^ 1, self.t),
        )

    def along(self, step):
        z = lax.rem(self.z + step, 4)
        return self.links.copy(
            self.slots.at[self.rows(z, self.y)],
            self.from_z.at[step - 1],
            self.base + 3 + step,
            self.base + 3 + step,
            (z * 2 + self.y, self.t),
        )

    def start(self):
        for step in (2, 1, 3, 0):
            self.across(step).start()

    def pass_on(self, step):
        self.across(step).wait_recv()
        z = lax.rem(self.z + step, 4)
        at = self.rows(z, self.y)
        self.slots[at, :] = (self.slots[at, :].astype(F32) + self.from_y[step].astype(F32)).astype(BF)
        self.along(step).start()

    def total(self):
        self.across(0).wait_recv()
        value = self.slots[self.rows(self.z, self.y), :].astype(F32) + self.from_y[0].astype(F32)
        for step in (1, 2, 3):
            self.along(step).wait_recv()
            value = value + self.from_z[step - 1].astype(F32)
        return value

    def finish(self):
        for step in range(4):
            self.across(step).wait_send()
        for step in (1, 2, 3):
            self.along(step).wait_send()


def kernel(
    seg_ref, par_ref, x_ref, cot_ref, g1_ref, wq_in, wk_in, wv_in, wo_in, g2_ref, wu_in, wd_in,
    out_ref, ing_ref, gg1_ref, gq_out, gk_out, gv_out, gout_ref, gg2_ref, gup_ref, gdown_ref,
    xe_ref, n1_ref, n2_ref, mid_ref, gmid_ref, w_ref, f_ref, cot_all, wout_ref, wo_ref, wq_ref, wk_ref, wv_ref,
    q_ref, k_ref, v_ref, turn_ref, ct_ref, l_ref, gain_ref, delta_ref, pool_ref, e_ref, tri_ref,
    a_ref, gu_ref, down_own, gn_own, down_buf, gn_buf, gmb_ref,
    gfy_ref, gfz_ref, go_ref, goy_ref, goz_ref, gay_ref, gaz_ref, dqt_ref, near_buf, far_buf, gt_buf, gd_buf, send, recv,
):
    dp, t = lax.axis_index("dp"), lax.axis_index("tensor")
    rows, width = x_ref.shape
    token = 4 * rows
    ext = token + WINDOW
    blocks = token // SEG
    back = WINDOW // SEG
    lag = WINDOW - token
    per_tree = TREE // token
    place = lax.rem(dp, per_tree)
    wide = width // 4
    cols = q_ref.shape[1]
    deep = wu_in.shape[0]
    hidden = wu_in.shape[1]
    links = Links(send, recv)
    spread = lambda part: Spread(links, links.take(3), dp, t, part)
    x_spread = spread(lambda p: xe_ref.at[pl.ds(WINDOW + p * rows, rows)])
    part = rows // 2
    halo_half = lambda p, j: xe_ref.at[pl.ds(lag + p * rows + j * part, part)]
    halo_spreads = [spread(lambda p, j=j: halo_half(p, j)) for j in range(2)]
    cot_spread = spread(lambda p: cot_all.at[pl.ds(p * rows, rows)])
    wout_spread = spread(lambda p: wout_ref.at[pl.ds(p * wide, wide)])
    gmb_spreads = [spread(lambda p, j=j: gmb_ref.at[pl.ds(p * rows + j * part, part)]) for j in range(2)]
    slot = deep + 16
    a_slot = lambda s: pl.ds(pl.multiple_of(s * slot, 16), slot)
    half = width // 2
    a_gathers = [
        Gather(links, links.take(8), dp, t, lambda s, j=j: w_ref.at[a_slot(s), pl.ds(j * half, half)]) for j in range(2)
    ]
    f_slot = lambda s: pl.ds(pl.multiple_of(s * deep, deep), deep)
    u_gather = Gather(links, links.take(8), dp, t, lambda s: f_ref.at[f_slot(s), pl.ds(0, hidden)])
    d_gather = Gather(links, links.take(8), dp, t, lambda s: f_ref.at[f_slot(s), pl.ds(hidden, hidden)])
    h1 = links.take(2)
    h2 = links.take(1)
    halo_copy = lambda j: links.copy(
        x_ref.at[pl.ds(j * part, part)], halo_half(t, j), h1 + j, h1 + j, (lax.rem(dp + 1, 8), t)
    )
    far_copy = lambda: links.copy(
        xe_ref.at[pl.ds(WINDOW + token - lag, lag)], xe_ref.at[pl.ds(0, lag)], h2, h2, (lax.rem(dp + 2, 8), t)
    )
    c_base = links.take(3 * blocks)

    def c_spread(i):
        at = pl.multiple_of(i * SEG, SEG)
        return Spread(links, c_base + 3 * i, dp, t, lambda p: ct_ref.at[pl.ds(p * wide, wide), pl.ds(at, SEG)])

    down_fold = Fold(links, links.take(3), dp, t, lambda i: down_buf.at[i], lambda i: down_buf.at[3 + i])
    gn_folds = [
        Fold(
            links,
            links.take(3),
            dp,
            t,
            lambda i, j=j: gn_buf.at[i, pl.ds(j * part, part)],
            lambda i, j=j: gn_buf.at[3 + i, pl.ds(j * part, part)],
        )
        for j in range(2)
    ]
    gn1_fold = Fold(links, links.take(3), dp, t, lambda i: gn_buf.at[i], lambda i: gn_buf.at[3 + i])
    halo_fold = Fold(
        links,
        links.take(3),
        dp,
        t,
        lambda i: cot_all.at[pl.ds(i * rows, rows)],
        lambda i: n2_ref.at[pl.ds(i * rows, rows)],
    )
    f_settles = [
        Settle(
            links,
            links.take(7),
            dp,
            t,
            f_ref.at[:, pl.ds(j * hidden, hidden)],
            deep,
            gfy_ref.at[:, :, pl.ds(j * hidden, hidden)],
            gfz_ref.at[:, :, pl.ds(j * hidden, hidden)],
        )
        for j in range(2)
    ]
    o_settle = Settle(links, links.take(7), dp, t, go_ref, deep, goy_ref, goz_ref)
    a_settles = [
        Settle(
            links,
            links.take(7),
            dp,
            t,
            w_ref.at[:, pl.ds(a, n)],
            deep,
            gay_ref.at[:, :, pl.ds(a, n)],
            gaz_ref.at[:, :, pl.ds(a, n)],
        )
        for a, n in ((0, 2 * wide), (2 * wide, gay_ref.shape[2] - 2 * wide))
    ]
    b1 = links.take(1)
    b2 = links.take(1)
    near_back = lambda: links.copy(cot_all.at[pl.ds(3 * rows, rows)], near_buf, b1, b1, (lax.rem(dp + 7, 8), t))
    far_back = lambda: links.copy(far_buf.at[0], far_buf.at[1], b2, b2, (lax.rem(dp + 6, 8), t))
    gb = links.take(3)
    gd = links.take(7)

    def gain_copy(i):
        return links.copy(gt_buf.at[0], gt_buf.at[i + 1], gb + i, gb + i, (dp, t ^ (i + 1)))

    def gain_over(i):
        return links.copy(gd_buf.at[0], gd_buf.at[i + 1], gd + i, gd + i, (lax.rem(dp + i + 1, 8), t))

    barrier = pltpu.get_barrier_semaphore()
    for step in range(1, 8):
        pl.semaphore_signal(barrier, inc=1, device_id=(lax.rem(dp + step, 8), t), device_id_type=MESH)
    for flip in (1, 2, 3):
        pl.semaphore_signal(barrier, inc=1, device_id=(dp, t ^ flip), device_id_type=MESH)

    base = pl.multiple_of(dp * slot, 16)
    w_ref[pl.ds(base, deep), :] = jnp.concatenate(
        [wq_in[...], wk_in[...], wv_in[...], wo_in[...].astype(F32).T.astype(BF)], axis=1
    )
    lane = lax.broadcasted_iota(jnp.int32, (deep, width), 1)
    line = lax.broadcasted_iota(jnp.int32, (deep, width), 0)
    put = jnp.where(lane == line + dp * deep, 1.0, 0.0).astype(BF)
    two = jnp.concatenate([g1_ref[...], g2_ref[...], jnp.zeros((14, deep), BF)], axis=0)
    w_ref[pl.ds(base + deep, 16), :] = nn(two, put).astype(BF)
    xe_ref[pl.ds(WINDOW + t * rows, rows), :] = x_ref[...]
    pl.semaphore_wait(barrier, 10)
    a_gathers[0].start()
    x_spread.start()

    @pl.when(place < per_tree - 1)
    def _():
        halo_copy(0).start()

    f_ref[f_slot(dp), 0:hidden] = wu_in[...]
    f_ref[f_slot(dp), hidden : 2 * hidden] = wd_in[...]
    cot_all[pl.ds(t * rows, rows), :] = cot_ref[...]

    @pl.when(place < 1)
    def _():
        xe_ref[pl.ds(lag, token), :] = jnp.zeros((token, width), BF)

    @pl.when(place < 2)
    def _():
        xe_ref[pl.ds(0, lag), :] = jnp.zeros((lag, width), BF)

    row = lax.broadcasted_iota(jnp.int32, (SEG, SEG), 0)
    col = lax.broadcasted_iota(jnp.int32, (SEG, SEG), 1)
    tri_ref[0] = jnp.where(row <= col, 0.0, NEG)
    tri_ref[1] = jnp.where(row > col, 0.0, NEG)
    for step in (1, 3, 2):
        a_gathers[0].forward(step)
    a_gathers[1].start()

    @pl.when(place < per_tree - 1)
    def _():
        halo_copy(0).wait_send()
        halo_copy(1).start()

    @pl.when(place >= 1)
    def _():
        halo_copy(0).wait_recv()
        halo_spreads[0].start()

    x_spread.forward()
    for step in (1, 3, 2):
        a_gathers[1].forward(step)

    @pl.when(place >= 1)
    def _():
        halo_copy(1).wait_recv()
        halo_spreads[1].start()
        halo_spreads[0].forward()

    x_spread.wait()

    @pl.when(place < per_tree - 2)
    def _():
        far_copy().start()

    for item in a_gathers:
        item.wait()
    u_gather.start()
    weights = w_ref[...].reshape(8, slot, width)[:, 0:deep].reshape(width, width)
    for j, ref in enumerate((wq_ref, wk_ref, wv_ref)):
        ref[...] = jnp.concatenate(
            [weights[:, j * wide : (j + 1) * wide], jnp.zeros((width, cols - wide), BF)], axis=1
        )
    wo_ref[0:wide, :] = weights[:, 3 * wide : 4 * wide].T
    wo_ref[wide:cols, :] = jnp.zeros((cols - wide, width), BF)
    wout_ref[pl.ds(t * wide, wide), :] = wo_ref[0:wide, :]
    wout_spread.start()
    gain_ref[...] = jnp.sum(w_ref[...].reshape(8, slot, width)[:, deep:slot].astype(F32), axis=0)[0:8]

    def norm_rows(at):
        x = xe_ref[pl.ds(at, SEG), :].astype(F32)
        r = lax.rsqrt(jnp.mean(x * x, axis=-1, keepdims=True) + EPS)
        n = (x * r * gain_ref[0:1, :]).astype(BF)
        k_ref[pl.ds(at, SEG), :] = nn(n, wk_ref[...]).astype(BF)
        v = nn(n, wv_ref[...]).astype(BF)
        v_ref[pl.ds(at, SEG), :] = v
        turn_ref[:, pl.ds(at, SEG)] = v.T
        return n

    def own_rows(i, _):
        at = pl.multiple_of(i * SEG, SEG)
        n = norm_rows(WINDOW + at)
        n1_ref[pl.ds(at, SEG), :] = n
        q_ref[pl.ds(at, SEG), :] = (nn(n, wq_ref[...]).astype(BF).astype(F32) * HD**-0.5).astype(BF)
        return 0

    lax.fori_loop(0, blocks, own_rows, 0)

    @pl.when(place >= 1)
    def _():
        halo_spreads[1].forward()
        for item in halo_spreads:
            item.wait()
            item.finish()

    cot_spread.start()

    @pl.when(place >= 2)
    def _():
        far_copy().wait_recv()

    def halo_rows(i, _):
        at = pl.multiple_of(i * SEG, SEG)
        xe_ref[pl.ds(at, SEG), :] = norm_rows(at)
        return 0

    lax.fori_loop(0, back, halo_rows, 0)
    span = (back + 1) * SEG

    def scores(i, h):
        at = pl.multiple_of(i * SEG, SEG)
        q = q_ref[pl.ds(at, SEG), :]
        qm = jnp.where(head_mask(h, SEG, cols), q, jnp.zeros_like(q))
        pool_ref[h * span : (h + 1) * span, :] = nt(k_ref[pl.ds(at, span), :], qm)

    scores(0, 0)

    def attend(i, _):
        at = pl.multiple_of(i * SEG, SEG)
        biases = [block_bias(seg_ref, par_ref, dp * blocks + i, back - j) for j in range(back + 1)]
        for h in range(3):
            if h < 2:
                scores(i, h + 1)
            else:
                scores(jnp.minimum(i + 1, blocks - 1), 0)
            top = None
            for j in range(back + 1):
                here = pl.ds(h * span + j * SEG, SEG)
                s = pool_ref[here, :]
                if j == 0 or j == back:
                    s = s + tri_ref[1 if j == 0 else 0]
                    pool_ref[here, :] = s
                best = jnp.max(s, axis=0, keepdims=True) + biases[j]
                top = best if top is None else jnp.maximum(top, best)
            top = top * LOG2E
            total = None
            for j in range(back + 1):
                e = jnp.exp2(pool_ref[pl.ds(h * span + j * SEG, SEG), :] * LOG2E - (top - biases[j]))
                part = jnp.sum(e, axis=0, keepdims=True)
                total = part if total is None else total + part
                e_ref[h, j * SEG : (j + 1) * SEG, :] = e.astype(BF)
            o = nn(turn_ref[h * HD : (h + 1) * HD, pl.ds(at, span)], e_ref[h])
            ct_ref[pl.ds(t * wide + h * HD, HD), pl.ds(at, SEG)] = (o / total).astype(BF)
            l_ref[h : h + 1, pl.ds(at, SEG)] = top + jnp.log(total) * LOG2E
        c_spread(i).start()

        @pl.when(i == 0)
        def _():
            for step in (1, 3, 2):
                u_gather.forward(step)
            d_gather.start()

        @pl.when(i > 0)
        def _():
            c_spread(i - 1).forward()

        return 0

    lax.fori_loop(0, blocks, attend, 0)
    c_spread(blocks - 1).forward()
    for step in (1, 3, 2):
        d_gather.forward(step)
    wout_spread.forward()
    wout_spread.wait()

    def middle(i, _):
        at = pl.multiple_of(i * SEG, SEG)
        c_spread(i).wait()
        m = xe_ref[pl.ds(WINDOW + at, SEG), :].astype(F32) + tn(ct_ref[:, pl.ds(at, SEG)], wout_ref[...])
        for j in range(width // 256):
            pool_ref[pl.ds(j * token + at, SEG), :] = m[:, j * 256 : (j + 1) * 256]
        r = lax.rsqrt(jnp.mean(m * m, axis=-1, keepdims=True) + EPS)
        n2_ref[pl.ds(at, SEG), :] = (m * r * gain_ref[1:2, :]).astype(BF)
        return 0

    lax.fori_loop(0, blocks, middle, 0)
    for j in range(width // 256):
        mid_ref[:, j * 256 : (j + 1) * 256] = pool_ref[pl.ds(j * token + t * rows, rows), :]
    cot_spread.forward()
    cot_spread.wait()
    u_gather.wait()
    d_gather.wait()

    def feed(k, _):
        at = (t ^ (3 - k)) * rows
        up = f_ref[:, 0:hidden]
        down_t = f_ref[:, hidden : 2 * hidden]
        u = nn(n2_ref[pl.ds(at, rows), :], up)
        cdf = 0.5 * (1.0 + lax.erf(u * 0.7071067811865476))
        act = (u * cdf).astype(BF)
        a_ref[pl.ds(at, rows), :] = act
        slope = cdf + u * jnp.exp2(u * u * (-0.5 * LOG2E)) * 0.3989422804014327
        gu = (nn(cot_all[pl.ds(at, rows), :], down_t) * slope).astype(BF)
        gu_ref[pl.ds(at, rows), :] = gu
        gn_own[...] = nt(gu, up)
        down_own[...] = nt(act, down_t)
        for i in range(3):

            @pl.when(k == i)
            def _():
                for j in range(2):
                    gn_folds[j].put(i, gn_own[j * part : (j + 1) * part, :])
                    if i != 1 or j == 0:
                        gn_folds[j].copy(i).start()
                down_fold.put(i, down_own[...])
                if i != 1:
                    down_fold.copy(i).start()

        return 0

    lax.fori_loop(0, 4, feed, 0)
    gn_folds[1].copy(1).start()
    for item in (x_spread, cot_spread, wout_spread, *a_gathers, u_gather, d_gather):
        item.finish()
    for i in range(blocks):
        c_spread(i).finish()

    @pl.when(place < per_tree - 1)
    def _():
        halo_copy(1).wait_send()

    @pl.when(place < per_tree - 2)
    def _():
        far_copy().wait_send()

    ones = jnp.ones((8, hidden), BF)

    def ffn_grads(j, _):
        at = pl.multiple_of(j * 256, 256)
        g = tn(n2_ref[:, pl.ds(at, 256)], gu_ref[...])
        gt_buf[0, :, pl.ds(at, 256)] = nt(ones, (g * f_ref[pl.ds(at, 256), 0:hidden].astype(F32)).astype(BF))
        f_ref[pl.ds(at, 256), 0:hidden] = g.astype(BF)
        return 0

    lax.fori_loop(0, width // 256, ffn_grads, 0)
    f_settles[0].start()

    def down_grads(j, _):
        at = pl.multiple_of(j * 256, 256)
        f_ref[pl.ds(at, 256), hidden : 2 * hidden] = tn(cot_all[:, pl.ds(at, 256)], a_ref[...]).astype(BF)
        return 0

    lax.fori_loop(0, width // 256, down_grads, 0)

    for j in range(2):
        here = slice(j * part, (j + 1) * part)
        gn2 = gn_folds[j].total(gn_own[here, :])
        mid = mid_ref[here, :]
        r2 = lax.rsqrt(jnp.mean(mid * mid, axis=-1, keepdims=True) + EPS)
        hat2 = mid * r2
        scaled = gn2 * gain_ref[1:2, :]
        inner = jnp.mean(scaled * hat2, axis=-1, keepdims=True)
        gmid = cot_ref[here, :].astype(F32) + r2 * (scaled - hat2 * inner)
        gmid_ref[here, :] = gmid
        gmb_ref[pl.ds(t * rows + j * part, part), :] = gmid.astype(BF)
        gmb_spreads[j].start()
    f_settles[1].start()
    for item in gn_folds:
        item.finish()

    def turn_keys(i, _):
        at = pl.multiple_of(i * SEG, SEG)
        turn_ref[:, pl.ds(at, SEG)] = k_ref[pl.ds(at, SEG), :].T
        return 0

    lax.fori_loop(0, blocks + back, turn_keys, 0)

    def mask_queries(i, _):
        at = pl.multiple_of(i * SEG, SEG)
        q = q_ref[pl.ds(at, SEG), :]
        for h in range(3):
            a_ref[pl.ds(at, SEG), h * cols : (h + 1) * cols] = jnp.where(head_mask(h, SEG, cols), q, jnp.zeros_like(q))
        return 0

    lax.fori_loop(0, blocks, mask_queries, 0)
    for item in gmb_spreads:
        item.forward()
    for item in gmb_spreads:
        item.wait()
    down_fold.copy(1).start()

    def context_grads(i, _):
        at = pl.multiple_of(i * SEG, SEG)
        low = nt(gmb_ref[pl.ds(at, SEG), :], wo_ref[...]).astype(BF)
        gct = low.astype(F32).T
        for h in range(3):
            gu_ref[pl.ds(at, SEG), h * cols : (h + 1) * cols] = jnp.where(
                head_mask(h, SEG, cols), low, jnp.zeros_like(low)
            )
            c = ct_ref[pl.ds(t * wide + h * HD, HD), pl.ds(at, SEG)].astype(F32)
            delta_ref[h : h + 1, pl.ds(at, SEG)] = jnp.sum(gct[h * HD : (h + 1) * HD] * c, axis=0, keepdims=True)
        return 0

    lax.fori_loop(0, blocks, context_grads, 0)
    for step in (2, 1, 3):
        f_settles[0].pass_on(step)
    go_ref[...] = nn(ct_ref[pl.ds(t * wide, wide), :], gmb_ref[...]).astype(BF).T
    o_settle.start()
    qm_ref, gm_ref = a_ref, gu_ref

    def piece(i, lo, hi, first):
        at, n = i * SEG, hi - lo
        keys = pl.ds(lo * SEG, n * SEG)
        values = pl.ds(ext + lo * SEG, n * SEG)
        for h in range(3):
            head = slice(h * cols, (h + 1) * cols)
            turned = slice(h * HD, (h + 1) * HD)
            qm, gm = qm_ref[at : at + SEG, head], gm_ref[at : at + SEG, head]
            s = nt(k_ref[keys, :], qm)
            g = nt(v_ref[keys, :], gm)
            logsum, delta = l_ref[h : h + 1, at : at + SEG], delta_ref[h : h + 1, at : at + SEG]
            for j in range(n):
                bias = block_bias(seg_ref, par_ref, dp * blocks + i, back + i - lo - j)
                part = slice(j * SEG, (j + 1) * SEG)
                x = s[part] * LOG2E
                if lo + j == i:
                    x = x + tri_ref[1]
                if lo + j == i + back:
                    x = x + tri_ref[0]
                p = jnp.exp2(x - (logsum - bias))
                e_ref[h, part, :] = p.astype(BF)
                xe_ref[WINDOW + j * SEG : WINDOW + (j + 1) * SEG, head] = (p * (g[part] - delta)).astype(BF)
            dv = nn(e_ref[h, 0 : n * SEG, :], gm)
            ds = xe_ref[WINDOW : WINDOW + n * SEG, head]
            dk = nn(ds, qm)
            dq = nn(turn_ref[turned, keys], ds)
            if first and h == 0:
                pool_ref[values, :] = dv
                pool_ref[keys, :] = dk
            else:
                pool_ref[values, :] += dv
                pool_ref[keys, :] += dk
            if lo == i:
                dqt_ref[turned, at : at + SEG] = dq
            else:
                dqt_ref[turned, at : at + SEG] += dq

    def outer(at, k, fold, with_query):
        gk = pool_ref[pl.ds(at, rows), 0:wide].astype(BF)
        gv = pool_ref[pl.ds(ext + at, rows), 0:wide].astype(BF)
        k_ref[pl.ds(at, rows), 0:wide] = gk
        v_ref[pl.ds(at, rows), 0:wide] = gv
        part = nt(gk, wk_ref[:, 0:wide]) + nt(gv, wv_ref[:, 0:wide])
        if with_query:
            part = part + nt(q_ref[pl.ds(at - WINDOW, rows), 0:wide], wq_ref[:, 0:wide])
        gn_own[...] = part
        if with_query:

            @pl.when((place < per_tree - 2) & (t ^ (3 - k) == 3))
            def _():
                far_back().wait_recv()
                gn_own[rows - lag :, :] += far_buf[1].astype(F32)

        for i in range(3):

            @pl.when(k == i)
            def _():
                fold.put(i, gn_own[...])
                fold.copy(i).start()

    piece(0, 0, 3, True)
    piece(0, 3, back, True)
    for i in range(1, blocks):
        piece(i, i, back, False)

    @pl.when(place >= 2)
    def _():
        gk = pool_ref[0:lag, 0:wide].astype(BF)
        gv = pool_ref[ext : ext + lag, 0:wide].astype(BF)
        far_buf[0] = (nt(gk, wk_ref[:, 0:wide]) + nt(gv, wv_ref[:, 0:wide])).astype(BF)
        far_back().start()

    k_ref[0:lag, 0:wide] = pool_ref[0:lag, 0:wide].astype(BF)
    v_ref[0:lag, 0:wide] = pool_ref[ext : ext + lag, 0:wide].astype(BF)

    def halo_outer(k, _):
        outer(lag + (t ^ (3 - k)) * rows, k, halo_fold, False)
        return 0

    lax.fori_loop(0, 4, halo_outer, 0)
    for step in (2, 1, 3):
        f_settles[1].pass_on(step)
    for i in range(blocks - 1, 1, -1):
        piece(i, back, back + i + 1, i == blocks - 1)

    for step in (2, 1, 3):
        o_settle.pass_on(step)
    for i in range(1, -1, -1):
        piece(i, back, back + i + 1, False)

    cot_all[3 * rows : 4 * rows, :] = halo_fold.total(gn_own[...]).astype(BF)

    @pl.when(place >= 1)
    def _():
        near_back().start()

    def turn_queries(i, _):
        at = pl.multiple_of(i * SEG, SEG)
        q_ref[pl.ds(at, SEG), 0:wide] = (dqt_ref[:, pl.ds(at, SEG)] * HD**-0.5).astype(BF).T
        return 0

    lax.fori_loop(0, blocks, turn_queries, 0)

    keep = pl.ds(WINDOW, token)
    own_k, own_v = pool_ref[keep, 0:wide].astype(BF), pool_ref[pl.ds(ext + WINDOW, token), 0:wide].astype(BF)
    k_ref[keep, 0:wide] = own_k
    v_ref[keep, 0:wide] = own_v
    grads = [
        tn(xe_ref[0:WINDOW, :], ref[0:WINDOW, 0:wide]) + tn(n1_ref[...], ref[WINDOW:, 0:wide]) for ref in (k_ref, v_ref)
    ]
    w_ref[0:width, 0 : 2 * wide] = jnp.concatenate([g.astype(BF) for g in grads], axis=1)
    a_settles[0].start()
    grads.append(tn(n1_ref[...], q_ref[:, 0:wide]))
    w_ref[0:width, 2 * wide : 3 * wide] = grads[2].astype(BF)
    a_settles[1].start()
    def own_outer(k, _):
        outer(WINDOW + (t ^ (3 - k)) * rows, k, gn1_fold, True)
        return 0

    lax.fori_loop(0, 4, own_outer, 0)
    terms = sum(g * w[:, 0:wide].astype(F32) for g, w in zip(grads, (wk_ref, wv_ref, wq_ref)))
    first_row = lax.broadcasted_iota(jnp.int32, (8, width), 0) == 0
    gt_buf[0] = jnp.where(first_row, nt(ones[:, 0:wide], terms.astype(BF)), gt_buf[0])
    for i in range(3):
        gain_copy(i).start()
    for step in (2, 1, 3):
        a_settles[0].pass_on(step)
    total = gt_buf[0]
    for i in range(3):
        gain_copy(i).wait_recv()
        total = total + gt_buf[i + 1]
    gd_buf[0] = total
    for i in range(7):
        gain_over(i).start()
    gup_ref[...] = f_settles[0].total()
    gdown_ref[...] = f_settles[1].total()
    gout_ref[...] = o_settle.total().T

    for step in (2, 1, 3):
        a_settles[1].pass_on(step)
    out_ref[...] = (mid_ref[...] + down_fold.total(down_own[...])).astype(BF)
    gn1 = gn1_fold.total(gn_own[...])

    @pl.when(place < per_tree - 1)
    def _():
        near_back().wait_recv()
        gn_own[...] = near_buf[...].astype(F32)

    @pl.when(place == per_tree - 1)
    def _():
        gn_own[...] = jnp.zeros((rows, width), F32)

    gn1 = gn1 + gn_own[...]
    x = x_ref[...].astype(F32)
    r1 = lax.rsqrt(jnp.mean(x * x, axis=-1, keepdims=True) + EPS)
    hat1 = x * r1
    scaled = gn1 * gain_ref[0:1, :]
    inner = jnp.mean(scaled * hat1, axis=-1, keepdims=True)
    ing_ref[...] = (gmid_ref[...] + r1 * (scaled - hat1 * inner)).astype(BF)

    total = gd_buf[0]
    for i in range(7):
        gain_over(i).wait_recv()
        total = total + gd_buf[i + 1]
    total = pltpu.roll(total, lax.rem(8 - dp, 8) * deep, 1)
    gg1_ref[...] = total[0:1, 0:deep] / g1_ref[...].astype(F32)
    gg2_ref[...] = total[1:2, 0:deep] / g2_ref[...].astype(F32)
    ga = a_settles[0].total()
    gk_out[...] = ga[:, 0:wide]
    gv_out[...] = ga[:, wide : 2 * wide]
    gq_out[...] = a_settles[1].total()[:, 0:wide]
    for i in range(3):
        gain_copy(i).wait_send()
    for i in range(7):
        gain_over(i).wait_send()
    for item in (down_fold, halo_fold, gn1_fold, *gmb_spreads, *f_settles, o_settle, *a_settles):
        item.finish()

    @pl.when(place >= 1)
    def _():
        near_back().wait_send()

    @pl.when(place >= 2)
    def _():
        far_back().wait_send()


def fast_shards(
    layer_input, cotangent, segments, parents, norm1_gain, w_query, w_key, w_value, w_out, norm2_gain, w_up, w_down,
):
    rows, width = layer_input.shape
    token = 4 * rows
    ext = token + WINDOW
    wide = width // 4
    cols = 256 * pl.cdiv(wide, 256)
    deep, hidden = w_up.shape
    blocks = token // SEG
    span = WINDOW + SEG
    shape = jax.ShapeDtypeStruct
    vmem = pl.BlockSpec(memory_space=pltpu.VMEM)
    smem = pl.BlockSpec(memory_space=pltpu.SMEM)
    copies = 7 * 3 + 4 * 8 + 3 + 3 * blocks + 5 * 3 + 5 * 7 + 2 + 3 + 7
    results = pl.pallas_call(
        kernel,
        out_shape=[
            shape((rows, width), BF),
            shape((rows, width), BF),
            shape((1, deep), F32),
            shape((deep, wide), F32),
            shape((deep, wide), F32),
            shape((deep, wide), F32),
            shape((wide, deep), F32),
            shape((1, deep), F32),
            shape((deep, hidden), F32),
            shape((deep, hidden), F32),
        ],
        in_specs=[smem, smem] + [vmem] * 10,
        out_specs=[vmem] * 10,
        scratch_shapes=[
            pltpu.VMEM((ext, width), BF),
            pltpu.VMEM((token, width), BF),
            pltpu.VMEM((token, width), BF),
            pltpu.VMEM((rows, width), F32),
            pltpu.VMEM((rows, width), F32),
            pltpu.VMEM((8 * (deep + 16), width), BF),
            pltpu.VMEM((width, 2 * hidden), BF),
            pltpu.VMEM((token, width), BF),
            pltpu.VMEM((width, width), BF),
            pltpu.VMEM((cols, width), BF),
            pltpu.VMEM((width, cols), BF),
            pltpu.VMEM((width, cols), BF),
            pltpu.VMEM((width, cols), BF),
            pltpu.VMEM((token, cols), BF),
            pltpu.VMEM((ext, cols), BF),
            pltpu.VMEM((ext, cols), BF),
            pltpu.VMEM((cols, ext), BF),
            pltpu.VMEM((width, token), BF),
            pltpu.VMEM((8, token), F32),
            pltpu.VMEM((8, width), F32),
            pltpu.VMEM((8, token), F32),
            pltpu.VMEM((2 * ext, SEG), F32),
            pltpu.VMEM((3, span, SEG), BF),
            pltpu.VMEM((2, SEG, SEG), F32),
            pltpu.VMEM((token, hidden), BF),
            pltpu.VMEM((token, hidden), BF),
            pltpu.VMEM((rows, width), F32),
            pltpu.VMEM((rows, width), F32),
            pltpu.VMEM((6, rows, width), BF),
            pltpu.VMEM((6, rows, width), BF),
            pltpu.VMEM((token, width), BF),
            pltpu.VMEM((4, deep, 2 * hidden), BF),
            pltpu.VMEM((3, deep, 2 * hidden), BF),
            pltpu.VMEM((width, wide), BF),
            pltpu.VMEM((4, deep, wide), BF),
            pltpu.VMEM((3, deep, wide), BF),
            pltpu.VMEM((4, deep, 128 * pl.cdiv(3 * wide, 128)), BF),
            pltpu.VMEM((3, deep, 128 * pl.cdiv(3 * wide, 128)), BF),
            pltpu.VMEM((wide, token), F32),
            pltpu.VMEM((rows, width), BF),
            pltpu.VMEM((2, WINDOW - token, width), BF),
            pltpu.VMEM((4, 8, width), F32),
            pltpu.VMEM((8, 8, width), F32),
            pltpu.SemaphoreType.DMA((copies,)),
            pltpu.SemaphoreType.DMA((copies,)),
        ],
        compiler_params=pltpu.CompilerParams(
            collective_id=0, has_side_effects=True, vmem_limit_bytes=64 << 20
        ),
    )(
        segments, parents, layer_input, cotangent, norm1_gain[None], w_query, w_key, w_value, w_out,
        norm2_gain[None], w_up, w_down.T,
    )
    results = list(hand_over(results))
    results[2], results[7], results[9] = results[2][0], results[7][0], results[9].T
    return tuple(results)


def hand_over(arrays):
    def body(*refs):
        for source, target in zip(refs[: len(arrays)], refs[len(arrays) :]):
            target[...] = source[...]

    vmem = pl.BlockSpec(memory_space=pltpu.VMEM)
    return pl.pallas_call(
        body,
        out_shape=[jax.ShapeDtypeStruct(a.shape, a.dtype) for a in arrays],
        in_specs=[vmem] * len(arrays),
        out_specs=[vmem] * len(arrays),
    )(*arrays)


epsilon = 1e-06
masked_score = -1e30


def from_behind(block, axis, distance):
    devices = range(lax.axis_size(axis))
    route = [(i - distance, i) for i in devices if i - distance in devices]
    return lax.ppermute(block, axis, route)


def split_up(x, dim, peers):
    dims = x.shape
    tiles = x.reshape(*dims[:dim], peers, dims[dim] // peers, *dims[dim + 1 :])
    return jnp.moveaxis(tiles, dim, 0)


def sum_at_owner(x, axis, dim):
    tiles = split_up(x, dim, lax.axis_size(axis))
    arrived = lax.all_to_all(tiles, axis, split_axis=0, concat_axis=0, tiled=True)
    return arrived.astype(jnp.float32).sum(axis=0)


def side_by_side(arrays, axis, dim, along):
    widths = [math.prod(a.shape[along:]) for a in arrays]
    both = jnp.concatenate(
        [a.reshape(*a.shape[:along], w) for a, w in zip(arrays, widths)], axis=along
    )
    whole = sum_at_owner(both, axis, dim)
    tiles = jnp.split(whole, [sum(widths[:k]) for k in range(1, len(widths))], axis=along)
    return tuple((b.reshape(*whole.shape[:along], *a.shape[along:]) for a, b in zip(arrays, tiles)))


def gelu_exact(values):
    return jax.nn.gelu(values, approximate=False)


def row_scale(values):
    return lax.rsqrt(jnp.mean(values * values, axis=-1, keepdims=True) + epsilon)


def norm_backward(incoming, normal_hat, row_factor, gain):
    scaled = incoming * gain
    inner = jnp.mean(scaled * normal_hat, axis=-1, keepdims=True)
    return (row_factor * (scaled - normal_hat * inner), jnp.sum(incoming * normal_hat, axis=0))


def parent_of(seg_ids, parents):
    seg_table = jnp.arange(parents.shape[0], dtype=jnp.int32)
    hits = seg_ids[:, None] == seg_table[None, :]
    return jnp.sum(jnp.where(hits, parents[None, :], 0), axis=1)


def shards(
    layer_input,
    cotangent,
    segments,
    parents,
    norm1_gain,
    w_query,
    w_key,
    w_value,
    w_out,
    norm2_gain,
    w_up,
    w_down,
):
    gain_one, full_query, full_key, full_value, full_out, gain_two, full_up, full_down = (
        lax.all_gather(norm1_gain, "dp", axis=0, tiled=True),
        lax.all_gather(w_query, "dp", axis=0, tiled=True),
        lax.all_gather(w_key, "dp", axis=0, tiled=True),
        lax.all_gather(w_value, "dp", axis=0, tiled=True),
        lax.all_gather(w_out, "dp", axis=1, tiled=True),
        lax.all_gather(norm2_gain, "dp", axis=0, tiled=True),
        lax.all_gather(w_up, "dp", axis=0, tiled=True),
        lax.all_gather(w_down, "dp", axis=1, tiled=True),
    )
    gain_one = gain_one.astype(jnp.float32)
    gain_two = gain_two.astype(jnp.float32)
    row_count = layer_input.shape[0]
    token_count = row_count * lax.axis_size("tensor")
    position = lax.axis_index("dp") * token_count
    head_width = full_query.shape[1]
    head_count = head_width // HD
    scaling = HD ** (-0.5)
    block_rows = min(640, token_count)
    block_count = token_count // block_rows
    span = WINDOW + block_rows
    hop_count = (WINDOW + token_count - 1) // token_count
    inputs = layer_input.astype(jnp.float32)
    factor_one = row_scale(inputs)
    hat_one = inputs * factor_one
    normed = (hat_one * gain_one).astype(jnp.bfloat16)
    normed_all = lax.all_gather(normed, "tensor", axis=0, tiled=True)
    queries = jnp.dot(normed_all, full_query, preferred_element_type=jnp.float32).astype(
        jnp.bfloat16
    )
    keys_own = jnp.dot(normed_all, full_key, preferred_element_type=jnp.float32).astype(
        jnp.bfloat16
    )
    values_own = jnp.dot(normed_all, full_value, preferred_element_type=jnp.float32).astype(
        jnp.bfloat16
    )
    pair_own = jnp.concatenate([keys_own, values_own], axis=1)
    halo_parts = []
    for distance in range(1, hop_count + 1):
        length = min(token_count, WINDOW - (distance - 1) * token_count)
        piece = pair_own[token_count - length :]
        moved = from_behind(piece, "dp", distance)
        halo_parts.append(moved)
    pair_all = jnp.concatenate(halo_parts[::-1] + [pair_own], axis=0)
    seg_padded = jnp.concatenate([jnp.full((WINDOW,), -1, jnp.int32), segments])
    seg_keys = lax.dynamic_slice_in_dim(seg_padded, position, WINDOW + token_count, 0)
    seg_query = seg_keys[WINDOW:]
    parent_one = parent_of(seg_query, parents)
    parent_two = parent_of(parent_one, parents)
    query_spots = jnp.arange(block_rows, dtype=jnp.int32)
    key_spots = jnp.arange(span, dtype=jnp.int32)

    def scores_of(offset):
        query_block = lax.dynamic_slice_in_dim(queries, offset, block_rows, 0).reshape(
            block_rows, head_count, HD
        )
        pair_block = lax.dynamic_slice_in_dim(pair_all, offset, span, 0)
        key_block = pair_block[:, :head_width].reshape(span, head_count, HD)
        value_block = pair_block[:, head_width:].reshape(span, head_count, HD)
        own_seg = lax.dynamic_slice_in_dim(seg_query, offset, block_rows, 0)
        up_one = lax.dynamic_slice_in_dim(parent_one, offset, block_rows, 0)
        up_two = lax.dynamic_slice_in_dim(parent_two, offset, block_rows, 0)
        near_seg = lax.dynamic_slice_in_dim(seg_keys, offset, span, 0)
        gap = WINDOW + query_spots[:, None] - key_spots[None, :]
        same_path = (
            (near_seg[None, :] == own_seg[:, None])
            | (near_seg[None, :] == up_one[:, None])
            | (near_seg[None, :] == up_two[:, None])
        )
        allowed = (gap >= 0) & (gap < WINDOW) & same_path
        raw = (
            jnp.einsum("qhd,khd->hqk", query_block, key_block, preferred_element_type=jnp.float32)
            * scaling
        )
        return (jnp.where(allowed[None], raw, masked_score), query_block, key_block, value_block)

    def forward_block(block_index):
        scores, query_block, key_block, value_block = scores_of(block_index * block_rows)
        row_max = jnp.max(scores, axis=-1, keepdims=True)
        exponent = jnp.exp(scores - row_max)
        denominator = jnp.sum(exponent, axis=-1, keepdims=True)
        weights = (exponent / denominator).astype(jnp.bfloat16)
        mixed = jnp.einsum("hqk,khd->qhd", weights, value_block, preferred_element_type=jnp.float32)
        return (
            mixed.reshape(block_rows, head_width).astype(jnp.bfloat16),
            (row_max + jnp.log(denominator))[..., 0],
        )

    context_blocks, logsum_blocks = lax.map(forward_block, jnp.arange(block_count, dtype=jnp.int32))
    context = context_blocks.reshape(token_count, head_width)
    middle = inputs + lax.psum_scatter(
        jnp.dot(context, full_out, preferred_element_type=jnp.float32).astype(jnp.bfloat16),
        "tensor",
        scatter_dimension=0,
        tiled=True,
    ).astype(jnp.float32)
    factor_two = row_scale(middle)
    hat_two = middle * factor_two
    normed_two = (hat_two * gain_two).astype(jnp.bfloat16)
    normed_two_all = lax.all_gather(normed_two, "tensor", axis=0, tiled=True)
    upper = jnp.dot(normed_two_all, full_up, preferred_element_type=jnp.float32)
    active = gelu_exact(upper).astype(jnp.bfloat16)
    result = middle + lax.psum_scatter(
        jnp.dot(active, full_down, preferred_element_type=jnp.float32).astype(jnp.bfloat16),
        "tensor",
        scatter_dimension=0,
        tiled=True,
    ).astype(jnp.float32)
    incoming = cotangent.astype(jnp.float32)
    incoming_all = lax.all_gather(cotangent, "tensor", axis=0, tiled=True)
    grad_down = jnp.einsum("tf,td->fd", active, incoming_all, preferred_element_type=jnp.float32)
    grad_active = jnp.einsum(
        "td,fd->tf", incoming_all, full_down, preferred_element_type=jnp.float32
    )
    unused_value, gelu_pull = jax.vjp(gelu_exact, upper)
    grad_upper = gelu_pull(grad_active)[0].astype(jnp.bfloat16)
    grad_up = jnp.einsum(
        "tc,tf->cf", normed_two_all, grad_upper, preferred_element_type=jnp.float32
    )
    grad_normed_two = lax.psum_scatter(
        jnp.einsum("tf,cf->tc", grad_upper, full_up, preferred_element_type=jnp.float32).astype(
            jnp.bfloat16
        ),
        "tensor",
        scatter_dimension=0,
        tiled=True,
    ).astype(jnp.float32)
    through_two, gain_two_part = norm_backward(grad_normed_two, hat_two, factor_two, gain_two)
    grad_middle = incoming + through_two
    grad_middle_all = lax.all_gather(grad_middle.astype(jnp.bfloat16), "tensor", axis=0, tiled=True)
    grad_out = jnp.einsum("tc,td->cd", context, grad_middle_all, preferred_element_type=jnp.float32)
    grad_context = jnp.einsum(
        "td,cd->tc", grad_middle_all, full_out, preferred_element_type=jnp.float32
    ).astype(jnp.bfloat16)

    def backward_block(block_index, carry):
        grad_queries, grad_pairs = carry
        offset = block_index * block_rows
        scores, query_block, key_block, value_block = scores_of(offset)
        logsum = lax.dynamic_index_in_dim(logsum_blocks, block_index, 0, keepdims=False)
        probs = jnp.exp(scores - logsum[..., None])
        grad_rows = lax.dynamic_slice_in_dim(grad_context, offset, block_rows, 0).reshape(
            block_rows, head_count, HD
        )
        grad_probs = jnp.einsum(
            "qhd,khd->hqk", grad_rows, value_block, preferred_element_type=jnp.float32
        )
        inner = jnp.sum(probs * grad_probs, axis=-1, keepdims=True)
        grad_scores = (probs * (grad_probs - inner)).astype(jnp.bfloat16)
        grad_query_block = (
            jnp.einsum("hqk,khd->qhd", grad_scores, key_block, preferred_element_type=jnp.float32)
            * scaling
        )
        grad_key_block = (
            jnp.einsum("hqk,qhd->khd", grad_scores, query_block, preferred_element_type=jnp.float32)
            * scaling
        )
        grad_value_block = jnp.einsum(
            "hqk,qhd->khd",
            probs.astype(jnp.bfloat16),
            grad_rows,
            preferred_element_type=jnp.float32,
        )
        grad_queries = lax.dynamic_update_slice_in_dim(
            grad_queries, grad_query_block.reshape(block_rows, head_width), offset, 0
        )
        update = jnp.concatenate(
            [grad_key_block.reshape(span, head_width), grad_value_block.reshape(span, head_width)],
            axis=1,
        )
        current = lax.dynamic_slice_in_dim(grad_pairs, offset, span, 0)
        grad_pairs = lax.dynamic_update_slice_in_dim(grad_pairs, current + update, offset, 0)
        return (grad_queries, grad_pairs)

    start_carry = (
        jnp.zeros((token_count, head_width), jnp.float32),
        jnp.zeros((WINDOW + token_count, 2 * head_width), jnp.float32),
    )
    grad_queries, grad_pairs = lax.fori_loop(0, block_count, backward_block, start_carry)
    grad_own = grad_pairs[WINDOW:]
    for distance in range(1, hop_count + 1):
        length = min(token_count, WINDOW - (distance - 1) * token_count)
        first_row = WINDOW - (distance - 1) * token_count - length
        piece = grad_pairs[first_row : first_row + length]
        returned = from_behind(piece.astype(jnp.bfloat16), "dp", -distance).astype(piece.dtype)
        grad_own = grad_own + jnp.pad(returned, ((token_count - length, 0), (0, 0)))
    grad_keys = grad_own[:, :head_width].astype(jnp.bfloat16)
    grad_values = grad_own[:, head_width:].astype(jnp.bfloat16)
    grad_queries_low = grad_queries.astype(jnp.bfloat16)
    grad_query = jnp.einsum(
        "tc,tq->cq", normed_all, grad_queries_low, preferred_element_type=jnp.float32
    )
    grad_key = jnp.einsum("tc,tq->cq", normed_all, grad_keys, preferred_element_type=jnp.float32)
    grad_value = jnp.einsum(
        "tc,tq->cq", normed_all, grad_values, preferred_element_type=jnp.float32
    )
    part_query = jnp.einsum(
        "tq,cq->tc", grad_queries_low, full_query, preferred_element_type=jnp.float32
    )
    part_key = jnp.einsum("tq,cq->tc", grad_keys, full_key, preferred_element_type=jnp.float32)
    part_value = jnp.einsum(
        "tq,cq->tc", grad_values, full_value, preferred_element_type=jnp.float32
    )
    grad_normed = lax.psum_scatter(
        (part_query + part_key + part_value).astype(jnp.bfloat16),
        "tensor",
        scatter_dimension=0,
        tiled=True,
    ).astype(jnp.float32)
    through_one, gain_one_part = norm_backward(grad_normed, hat_one, factor_one, gain_one)
    grad_inputs = grad_middle + through_one
    gain_one_sum, gain_two_sum = lax.psum((gain_one_part, gain_two_part), "tensor")
    summed = (
        *side_by_side(
            (
                gain_one_sum.astype(jnp.bfloat16),
                grad_query.astype(jnp.bfloat16),
                grad_key.astype(jnp.bfloat16),
                grad_value.astype(jnp.bfloat16),
            ),
            "dp",
            0,
            1,
        ),
        sum_at_owner(grad_out.astype(jnp.bfloat16), "dp", 1),
        *side_by_side(
            (gain_two_sum.astype(jnp.bfloat16), grad_up.astype(jnp.bfloat16)), "dp", 0, 1
        ),
        sum_at_owner(grad_down.astype(jnp.bfloat16), "dp", 1),
    )
    return (
        result.astype(jnp.bfloat16),
        grad_inputs.astype(jnp.bfloat16),
        summed[0],
        summed[1],
        summed[2],
        summed[3],
        summed[4],
        summed[5],
        summed[6],
        summed[7],
    )


def solution(mesh):
    fast = mesh.shape["dp"] == 8 and mesh.shape["tensor"] == 4
    return jax.shard_map(
        fast_shards if fast else shards,
        mesh=mesh,
        in_specs=(
            P(("dp", "tensor"), None),
            P(("dp", "tensor"), None),
            P(),
            P(),
            P("dp"),
            P("dp", "tensor"),
            P("dp", "tensor"),
            P("dp", "tensor"),
            P("tensor", "dp"),
            P("dp"),
            P("dp", "tensor"),
            P("tensor", "dp"),
        ),
        out_specs=(
            P(("dp", "tensor"), None),
            P(("dp", "tensor"), None),
            P("dp"),
            P("dp", "tensor"),
            P("dp", "tensor"),
            P("dp", "tensor"),
            P("tensor", "dp"),
            P("dp"),
            P("dp", "tensor"),
            P("tensor", "dp"),
        ),
        check_vma=False,
    )
```

```python
import functools
import math

import jax
import jax.numpy as jnp
from jax import lax
from jax.experimental import pallas as pl
from jax.experimental.pallas import tpu as pltpu
from jax.sharding import PartitionSpec as P

MESH = pl.DeviceIdType.MESH
BF = jnp.bfloat16
F32 = jnp.float32
HD = 64
WINDOW = 1536
SEG = 256
TREE = 5120
LOG2E = 1.4426950408889634
NEG = -1e30
EPS = 1e-6


def nt(a, b):
    return lax.dot_general(a, b, (((1,), (1,)), ((), ())), preferred_element_type=F32)


def nn(a, b):
    return jnp.dot(a, b, preferred_element_type=F32)


def tn(a, b):
    return lax.dot_general(a, b, (((0,), (0,)), ((), ())), preferred_element_type=F32)


class Links:
    def __init__(self, send, recv):
        self.send, self.recv, self.used = send, recv, 0

    def take(self, count):
        base = self.used
        self.used += count
        return base

    def copy(self, src, dst, send, recv, device):
        return pltpu.make_async_remote_copy(
            src_ref=src,
            dst_ref=dst,
            send_sem=self.send.at[send],
            recv_sem=self.recv.at[recv],
            device_id=device,
            device_id_type=MESH,
        )


class Spread:
    def __init__(self, links, base, dp, t, part):
        self.links, self.base, self.dp, self.t, self.part = links, base, dp, t, part

    def leave(self, i):
        flip, what = ((1, 0), (2, 0), (1, 2))[i]
        ref = self.part(self.t ^ what)
        return self.links.copy(ref, ref, self.base + i, self.base + i, (self.dp, self.t ^ flip))

    def come(self, i):
        flip, what = ((1, 1), (2, 2), (1, 3))[i]
        ref = self.part(self.t ^ what)
        return self.links.copy(ref, ref, self.base + i, self.base + i, (self.dp, self.t ^ flip))

    def start(self):
        self.leave(1).start()
        self.leave(0).start()

    def forward(self):
        self.come(1).wait_recv()
        self.leave(2).start()

    def wait(self):
        self.come(0).wait_recv()
        self.come(2).wait_recv()

    def finish(self):
        for i in range(3):
            self.leave(i).wait_send()


class Gather:
    def __init__(self, links, base, dp, t, slot):
        self.links, self.base, self.dp, self.t, self.slot = links, base, dp, t, slot
        self.z, self.y = dp // 2, dp % 2

    def at(self, step):
        z = lax.rem(self.z + step, 4)
        return z, z * 2 + self.y

    def along(self, step):
        z, peer = self.at(step)
        return self.links.copy(self.slot(self.dp), self.slot(self.dp), self.base + step - 1, self.base + self.z, (peer, self.t))

    def came(self, step):
        z, peer = self.at(step)
        return self.links.copy(self.slot(peer), self.slot(peer), self.base + step - 1, self.base + z, (peer, self.t))

    def across(self, step):
        z, peer = self.at(step)
        return self.links.copy(self.slot(peer), self.slot(peer), self.base + 4 + step, self.base + 4 + z, (self.dp ^ 1, self.t))

    def crossed(self, step):
        z, peer = self.at(step)
        other = z * 2 + (1 - self.y)
        return self.links.copy(self.slot(other), self.slot(other), self.base + 4 + step, self.base + 4 + z, (self.dp ^ 1, self.t))

    def start(self):
        self.across(0).start()
        for step in (1, 3, 2):
            self.along(step).start()

    def forward(self, step):
        self.came(step).wait_recv()
        self.across(step).start()

    def wait(self):
        for step in range(4):
            self.crossed(step).wait_recv()

    def finish(self):
        for step in range(1, 4):
            self.along(step).wait_send()
        for step in range(4):
            self.across(step).wait_send()


def head_mask(h, rows, width):
    lane = lax.broadcasted_iota(jnp.int32, (rows, width), 1)
    return (lane >= h * HD) & (lane < (h + 1) * HD)


def block_bias(seg_ref, par_ref, block, back):
    own = seg_ref[block * SEG]
    one = par_ref[own]
    two = par_ref[one]
    far = block - back
    near = seg_ref[jnp.maximum(far, 0) * SEG]
    ok = ((near == own) | (near == one) | (near == two)) & (far >= 0)
    return jnp.where(ok, jnp.float32(0.0), jnp.float32(NEG))


class Fold:
    def __init__(self, links, base, dp, t, out, into):
        self.links, self.base, self.dp, self.t, self.out, self.into = links, base, dp, t, out, into

    def copy(self, i):
        flip = (1, 2, 1)[i]
        return self.links.copy(
            self.out(i), self.into(i), self.base + i, self.base + i, (self.dp, self.t ^ flip)
        )

    def put(self, i, value):
        if i == 1:
            self.copy(0).wait_recv()
            value = value + self.into(0)[...].astype(F32)
        self.out(i)[...] = value.astype(BF)

    def total(self, value):
        self.copy(1).wait_recv()
        self.copy(2).wait_recv()
        return value + self.into(2)[...].astype(F32) + self.into(1)[...].astype(F32)

    def finish(self):
        for i in range(3):
            self.copy(i).wait_send()


class Settle:
    def __init__(self, links, base, dp, t, slots, deep, from_y, from_z):
        self.links, self.base, self.dp, self.t = links, base, dp, t
        self.slots, self.deep, self.from_y, self.from_z = slots, deep, from_y, from_z
        self.z, self.y = dp // 2, lax.rem(dp, 2)

    def rows(self, z, y):
        return pl.ds(pl.multiple_of((z * 2 + y) * self.deep, self.deep), self.deep)

    def across(self, step):
        z = lax.rem(self.z + step, 4)
        return self.links.copy(
            self.slots.at[self.rows(z, 1 - self.y)],
            self.from_y.at[step],
            self.base + step,
            self.base + step,
            (self.dp ^ 1, self.t),
        )

    def along(self, step):
        z = lax.rem(self.z + step, 4)
        return self.links.copy(
            self.slots.at[self.rows(z, self.y)],
            self.from_z.at[step - 1],
            self.base + 3 + step,
            self.base + 3 + step,
            (z * 2 + self.y, self.t),
        )

    def start(self, steps=(2, 1, 3, 0)):
        for step in steps:
            self.across(step).start()

    def pass_on(self, step):
        self.across(step).wait_recv()
        z = lax.rem(self.z + step, 4)
        at = self.rows(z, self.y)
        self.slots[at, :] = (self.slots[at, :].astype(F32) + self.from_y[step].astype(F32)).astype(BF)
        self.along(step).start()

    def total(self):
        self.across(0).wait_recv()
        value = self.slots[self.rows(self.z, self.y), :].astype(F32) + self.from_y[0].astype(F32)
        for step in (1, 2, 3):
            self.along(step).wait_recv()
            value = value + self.from_z[step - 1].astype(F32)
        return value

    def finish(self):
        for step in range(4):
            self.across(step).wait_send()
        for step in (1, 2, 3):
            self.along(step).wait_send()


def kernel(
    seg_ref, par_ref, x_ref, cot_ref, g1_ref, wq_in, wk_in, wv_in, wo_in, g2_ref, wu_in, wd_in,
    out_ref, ing_ref, gg1_ref, gq_out, gk_out, gv_out, gout_ref, gg2_ref, gup_ref, gdown_ref,
    xe_ref, n1_ref, n2_ref, mid_ref, gmid_ref, w_ref, f_ref, cot_all, wout_ref, wo_ref, wq_ref, wk_ref, wv_ref,
    q_ref, k_ref, v_ref, turn_ref, ct_ref, l_ref, gain_ref, delta_ref, pool_ref, e_ref, tri_ref,
    a_ref, gu_ref, down_own, gn_own, down_buf, gn_buf, gmb_ref,
    gfy_ref, gfz_ref, go_ref, goy_ref, goz_ref, gay_ref, gaz_ref, dqt_ref, near_buf, far_buf, gt_buf, gd_buf, send, recv,
):
    dp, t = lax.axis_index("dp"), lax.axis_index("tensor")
    rows, width = x_ref.shape
    token = 4 * rows
    ext = token + WINDOW
    blocks = token // SEG
    back = WINDOW // SEG
    lag = WINDOW - token
    per_tree = TREE // token
    place = lax.rem(dp, per_tree)
    wide = width // 4
    cols = q_ref.shape[1]
    deep = wu_in.shape[0]
    hidden = wu_in.shape[1]
    links = Links(send, recv)
    spread = lambda part: Spread(links, links.take(3), dp, t, part)
    x_spread = spread(lambda p: xe_ref.at[pl.ds(WINDOW + p * rows, rows)])
    part = rows // 2
    halo_half = lambda p, j: xe_ref.at[pl.ds(lag + p * rows + j * part, part)]
    halo_spreads = [spread(lambda p, j=j: halo_half(p, j)) for j in range(2)]
    cot_spread = spread(lambda p: cot_all.at[pl.ds(p * rows, rows)])
    wout_spread = spread(lambda p: wout_ref.at[pl.ds(p * wide, wide)])
    gmb_spreads = [spread(lambda p, j=j: gmb_ref.at[pl.ds(p * rows + j * part, part)]) for j in range(2)]
    slot = deep + 16
    a_slot = lambda s: pl.ds(pl.multiple_of(s * slot, 16), slot)
    half = width // 2
    a_gathers = [
        Gather(links, links.take(8), dp, t, lambda s, j=j: w_ref.at[a_slot(s), pl.ds(j * half, half)]) for j in range(2)
    ]
    f_slot = lambda s: pl.ds(pl.multiple_of(s * deep, deep), deep)
    u_gather = Gather(links, links.take(8), dp, t, lambda s: f_ref.at[f_slot(s), pl.ds(0, hidden)])
    d_gather = Gather(links, links.take(8), dp, t, lambda s: f_ref.at[f_slot(s), pl.ds(hidden, hidden)])
    h1 = links.take(2)
    h2 = links.take(1)
    halo_copy = lambda j: links.copy(
        x_ref.at[pl.ds(j * part, part)], halo_half(t, j), h1 + j, h1 + j, (lax.rem(dp + 1, 8), t)
    )
    far_copy = lambda: links.copy(
        xe_ref.at[pl.ds(WINDOW + token - lag, lag)], xe_ref.at[pl.ds(0, lag)], h2, h2, (lax.rem(dp + 2, 8), t)
    )
    c_base = links.take(3 * blocks)

    def c_spread(i):
        at = pl.multiple_of(i * SEG, SEG)
        return Spread(links, c_base + 3 * i, dp, t, lambda p: ct_ref.at[pl.ds(p * wide, wide), pl.ds(at, SEG)])

    down_fold = Fold(links, links.take(3), dp, t, lambda i: down_buf.at[i], lambda i: down_buf.at[3 + i])
    gn_folds = [
        Fold(
            links,
            links.take(3),
            dp,
            t,
            lambda i, j=j: gn_buf.at[i, pl.ds(j * part, part)],
            lambda i, j=j: gn_buf.at[3 + i, pl.ds(j * part, part)],
        )
        for j in range(2)
    ]
    gn1_fold = Fold(links, links.take(3), dp, t, lambda i: gn_buf.at[i], lambda i: gn_buf.at[3 + i])
    halo_fold = Fold(
        links,
        links.take(3),
        dp,
        t,
        lambda i: cot_all.at[pl.ds(i * rows, rows)],
        lambda i: n2_ref.at[pl.ds(i * rows, rows)],
    )
    f_settles = [
        Settle(
            links,
            links.take(7),
            dp,
            t,
            f_ref.at[:, pl.ds(j * hidden, hidden)],
            deep,
            gfy_ref.at[:, :, pl.ds(j * hidden, hidden)],
            gfz_ref.at[:, :, pl.ds(j * hidden, hidden)],
        )
        for j in range(2)
    ]
    o_settle = Settle(links, links.take(7), dp, t, go_ref, deep, goy_ref, goz_ref)
    a_settles = [
        Settle(
            links,
            links.take(7),
            dp,
            t,
            w_ref.at[:, pl.ds(a, n)],
            deep,
            gay_ref.at[:, :, pl.ds(a, n)],
            gaz_ref.at[:, :, pl.ds(a, n)],
        )
        for a, n in ((0, 2 * wide), (2 * wide, gay_ref.shape[2] - 2 * wide))
    ]
    b1 = links.take(1)
    b2 = links.take(1)
    near_back = lambda: links.copy(cot_all.at[pl.ds(3 * rows, rows)], near_buf, b1, b1, (lax.rem(dp + 7, 8), t))
    far_back = lambda: links.copy(far_buf.at[0], far_buf.at[1], b2, b2, (lax.rem(dp + 6, 8), t))
    gb = links.take(3)
    gd = links.take(7)

    def gain_copy(i):
        return links.copy(gt_buf.at[0], gt_buf.at[i + 1], gb + i, gb + i, (dp, t ^ (i + 1)))

    def gain_over(i):
        return links.copy(gd_buf.at[0], gd_buf.at[i + 1], gd + i, gd + i, (lax.rem(dp + i + 1, 8), t))

    barrier = pltpu.get_barrier_semaphore()
    for step in range(1, 8):
        pl.semaphore_signal(barrier, inc=1, device_id=(lax.rem(dp + step, 8), t), device_id_type=MESH)
    for flip in (1, 2, 3):
        pl.semaphore_signal(barrier, inc=1, device_id=(dp, t ^ flip), device_id_type=MESH)

    base = pl.multiple_of(dp * slot, 16)
    w_ref[pl.ds(base, deep), :] = jnp.concatenate(
        [wq_in[...], wk_in[...], wv_in[...], wo_in[...].astype(F32).T.astype(BF)], axis=1
    )
    lane = lax.broadcasted_iota(jnp.int32, (deep, width), 1)
    line = lax.broadcasted_iota(jnp.int32, (deep, width), 0)
    put = jnp.where(lane == line + dp * deep, 1.0, 0.0).astype(BF)
    two = jnp.concatenate([g1_ref[...], g2_ref[...], jnp.zeros((14, deep), BF)], axis=0)
    w_ref[pl.ds(base + deep, 16), :] = nn(two, put).astype(BF)
    xe_ref[pl.ds(WINDOW + t * rows, rows), :] = x_ref[...]
    pl.semaphore_wait(barrier, 10)
    a_gathers[0].start()
    x_spread.start()

    @pl.when(place < per_tree - 1)
    def _():
        halo_copy(0).start()

    f_ref[f_slot(dp), 0:hidden] = wu_in[...]
    f_ref[f_slot(dp), hidden : 2 * hidden] = wd_in[...]
    cot_all[pl.ds(t * rows, rows), :] = cot_ref[...]

    @pl.when(place < 1)
    def _():
        xe_ref[pl.ds(lag, token), :] = jnp.zeros((token, width), BF)

    @pl.when(place < 2)
    def _():
        xe_ref[pl.ds(0, lag), :] = jnp.zeros((lag, width), BF)

    row = lax.broadcasted_iota(jnp.int32, (SEG, SEG), 0)
    col = lax.broadcasted_iota(jnp.int32, (SEG, SEG), 1)
    tri_ref[0] = jnp.where(row <= col, 0.0, NEG)
    tri_ref[1] = jnp.where(row > col, 0.0, NEG)
    for step in (1, 3, 2):
        a_gathers[0].forward(step)
    a_gathers[1].start()

    @pl.when(place < per_tree - 1)
    def _():
        halo_copy(0).wait_send()
        halo_copy(1).start()

    @pl.when(place >= 1)
    def _():
        halo_copy(0).wait_recv()
        halo_spreads[0].start()

    x_spread.forward()
    for step in (1, 3, 2):
        a_gathers[1].forward(step)

    @pl.when(place >= 1)
    def _():
        halo_copy(1).wait_recv()
        halo_spreads[1].start()
        halo_spreads[0].forward()

    x_spread.wait()

    @pl.when(place < per_tree - 2)
    def _():
        far_copy().start()

    for item in a_gathers:
        item.wait()
    u_gather.start()
    weights = w_ref[...].reshape(8, slot, width)[:, 0:deep].reshape(width, width)
    for j, ref in enumerate((wq_ref, wk_ref, wv_ref)):
        ref[...] = jnp.concatenate(
            [weights[:, j * wide : (j + 1) * wide], jnp.zeros((width, cols - wide), BF)], axis=1
        )
    wo_ref[0:wide, :] = weights[:, 3 * wide : 4 * wide].T
    wo_ref[wide:cols, :] = jnp.zeros((cols - wide, width), BF)
    wout_ref[pl.ds(t * wide, wide), :] = wo_ref[0:wide, :]
    wout_spread.start()
    gain_ref[...] = jnp.sum(w_ref[...].reshape(8, slot, width)[:, deep:slot].astype(F32), axis=0)[0:8]

    def norm_rows(at):
        x = xe_ref[pl.ds(at, SEG), :].astype(F32)
        r = lax.rsqrt(jnp.mean(x * x, axis=-1, keepdims=True) + EPS)
        n = (x * r * gain_ref[0:1, :]).astype(BF)
        k_ref[pl.ds(at, SEG), :] = nn(n, wk_ref[...]).astype(BF)
        v = nn(n, wv_ref[...]).astype(BF)
        v_ref[pl.ds(at, SEG), :] = v
        turn_ref[:, pl.ds(at, SEG)] = v.T
        return n

    def own_rows(i, _):
        at = pl.multiple_of(i * SEG, SEG)
        n = norm_rows(WINDOW + at)
        n1_ref[pl.ds(at, SEG), :] = n
        q_ref[pl.ds(at, SEG), :] = (nn(n, wq_ref[...]).astype(BF).astype(F32) * HD**-0.5).astype(BF)
        return 0

    lax.fori_loop(0, blocks, own_rows, 0)

    @pl.when(place >= 1)
    def _():
        halo_spreads[1].forward()
        for item in halo_spreads:
            item.wait()
            item.finish()

    cot_spread.start()

    @pl.when(place >= 2)
    def _():
        far_copy().wait_recv()

    def halo_rows(i, _):
        at = pl.multiple_of(i * SEG, SEG)
        xe_ref[pl.ds(at, SEG), :] = norm_rows(at)
        return 0

    lax.fori_loop(0, back, halo_rows, 0)
    span = (back + 1) * SEG

    def scores(i, h):
        at = pl.multiple_of(i * SEG, SEG)
        q = q_ref[pl.ds(at, SEG), :]
        qm = jnp.where(head_mask(h, SEG, cols), q, jnp.zeros_like(q))
        pool_ref[h * span : (h + 1) * span, :] = nt(k_ref[pl.ds(at, span), :], qm)

    scores(0, 0)

    def attend(i, _):
        at = pl.multiple_of(i * SEG, SEG)
        biases = [block_bias(seg_ref, par_ref, dp * blocks + i, back - j) for j in range(back + 1)]
        for h in range(3):
            if h < 2:
                scores(i, h + 1)
            else:
                scores(jnp.minimum(i + 1, blocks - 1), 0)
            top = None
            for j in range(back + 1):
                here = pl.ds(h * span + j * SEG, SEG)
                s = pool_ref[here, :]
                if j == 0 or j == back:
                    s = s + tri_ref[1 if j == 0 else 0]
                    pool_ref[here, :] = s
                best = jnp.max(s, axis=0, keepdims=True) + biases[j]
                top = best if top is None else jnp.maximum(top, best)
            top = top * LOG2E
            total = None
            for j in range(back + 1):
                e = jnp.exp2(pool_ref[pl.ds(h * span + j * SEG, SEG), :] * LOG2E - (top - biases[j]))
                part = jnp.sum(e, axis=0, keepdims=True)
                total = part if total is None else total + part
                e_ref[h, j * SEG : (j + 1) * SEG, :] = e.astype(BF)
            o = nn(turn_ref[h * HD : (h + 1) * HD, pl.ds(at, span)], e_ref[h])
            ct_ref[pl.ds(t * wide + h * HD, HD), pl.ds(at, SEG)] = (o / total).astype(BF)
            l_ref[h : h + 1, pl.ds(at, SEG)] = top + jnp.log(total) * LOG2E
        c_spread(i).start()

        @pl.when(i == 0)
        def _():
            for step in (1, 3, 2):
                u_gather.forward(step)
            d_gather.start()

        @pl.when(i > 0)
        def _():
            c_spread(i - 1).forward()

        @pl.when(i == 2)
        def _():
            wout_spread.forward()

        return 0

    lax.fori_loop(0, blocks, attend, 0)
    c_spread(blocks - 1).forward()
    for step in (1, 3, 2):
        d_gather.forward(step)
    cot_spread.forward()
    wout_spread.wait()

    def middle(i, _):
        at = pl.multiple_of(i * SEG, SEG)
        c_spread(i).wait()
        m = xe_ref[pl.ds(WINDOW + at, SEG), :].astype(F32) + tn(ct_ref[:, pl.ds(at, SEG)], wout_ref[...])
        for j in range(width // 256):
            pool_ref[pl.ds(j * token + at, SEG), :] = m[:, j * 256 : (j + 1) * 256]
        r = lax.rsqrt(jnp.mean(m * m, axis=-1, keepdims=True) + EPS)
        n2_ref[pl.ds(at, SEG), :] = (m * r * gain_ref[1:2, :]).astype(BF)
        return 0

    lax.fori_loop(0, blocks, middle, 0)
    for j in range(width // 256):
        mid_ref[:, j * 256 : (j + 1) * 256] = pool_ref[pl.ds(j * token + t * rows, rows), :]
    cot_spread.wait()
    u_gather.wait()
    d_gather.wait()

    def feed(k, _):
        at = (t ^ (3 - k)) * rows
        up = f_ref[:, 0:hidden]
        down_t = f_ref[:, hidden : 2 * hidden]
        u = nn(n2_ref[pl.ds(at, rows), :], up)
        cdf = 0.5 * (1.0 + lax.erf(u * 0.7071067811865476))
        act = (u * cdf).astype(BF)
        a_ref[pl.ds(at, rows), :] = act
        slope = cdf + u * jnp.exp2(u * u * (-0.5 * LOG2E)) * 0.3989422804014327
        gu = (nn(cot_all[pl.ds(at, rows), :], down_t) * slope).astype(BF)
        gu_ref[pl.ds(at, rows), :] = gu
        gn_own[...] = nt(gu, up)
        down_own[...] = nt(act, down_t)
        for i in range(3):

            @pl.when(k == i)
            def _():
                for j in range(2):
                    gn_folds[j].put(i, gn_own[j * part : (j + 1) * part, :])
                    if i != 1 or j == 0:
                        gn_folds[j].copy(i).start()
                down_fold.put(i, down_own[...])
                if i != 1:
                    down_fold.copy(i).start()

        return 0

    lax.fori_loop(0, 4, feed, 0)
    gn_folds[1].copy(1).start()
    for item in (x_spread, cot_spread, wout_spread, *a_gathers, u_gather, d_gather):
        item.finish()
    for i in range(blocks):
        c_spread(i).finish()

    @pl.when(place < per_tree - 1)
    def _():
        halo_copy(1).wait_send()

    @pl.when(place < per_tree - 2)
    def _():
        far_copy().wait_send()

    ones = jnp.ones((8, hidden), BF)

    def ffn_grads(j, _):
        at = pl.multiple_of(j * 256, 256)
        g = tn(n2_ref[:, pl.ds(at, 256)], gu_ref[...])
        gt_buf[0, :, pl.ds(at, 256)] = nt(ones, (g * f_ref[pl.ds(at, 256), 0:hidden].astype(F32)).astype(BF))
        f_ref[pl.ds(at, 256), 0:hidden] = g.astype(BF)
        return 0

    lax.fori_loop(0, width // 256, ffn_grads, 0)
    f_settles[0].start()

    def down_grads(j, _):
        at = pl.multiple_of(j * 256, 256)
        f_ref[pl.ds(at, 256), hidden : 2 * hidden] = tn(cot_all[:, pl.ds(at, 256)], a_ref[...]).astype(BF)
        return 0

    lax.fori_loop(0, width // 256, down_grads, 0)

    for j in range(2):
        here = slice(j * part, (j + 1) * part)
        gn2 = gn_folds[j].total(gn_own[here, :])
        mid = mid_ref[here, :]
        r2 = lax.rsqrt(jnp.mean(mid * mid, axis=-1, keepdims=True) + EPS)
        hat2 = mid * r2
        scaled = gn2 * gain_ref[1:2, :]
        inner = jnp.mean(scaled * hat2, axis=-1, keepdims=True)
        gmid = cot_ref[here, :].astype(F32) + r2 * (scaled - hat2 * inner)
        gmid_ref[here, :] = gmid
        gmb_ref[pl.ds(t * rows + j * part, part), :] = gmid.astype(BF)
        gmb_spreads[j].start()
    f_settles[1].start()
    for item in gn_folds:
        item.finish()

    def turn_keys(i, _):
        at = pl.multiple_of(i * SEG, SEG)
        turn_ref[:, pl.ds(at, SEG)] = k_ref[pl.ds(at, SEG), :].T
        return 0

    lax.fori_loop(0, blocks + back, turn_keys, 0)

    def mask_queries(i, _):
        at = pl.multiple_of(i * SEG, SEG)
        q = q_ref[pl.ds(at, SEG), :]
        for h in range(3):
            a_ref[pl.ds(at, SEG), h * cols : (h + 1) * cols] = jnp.where(head_mask(h, SEG, cols), q, jnp.zeros_like(q))
        return 0

    lax.fori_loop(0, blocks, mask_queries, 0)
    for item in gmb_spreads:
        item.forward()
    for item in gmb_spreads:
        item.wait()
    down_fold.copy(1).start()

    def context_grads(i, _):
        at = pl.multiple_of(i * SEG, SEG)
        low = nt(gmb_ref[pl.ds(at, SEG), :], wo_ref[...]).astype(BF)
        gct = low.astype(F32).T
        for h in range(3):
            gu_ref[pl.ds(at, SEG), h * cols : (h + 1) * cols] = jnp.where(
                head_mask(h, SEG, cols), low, jnp.zeros_like(low)
            )
            c = ct_ref[pl.ds(t * wide + h * HD, HD), pl.ds(at, SEG)].astype(F32)
            delta_ref[h : h + 1, pl.ds(at, SEG)] = jnp.sum(gct[h * HD : (h + 1) * HD] * c, axis=0, keepdims=True)
        return 0

    lax.fori_loop(0, blocks, context_grads, 0)
    for step in (2, 1, 3):
        f_settles[0].pass_on(step)
    go_ref[...] = nn(ct_ref[pl.ds(t * wide, wide), :], gmb_ref[...]).astype(BF).T
    o_settle.start()
    qm_ref, gm_ref = a_ref, gu_ref

    def piece(i, lo, hi, first):
        at, n = i * SEG, hi - lo
        keys = pl.ds(lo * SEG, n * SEG)
        values = pl.ds(ext + lo * SEG, n * SEG)
        for h in range(3):
            head = slice(h * cols, (h + 1) * cols)
            turned = slice(h * HD, (h + 1) * HD)
            qm, gm = qm_ref[at : at + SEG, head], gm_ref[at : at + SEG, head]
            s = nt(k_ref[keys, :], qm)
            g = nt(v_ref[keys, :], gm)
            logsum, delta = l_ref[h : h + 1, at : at + SEG], delta_ref[h : h + 1, at : at + SEG]
            for j in range(n):
                bias = block_bias(seg_ref, par_ref, dp * blocks + i, back + i - lo - j)
                part = slice(j * SEG, (j + 1) * SEG)
                x = s[part] * LOG2E
                if lo + j == i:
                    x = x + tri_ref[1]
                if lo + j == i + back:
                    x = x + tri_ref[0]
                p = jnp.exp2(x - (logsum - bias))
                e_ref[h, part, :] = p.astype(BF)
                xe_ref[WINDOW + j * SEG : WINDOW + (j + 1) * SEG, head] = (p * (g[part] - delta)).astype(BF)
            dv = nn(e_ref[h, 0 : n * SEG, :], gm)
            ds = xe_ref[WINDOW : WINDOW + n * SEG, head]
            dk = nn(ds, qm)
            dq = nn(turn_ref[turned, keys], ds)
            if first and h == 0:
                pool_ref[values, :] = dv
                pool_ref[keys, :] = dk
            else:
                pool_ref[values, :] += dv
                pool_ref[keys, :] += dk
            if lo == i:
                dqt_ref[turned, at : at + SEG] = dq
            else:
                dqt_ref[turned, at : at + SEG] += dq

    def outer(at, k, fold, with_query):
        gk = pool_ref[pl.ds(at, rows), 0:wide].astype(BF)
        gv = pool_ref[pl.ds(ext + at, rows), 0:wide].astype(BF)
        k_ref[pl.ds(at, rows), 0:wide] = gk
        v_ref[pl.ds(at, rows), 0:wide] = gv
        part = nt(gk, wk_ref[:, 0:wide]) + nt(gv, wv_ref[:, 0:wide])
        if with_query:
            part = part + nt(q_ref[pl.ds(at - WINDOW, rows), 0:wide], wq_ref[:, 0:wide])
        gn_own[...] = part
        if with_query:

            @pl.when((place < per_tree - 2) & (t ^ (3 - k) == 3))
            def _():
                far_back().wait_recv()
                gn_own[rows - lag :, :] += far_buf[1].astype(F32)

        for i in range(3):

            @pl.when(k == i)
            def _():
                fold.put(i, gn_own[...])
                fold.copy(i).start()

    piece(0, 0, 3, True)
    piece(0, 3, back, True)
    for i in range(1, blocks):
        piece(i, i, back, False)

    @pl.when(place >= 2)
    def _():
        gk = pool_ref[0:lag, 0:wide].astype(BF)
        gv = pool_ref[ext : ext + lag, 0:wide].astype(BF)
        far_buf[0] = (nt(gk, wk_ref[:, 0:wide]) + nt(gv, wv_ref[:, 0:wide])).astype(BF)
        far_back().start()

    k_ref[0:lag, 0:wide] = pool_ref[0:lag, 0:wide].astype(BF)
    v_ref[0:lag, 0:wide] = pool_ref[ext : ext + lag, 0:wide].astype(BF)

    def halo_outer(k, _):
        outer(lag + (t ^ (3 - k)) * rows, k, halo_fold, False)
        return 0

    lax.fori_loop(0, 4, halo_outer, 0)
    for step in (2, 1, 3):
        f_settles[1].pass_on(step)
    for i in range(blocks - 1, 1, -1):
        piece(i, back, back + i + 1, i == blocks - 1)

    for step in (2, 1, 3):
        o_settle.pass_on(step)
    for i in range(1, -1, -1):
        piece(i, back, back + i + 1, False)

    cot_all[3 * rows : 4 * rows, :] = halo_fold.total(gn_own[...]).astype(BF)

    @pl.when(place >= 1)
    def _():
        near_back().start()

    def turn_queries(i, _):
        at = pl.multiple_of(i * SEG, SEG)
        q_ref[pl.ds(at, SEG), 0:wide] = (dqt_ref[:, pl.ds(at, SEG)] * HD**-0.5).astype(BF).T
        return 0

    lax.fori_loop(0, blocks, turn_queries, 0)

    keep = pl.ds(WINDOW, token)
    own_k, own_v = pool_ref[keep, 0:wide].astype(BF), pool_ref[pl.ds(ext + WINDOW, token), 0:wide].astype(BF)
    k_ref[keep, 0:wide] = own_k
    v_ref[keep, 0:wide] = own_v
    grads = [
        tn(xe_ref[0:WINDOW, :], ref[0:WINDOW, 0:wide]) + tn(n1_ref[...], ref[WINDOW:, 0:wide]) for ref in (k_ref, v_ref)
    ]
    w_ref[0:width, 0 : 2 * wide] = jnp.concatenate([g.astype(BF) for g in grads], axis=1)
    a_settles[0].start()
    grads.append(tn(n1_ref[...], q_ref[:, 0:wide]))
    w_ref[0:width, 2 * wide : 3 * wide] = grads[2].astype(BF)
    a_settles[1].start()
    def own_outer(k, _):
        outer(WINDOW + (t ^ (3 - k)) * rows, k, gn1_fold, True)
        return 0

    lax.fori_loop(0, 4, own_outer, 0)
    terms = sum(g * w[:, 0:wide].astype(F32) for g, w in zip(grads, (wk_ref, wv_ref, wq_ref)))
    first_row = lax.broadcasted_iota(jnp.int32, (8, width), 0) == 0
    gt_buf[0] = jnp.where(first_row, nt(ones[:, 0:wide], terms.astype(BF)), gt_buf[0])
    for i in range(3):
        gain_copy(i).start()
    for step in (2, 1, 3):
        a_settles[0].pass_on(step)
    total = gt_buf[0]
    for i in range(3):
        gain_copy(i).wait_recv()
        total = total + gt_buf[i + 1]
    gd_buf[0] = total
    for i in range(7):
        gain_over(i).start()
    gup_ref[...] = f_settles[0].total()
    gdown_ref[...] = f_settles[1].total()
    gout_ref[...] = o_settle.total().T

    for step in (2, 1, 3):
        a_settles[1].pass_on(step)
    out_ref[...] = (mid_ref[...] + down_fold.total(down_own[...])).astype(BF)
    gn1 = gn1_fold.total(gn_own[...])

    @pl.when(place < per_tree - 1)
    def _():
        near_back().wait_recv()
        gn_own[...] = near_buf[...].astype(F32)

    @pl.when(place == per_tree - 1)
    def _():
        gn_own[...] = jnp.zeros((rows, width), F32)

    gn1 = gn1 + gn_own[...]
    x = x_ref[...].astype(F32)
    r1 = lax.rsqrt(jnp.mean(x * x, axis=-1, keepdims=True) + EPS)
    hat1 = x * r1
    scaled = gn1 * gain_ref[0:1, :]
    inner = jnp.mean(scaled * hat1, axis=-1, keepdims=True)
    ing_ref[...] = (gmid_ref[...] + r1 * (scaled - hat1 * inner)).astype(BF)

    total = gd_buf[0]
    for i in range(7):
        gain_over(i).wait_recv()
        total = total + gd_buf[i + 1]
    total = pltpu.roll(total, lax.rem(8 - dp, 8) * deep, 1)
    gg1_ref[...] = total[0:1, 0:deep] / g1_ref[...].astype(F32)
    gg2_ref[...] = total[1:2, 0:deep] / g2_ref[...].astype(F32)
    ga = a_settles[0].total()
    gk_out[...] = ga[:, 0:wide]
    gv_out[...] = ga[:, wide : 2 * wide]
    gq_out[...] = a_settles[1].total()[:, 0:wide]
    for i in range(3):
        gain_copy(i).wait_send()
    for i in range(7):
        gain_over(i).wait_send()
    for item in (down_fold, halo_fold, gn1_fold, *gmb_spreads, *f_settles, o_settle, *a_settles):
        item.finish()

    @pl.when(place >= 1)
    def _():
        near_back().wait_send()

    @pl.when(place >= 2)
    def _():
        far_back().wait_send()


def fast_shards(
    layer_input, cotangent, segments, parents, norm1_gain, w_query, w_key, w_value, w_out, norm2_gain, w_up, w_down,
):
    rows, width = layer_input.shape
    token = 4 * rows
    ext = token + WINDOW
    wide = width // 4
    cols = 256 * pl.cdiv(wide, 256)
    deep, hidden = w_up.shape
    blocks = token // SEG
    span = WINDOW + SEG
    shape = jax.ShapeDtypeStruct
    vmem = pl.BlockSpec(memory_space=pltpu.VMEM)
    smem = pl.BlockSpec(memory_space=pltpu.SMEM)
    copies = 7 * 3 + 4 * 8 + 3 + 3 * blocks + 5 * 3 + 5 * 7 + 2 + 3 + 7
    results = pl.pallas_call(
        kernel,
        out_shape=[
            shape((rows, width), BF),
            shape((rows, width), BF),
            shape((1, deep), F32),
            shape((deep, wide), F32),
            shape((deep, wide), F32),
            shape((deep, wide), F32),
            shape((wide, deep), F32),
            shape((1, deep), F32),
            shape((deep, hidden), F32),
            shape((deep, hidden), F32),
        ],
        in_specs=[smem, smem] + [vmem] * 10,
        out_specs=[vmem] * 10,
        scratch_shapes=[
            pltpu.VMEM((ext, width), BF),
            pltpu.VMEM((token, width), BF),
            pltpu.VMEM((token, width), BF),
            pltpu.VMEM((rows, width), F32),
            pltpu.VMEM((rows, width), F32),
            pltpu.VMEM((8 * (deep + 16), width), BF),
            pltpu.VMEM((width, 2 * hidden), BF),
            pltpu.VMEM((token, width), BF),
            pltpu.VMEM((width, width), BF),
            pltpu.VMEM((cols, width), BF),
            pltpu.VMEM((width, cols), BF),
            pltpu.VMEM((width, cols), BF),
            pltpu.VMEM((width, cols), BF),
            pltpu.VMEM((token, cols), BF),
            pltpu.VMEM((ext, cols), BF),
            pltpu.VMEM((ext, cols), BF),
            pltpu.VMEM((cols, ext), BF),
            pltpu.VMEM((width, token), BF),
            pltpu.VMEM((8, token), F32),
            pltpu.VMEM((8, width), F32),
            pltpu.VMEM((8, token), F32),
            pltpu.VMEM((2 * ext, SEG), F32),
            pltpu.VMEM((3, span, SEG), BF),
            pltpu.VMEM((2, SEG, SEG), F32),
            pltpu.VMEM((token, hidden), BF),
            pltpu.VMEM((token, hidden), BF),
            pltpu.VMEM((rows, width), F32),
            pltpu.VMEM((rows, width), F32),
            pltpu.VMEM((6, rows, width), BF),
            pltpu.VMEM((6, rows, width), BF),
            pltpu.VMEM((token, width), BF),
            pltpu.VMEM((4, deep, 2 * hidden), BF),
            pltpu.VMEM((3, deep, 2 * hidden), BF),
            pltpu.VMEM((width, wide), BF),
            pltpu.VMEM((4, deep, wide), BF),
            pltpu.VMEM((3, deep, wide), BF),
            pltpu.VMEM((4, deep, 128 * pl.cdiv(3 * wide, 128)), BF),
            pltpu.VMEM((3, deep, 128 * pl.cdiv(3 * wide, 128)), BF),
            pltpu.VMEM((wide, token), F32),
            pltpu.VMEM((rows, width), BF),
            pltpu.VMEM((2, WINDOW - token, width), BF),
            pltpu.VMEM((4, 8, width), F32),
            pltpu.VMEM((8, 8, width), F32),
            pltpu.SemaphoreType.DMA((copies,)),
            pltpu.SemaphoreType.DMA((copies,)),
        ],
        compiler_params=pltpu.CompilerParams(
            collective_id=0, has_side_effects=True, vmem_limit_bytes=64 << 20
        ),
    )(
        segments, parents, layer_input, cotangent, norm1_gain[None], w_query, w_key, w_value, w_out,
        norm2_gain[None], w_up, w_down.T,
    )
    results = list(hand_over(results))
    results[2], results[7], results[9] = results[2][0], results[7][0], results[9].T
    return tuple(results)


def hand_over(arrays):
    def body(*refs):
        for source, target in zip(refs[: len(arrays)], refs[len(arrays) :]):
            target[...] = source[...]

    vmem = pl.BlockSpec(memory_space=pltpu.VMEM)
    return pl.pallas_call(
        body,
        out_shape=[jax.ShapeDtypeStruct(a.shape, a.dtype) for a in arrays],
        in_specs=[vmem] * len(arrays),
        out_specs=[vmem] * len(arrays),
    )(*arrays)


epsilon = 1e-06
masked_score = -1e30


def from_behind(block, axis, distance):
    devices = range(lax.axis_size(axis))
    route = [(i - distance, i) for i in devices if i - distance in devices]
    return lax.ppermute(block, axis, route)


def split_up(x, dim, peers):
    dims = x.shape
    tiles = x.reshape(*dims[:dim], peers, dims[dim] // peers, *dims[dim + 1 :])
    return jnp.moveaxis(tiles, dim, 0)


def sum_at_owner(x, axis, dim):
    tiles = split_up(x, dim, lax.axis_size(axis))
    arrived = lax.all_to_all(tiles, axis, split_axis=0, concat_axis=0, tiled=True)
    return arrived.astype(jnp.float32).sum(axis=0)


def side_by_side(arrays, axis, dim, along):
    widths = [math.prod(a.shape[along:]) for a in arrays]
    both = jnp.concatenate(
        [a.reshape(*a.shape[:along], w) for a, w in zip(arrays, widths)], axis=along
    )
    whole = sum_at_owner(both, axis, dim)
    tiles = jnp.split(whole, [sum(widths[:k]) for k in range(1, len(widths))], axis=along)
    return tuple((b.reshape(*whole.shape[:along], *a.shape[along:]) for a, b in zip(arrays, tiles)))


def gelu_exact(values):
    return jax.nn.gelu(values, approximate=False)


def row_scale(values):
    return lax.rsqrt(jnp.mean(values * values, axis=-1, keepdims=True) + epsilon)


def norm_backward(incoming, normal_hat, row_factor, gain):
    scaled = incoming * gain
    inner = jnp.mean(scaled * normal_hat, axis=-1, keepdims=True)
    return (row_factor * (scaled - normal_hat * inner), jnp.sum(incoming * normal_hat, axis=0))


def parent_of(seg_ids, parents):
    seg_table = jnp.arange(parents.shape[0], dtype=jnp.int32)
    hits = seg_ids[:, None] == seg_table[None, :]
    return jnp.sum(jnp.where(hits, parents[None, :], 0), axis=1)


def shards(
    layer_input,
    cotangent,
    segments,
    parents,
    norm1_gain,
    w_query,
    w_key,
    w_value,
    w_out,
    norm2_gain,
    w_up,
    w_down,
):
    gain_one, full_query, full_key, full_value, full_out, gain_two, full_up, full_down = (
        lax.all_gather(norm1_gain, "dp", axis=0, tiled=True),
        lax.all_gather(w_query, "dp", axis=0, tiled=True),
        lax.all_gather(w_key, "dp", axis=0, tiled=True),
        lax.all_gather(w_value, "dp", axis=0, tiled=True),
        lax.all_gather(w_out, "dp", axis=1, tiled=True),
        lax.all_gather(norm2_gain, "dp", axis=0, tiled=True),
        lax.all_gather(w_up, "dp", axis=0, tiled=True),
        lax.all_gather(w_down, "dp", axis=1, tiled=True),
    )
    gain_one = gain_one.astype(jnp.float32)
    gain_two = gain_two.astype(jnp.float32)
    row_count = layer_input.shape[0]
    token_count = row_count * lax.axis_size("tensor")
    position = lax.axis_index("dp") * token_count
    head_width = full_query.shape[1]
    head_count = head_width // HD
    scaling = HD ** (-0.5)
    block_rows = min(640, token_count)
    block_count = token_count // block_rows
    span = WINDOW + block_rows
    hop_count = (WINDOW + token_count - 1) // token_count
    inputs = layer_input.astype(jnp.float32)
    factor_one = row_scale(inputs)
    hat_one = inputs * factor_one
    normed = (hat_one * gain_one).astype(jnp.bfloat16)
    normed_all = lax.all_gather(normed, "tensor", axis=0, tiled=True)
    queries = jnp.dot(normed_all, full_query, preferred_element_type=jnp.float32).astype(
        jnp.bfloat16
    )
    keys_own = jnp.dot(normed_all, full_key, preferred_element_type=jnp.float32).astype(
        jnp.bfloat16
    )
    values_own = jnp.dot(normed_all, full_value, preferred_element_type=jnp.float32).astype(
        jnp.bfloat16
    )
    pair_own = jnp.concatenate([keys_own, values_own], axis=1)
    halo_parts = []
    for distance in range(1, hop_count + 1):
        length = min(token_count, WINDOW - (distance - 1) * token_count)
        piece = pair_own[token_count - length :]
        moved = from_behind(piece, "dp", distance)
        halo_parts.append(moved)
    pair_all = jnp.concatenate(halo_parts[::-1] + [pair_own], axis=0)
    seg_padded = jnp.concatenate([jnp.full((WINDOW,), -1, jnp.int32), segments])
    seg_keys = lax.dynamic_slice_in_dim(seg_padded, position, WINDOW + token_count, 0)
    seg_query = seg_keys[WINDOW:]
    parent_one = parent_of(seg_query, parents)
    parent_two = parent_of(parent_one, parents)
    query_spots = jnp.arange(block_rows, dtype=jnp.int32)
    key_spots = jnp.arange(span, dtype=jnp.int32)

    def scores_of(offset):
        query_block = lax.dynamic_slice_in_dim(queries, offset, block_rows, 0).reshape(
            block_rows, head_count, HD
        )
        pair_block = lax.dynamic_slice_in_dim(pair_all, offset, span, 0)
        key_block = pair_block[:, :head_width].reshape(span, head_count, HD)
        value_block = pair_block[:, head_width:].reshape(span, head_count, HD)
        own_seg = lax.dynamic_slice_in_dim(seg_query, offset, block_rows, 0)
        up_one = lax.dynamic_slice_in_dim(parent_one, offset, block_rows, 0)
        up_two = lax.dynamic_slice_in_dim(parent_two, offset, block_rows, 0)
        near_seg = lax.dynamic_slice_in_dim(seg_keys, offset, span, 0)
        gap = WINDOW + query_spots[:, None] - key_spots[None, :]
        same_path = (
            (near_seg[None, :] == own_seg[:, None])
            | (near_seg[None, :] == up_one[:, None])
            | (near_seg[None, :] == up_two[:, None])
        )
        allowed = (gap >= 0) & (gap < WINDOW) & same_path
        raw = (
            jnp.einsum("qhd,khd->hqk", query_block, key_block, preferred_element_type=jnp.float32)
            * scaling
        )
        return (jnp.where(allowed[None], raw, masked_score), query_block, key_block, value_block)

    def forward_block(block_index):
        scores, query_block, key_block, value_block = scores_of(block_index * block_rows)
        row_max = jnp.max(scores, axis=-1, keepdims=True)
        exponent = jnp.exp(scores - row_max)
        denominator = jnp.sum(exponent, axis=-1, keepdims=True)
        weights = (exponent / denominator).astype(jnp.bfloat16)
        mixed = jnp.einsum("hqk,khd->qhd", weights, value_block, preferred_element_type=jnp.float32)
        return (
            mixed.reshape(block_rows, head_width).astype(jnp.bfloat16),
            (row_max + jnp.log(denominator))[..., 0],
        )

    context_blocks, logsum_blocks = lax.map(forward_block, jnp.arange(block_count, dtype=jnp.int32))
    context = context_blocks.reshape(token_count, head_width)
    middle = inputs + lax.psum_scatter(
        jnp.dot(context, full_out, preferred_element_type=jnp.float32).astype(jnp.bfloat16),
        "tensor",
        scatter_dimension=0,
        tiled=True,
    ).astype(jnp.float32)
    factor_two = row_scale(middle)
    hat_two = middle * factor_two
    normed_two = (hat_two * gain_two).astype(jnp.bfloat16)
    normed_two_all = lax.all_gather(normed_two, "tensor", axis=0, tiled=True)
    upper = jnp.dot(normed_two_all, full_up, preferred_element_type=jnp.float32)
    active = gelu_exact(upper).astype(jnp.bfloat16)
    result = middle + lax.psum_scatter(
        jnp.dot(active, full_down, preferred_element_type=jnp.float32).astype(jnp.bfloat16),
        "tensor",
        scatter_dimension=0,
        tiled=True,
    ).astype(jnp.float32)
    incoming = cotangent.astype(jnp.float32)
    incoming_all = lax.all_gather(cotangent, "tensor", axis=0, tiled=True)
    grad_down = jnp.einsum("tf,td->fd", active, incoming_all, preferred_element_type=jnp.float32)
    grad_active = jnp.einsum(
        "td,fd->tf", incoming_all, full_down, preferred_element_type=jnp.float32
    )
    unused_value, gelu_pull = jax.vjp(gelu_exact, upper)
    grad_upper = gelu_pull(grad_active)[0].astype(jnp.bfloat16)
    grad_up = jnp.einsum(
        "tc,tf->cf", normed_two_all, grad_upper, preferred_element_type=jnp.float32
    )
    grad_normed_two = lax.psum_scatter(
        jnp.einsum("tf,cf->tc", grad_upper, full_up, preferred_element_type=jnp.float32).astype(
            jnp.bfloat16
        ),
        "tensor",
        scatter_dimension=0,
        tiled=True,
    ).astype(jnp.float32)
    through_two, gain_two_part = norm_backward(grad_normed_two, hat_two, factor_two, gain_two)
    grad_middle = incoming + through_two
    grad_middle_all = lax.all_gather(grad_middle.astype(jnp.bfloat16), "tensor", axis=0, tiled=True)
    grad_out = jnp.einsum("tc,td->cd", context, grad_middle_all, preferred_element_type=jnp.float32)
    grad_context = jnp.einsum(
        "td,cd->tc", grad_middle_all, full_out, preferred_element_type=jnp.float32
    ).astype(jnp.bfloat16)

    def backward_block(block_index, carry):
        grad_queries, grad_pairs = carry
        offset = block_index * block_rows
        scores, query_block, key_block, value_block = scores_of(offset)
        logsum = lax.dynamic_index_in_dim(logsum_blocks, block_index, 0, keepdims=False)
        probs = jnp.exp(scores - logsum[..., None])
        grad_rows = lax.dynamic_slice_in_dim(grad_context, offset, block_rows, 0).reshape(
            block_rows, head_count, HD
        )
        grad_probs = jnp.einsum(
            "qhd,khd->hqk", grad_rows, value_block, preferred_element_type=jnp.float32
        )
        inner = jnp.sum(probs * grad_probs, axis=-1, keepdims=True)
        grad_scores = (probs * (grad_probs - inner)).astype(jnp.bfloat16)
        grad_query_block = (
            jnp.einsum("hqk,khd->qhd", grad_scores, key_block, preferred_element_type=jnp.float32)
            * scaling
        )
        grad_key_block = (
            jnp.einsum("hqk,qhd->khd", grad_scores, query_block, preferred_element_type=jnp.float32)
            * scaling
        )
        grad_value_block = jnp.einsum(
            "hqk,qhd->khd",
            probs.astype(jnp.bfloat16),
            grad_rows,
            preferred_element_type=jnp.float32,
        )
        grad_queries = lax.dynamic_update_slice_in_dim(
            grad_queries, grad_query_block.reshape(block_rows, head_width), offset, 0
        )
        update = jnp.concatenate(
            [grad_key_block.reshape(span, head_width), grad_value_block.reshape(span, head_width)],
            axis=1,
        )
        current = lax.dynamic_slice_in_dim(grad_pairs, offset, span, 0)
        grad_pairs = lax.dynamic_update_slice_in_dim(grad_pairs, current + update, offset, 0)
        return (grad_queries, grad_pairs)

    start_carry = (
        jnp.zeros((token_count, head_width), jnp.float32),
        jnp.zeros((WINDOW + token_count, 2 * head_width), jnp.float32),
    )
    grad_queries, grad_pairs = lax.fori_loop(0, block_count, backward_block, start_carry)
    grad_own = grad_pairs[WINDOW:]
    for distance in range(1, hop_count + 1):
        length = min(token_count, WINDOW - (distance - 1) * token_count)
        first_row = WINDOW - (distance - 1) * token_count - length
        piece = grad_pairs[first_row : first_row + length]
        returned = from_behind(piece.astype(jnp.bfloat16), "dp", -distance).astype(piece.dtype)
        grad_own = grad_own + jnp.pad(returned, ((token_count - length, 0), (0, 0)))
    grad_keys = grad_own[:, :head_width].astype(jnp.bfloat16)
    grad_values = grad_own[:, head_width:].astype(jnp.bfloat16)
    grad_queries_low = grad_queries.astype(jnp.bfloat16)
    grad_query = jnp.einsum(
        "tc,tq->cq", normed_all, grad_queries_low, preferred_element_type=jnp.float32
    )
    grad_key = jnp.einsum("tc,tq->cq", normed_all, grad_keys, preferred_element_type=jnp.float32)
    grad_value = jnp.einsum(
        "tc,tq->cq", normed_all, grad_values, preferred_element_type=jnp.float32
    )
    part_query = jnp.einsum(
        "tq,cq->tc", grad_queries_low, full_query, preferred_element_type=jnp.float32
    )
    part_key = jnp.einsum("tq,cq->tc", grad_keys, full_key, preferred_element_type=jnp.float32)
    part_value = jnp.einsum(
        "tq,cq->tc", grad_values, full_value, preferred_element_type=jnp.float32
    )
    grad_normed = lax.psum_scatter(
        (part_query + part_key + part_value).astype(jnp.bfloat16),
        "tensor",
        scatter_dimension=0,
        tiled=True,
    ).astype(jnp.float32)
    through_one, gain_one_part = norm_backward(grad_normed, hat_one, factor_one, gain_one)
    grad_inputs = grad_middle + through_one
    gain_one_sum, gain_two_sum = lax.psum((gain_one_part, gain_two_part), "tensor")
    summed = (
        *side_by_side(
            (
                gain_one_sum.astype(jnp.bfloat16),
                grad_query.astype(jnp.bfloat16),
                grad_key.astype(jnp.bfloat16),
                grad_value.astype(jnp.bfloat16),
            ),
            "dp",
            0,
            1,
        ),
        sum_at_owner(grad_out.astype(jnp.bfloat16), "dp", 1),
        *side_by_side(
            (gain_two_sum.astype(jnp.bfloat16), grad_up.astype(jnp.bfloat16)), "dp", 0, 1
        ),
        sum_at_owner(grad_down.astype(jnp.bfloat16), "dp", 1),
    )
    return (
        result.astype(jnp.bfloat16),
        grad_inputs.astype(jnp.bfloat16),
        summed[0],
        summed[1],
        summed[2],
        summed[3],
        summed[4],
        summed[5],
        summed[6],
        summed[7],
    )


def solution(mesh):
    fast = mesh.shape["dp"] == 8 and mesh.shape["tensor"] == 4
    return jax.shard_map(
        fast_shards if fast else shards,
        mesh=mesh,
        in_specs=(
            P(("dp", "tensor"), None),
            P(("dp", "tensor"), None),
            P(),
            P(),
            P("dp"),
            P("dp", "tensor"),
            P("dp", "tensor"),
            P("dp", "tensor"),
            P("tensor", "dp"),
            P("dp"),
            P("dp", "tensor"),
            P("tensor", "dp"),
        ),
        out_specs=(
            P(("dp", "tensor"), None),
            P(("dp", "tensor"), None),
            P("dp"),
            P("dp", "tensor"),
            P("dp", "tensor"),
            P("dp", "tensor"),
            P("tensor", "dp"),
            P("dp"),
            P("dp", "tensor"),
            P("tensor", "dp"),
        ),
        check_vma=False,
    )
```
